32 devices in a mesh: row: 4 (over x, core), col: 8 (over z, y).
Axes of the slice: x: 2, y: 2, z: 4, core: 2. Of those that a mesh axis runs over, the one named last changes fastest.
Arguments:
- inputs: bfloat16 [8, 1024, 512], P('col', 'row'), may hold values from -6 to 6
- seg_start: int32 [8, 1024], P('col', 'row'), may hold values from 0 to 1023, as said below
- cotangent: bfloat16 [8, 1024, 512], P('col', 'row'), may hold values from -6 to 6
- project_weight: bfloat16 [512, 1536], P('row', 'col'), may hold values from -0.25 to 0.25
- project_bias: bfloat16 [1536], P(('row', 'col')), may hold values from -1.5 to 1.5
- output_weight: bfloat16 [512, 512], P('col', 'row'), may hold values from -0.75 to 0.75
- output_bias: bfloat16 [512], P(('row', 'col')), may hold values from -1.5 to 1.5
- up_weight: bfloat16 [512, 2048], P('row', 'col'), may hold values from -0.25 to 0.25
- up_bias: bfloat16 [2048], P(('row', 'col')), may hold values from -1.5 to 1.5
- down_weight: bfloat16 [2048, 512], P('col', 'row'), may hold values from -0.125 to 0.125
- down_bias: bfloat16 [512], P(('row', 'col')), may hold values from -1.5 to 1.5
- first_gain: bfloat16 [512], P(('row', 'col')), may hold values from 0.25 to 1.75
- first_bias: bfloat16 [512], P(('row', 'col')), may hold values from -1.5 to 1.5
- second_gain: bfloat16 [512], P(('row', 'col')), may hold values from 0.25 to 1.75
- second_bias: bfloat16 [512], P(('row', 'col')), may hold values from -1.5 to 1.5
Outputs:
- output: bfloat16 [8, 1024, 512], P('col', 'row')
- input_grad: float32 [8, 1024, 512], P('col', 'row')
- project_weight_grad: float32 [512, 1536], P('row', 'col')
- project_bias_grad: float32 [1536], P(('row', 'col'))
- output_weight_grad: float32 [512, 512], P('col', 'row')
- output_bias_grad: float32 [512], P(('row', 'col'))
- up_weight_grad: float32 [512, 2048], P('row', 'col')
- up_bias_grad: float32 [2048], P(('row', 'col'))
- down_weight_grad: float32 [2048, 512], P('col', 'row')
- down_bias_grad: float32 [512], P(('row', 'col'))
- first_gain_grad: float32 [512], P(('row', 'col'))
- first_bias_grad: float32 [512], P(('row', 'col'))
- second_gain_grad: float32 [512], P(('row', 'col'))
- second_bias_grad: float32 [512], P(('row', 'col'))
The draws below stay inside these ranges and needn't reach their ends.
Inputs may be any that keep to these rules, and one draw needn't show every extreme that they name: `seg_start`: for each token, the place within its sequence of its document's first token; documents are runs of consecutive tokens, and in every sequence one document starts before place 1024 / 4 and reaches place 3 * 256 or later.
All inputs are finite; a program needn't handle non-finite values.
Results may differ from the reference program's by a relative error of at most 0.012.
Values may be sent and summed in bfloat16 or wider, within the bound.
No kernel may reach another device: no remote copies, remote signals or barrier semaphores. Data moves between devices by JAX's collectives and lax.ppermute only.
A program may use at most 128 MiB of HBM per device.

```python
import math
import jax
import jax.numpy as jnp
from jax import lax

D = 512
HD = 64
ROT = 16
FF = 2048
LEN = 1024
SEQS = 8


def draw_seg_start(key, part):
    key = jax.random.fold_in(key, 11)
    open_key, close_key, break_key = jax.random.split(key, 3)
    places = jnp.arange(LEN, dtype=jnp.int32)[None, :]
    opening = jax.random.randint(open_key, (SEQS, 1), 1, LEN // 4)
    closing = jax.random.randint(close_key, (SEQS, 1), 3 * LEN // 4, LEN)
    breaks = jax.random.randint(break_key, (SEQS, LEN), 0, LEN // 4) == 0
    inside = (places > opening) & (places <= closing)
    breaks = breaks & jnp.logical_not(inside) | (places == opening) | (places == closing + 1)
    starts = jnp.where(breaks, places, 0).astype(jnp.int32)
    return lax.cummax(starts, axis=1)


def raised(values, key, source, target, blocks, factor):
    owner, partner = [(jnp.arange(values.shape[position]) // (values.shape[position] // blocks)).reshape([-1 if axis == position else 1 for axis in range(values.ndim)]) for position in (source, target)]
    chosen = jax.random.permutation(key, blocks)[partner]
    strong = (owner == chosen) | (owner == (partner + blocks // 2) % blocks)
    return jnp.where(strong, factor * values, values)


def block_scale(rng, dims, pieces, low, top_value):
    level, own = 1.0, jax.random.fold_in(rng, 6)
    for position, shards_of in pieces:
        draws = jnp.exp(jax.random.uniform(jax.random.fold_in(own, position), (shards_of,), jnp.float32, low / len(pieces), top_value / len(pieces)))
        level = level * jnp.repeat(draws, dims[position] // shards_of).reshape([-1 if axis == position else 1 for axis in range(len(dims))])
    return level


def gaussian(own_key, dims, width, most, cuts=(), held_as=jnp.bfloat16):
    values = width * jax.random.normal(own_key, dims, jnp.float32)
    if cuts:
        values = values * block_scale(own_key, dims, cuts, -0.22, 0.18)
    return jnp.clip(values, -most, most).astype(held_as)


def bell_draw_with(key, dims, scale, reach, cuts, heavy, kind=jnp.bfloat16):
    array = scale * jax.random.normal(key, dims, jnp.float32)
    if cuts:
        array = array * block_scale(key, dims, cuts, -0.22, 0.18)
    return jnp.clip(raised(array, jax.random.fold_in(key, 3), *heavy), -reach, reach).astype(kind)


def setup_inputs(seed: int = 0) -> dict:
    key_list = jax.random.split(jax.random.key(seed), 16)
    inputs = gaussian(key_list[0], (SEQS, LEN, D), 1.0, 6.0, ((0, 8), (1, 4)))
    seg_start = draw_seg_start(jax.random.fold_in(key_list[15], 71), 0)
    cotangent = bell_draw_with(key_list[2], (SEQS, LEN, D), 1.0, 6.0, ((0, 8), (1, 4)), (0, 2, 8, 2.0))
    project_weight = gaussian(key_list[3], (D, 3 * D), D ** -0.5, 0.25, ((0, 4), (1, 8)))
    project_bias = gaussian(key_list[4], (3 * D,), 0.3, 1.5, ((0, 32),))
    output_weight = gaussian(key_list[5], (D, D), (D // 8) ** -0.5, 0.75, ((0, 8), (1, 4)))
    output_bias = gaussian(key_list[6], (D,), 0.3, 1.5, ((0, 32),))
    up_weight = gaussian(key_list[7], (D, FF), D ** -0.5, 0.25, ((0, 4), (1, 8)))
    up_bias = gaussian(key_list[8], (FF,), 0.3, 1.5, ((0, 32),))
    down_weight = gaussian(key_list[9], (FF, D), FF ** -0.5, 0.125, ((0, 8), (1, 4)))
    down_bias = gaussian(key_list[10], (D,), 0.3, 1.5, ((0, 32),))
    first_gain = jnp.clip(1.0 + 0.15 * jax.random.normal(key_list[11], (D,), jnp.float32), 0.25, 1.75).astype(jnp.bfloat16)
    first_bias = gaussian(key_list[12], (D,), 0.3, 1.5, ((0, 32),))
    second_gain = jnp.clip(1.0 + 0.15 * jax.random.normal(key_list[13], (D,), jnp.float32), 0.25, 1.75).astype(jnp.bfloat16)
    second_bias = gaussian(key_list[14], (D,), 0.3, 1.5, ((0, 32),))
    return {"inputs": inputs, "seg_start": seg_start, "cotangent": cotangent, "project_weight": project_weight, "project_bias": project_bias, "output_weight": output_weight, "output_bias": output_bias, "up_weight": up_weight, "up_bias": up_bias, "down_weight": down_weight, "down_bias": down_bias, "first_gain": first_gain, "first_bias": first_bias, "second_gain": second_gain, "second_bias": second_bias}


EPS = 1e-05
HIGH = lax.Precision.HIGHEST
MASKED = -1e+30

@jax.custom_vjp
def low(v):
    return lax.optimization_barrier(v.astype(jnp.bfloat16)).astype(jnp.float32)

@jax.custom_vjp
def low_back(v):
    return v

def low_keep(v):
    return (low(v), None)

def low_pass(kept, grad):
    return (grad,)

def back_keep(v):
    return (v, None)

def back_low(kept, grad):
    return (low(grad),)
low.defvjp(low_keep, low_pass)
low_back.defvjp(back_keep, back_low)

def layer_norm(rows_in, gain, shift):
    average = lax.optimization_barrier(jnp.mean(rows_in, axis=-1, keepdims=True))
    centred = rows_in - average
    spread = lax.optimization_barrier(jnp.mean(centred * centred, axis=-1, keepdims=True))
    return centred * lax.rsqrt(spread + EPS) * gain + shift

def rotate(tensor, positions):
    half_rot = ROT // 2
    exponent = jnp.arange(half_rot, dtype=jnp.float32) * (2.0 / ROT)
    frequency = jnp.exp(exponent * -math.log(10000.0))
    angles = positions[..., None].astype(jnp.float32) * frequency
    cosine = jnp.cos(angles)[..., None, :]
    sine_part = jnp.sin(angles)[..., None, :]
    leading = tensor[..., :half_rot]
    trailing = tensor[..., half_rot:ROT]
    return jnp.concatenate([leading * cosine - trailing * sine_part, trailing * cosine + leading * sine_part, tensor[..., ROT:]], axis=-1)

def forward_group(params, inputs, seg_start):
    project_weight, project_bias, output_weight, output_bias, up_weight, up_bias, down_weight, down_bias, first_gain, first_bias, second_gain, second_bias = params
    seq_count, length, model_width = inputs.shape
    head_count = model_width // HD
    scaling = HD ** (-0.5)
    token_index = jnp.arange(length, dtype=jnp.int32)
    positions = token_index[None, :] - seg_start
    allowed = (seg_start[:, None, :, None] == seg_start[:, None, None, :]) & (token_index[:, None] >= token_index[None, :])
    normed_one = low(layer_norm(inputs, first_gain, first_bias))
    projected = low_back(jnp.einsum('gtd,df->gtf', normed_one, project_weight, precision=HIGH) + project_bias)
    projected = projected.reshape(seq_count, length, head_count, 3 * HD)
    queries = low(rotate(projected[..., :HD], positions))
    key_rows = low(rotate(projected[..., HD:2 * HD], positions))
    values = low(projected[..., 2 * HD:])
    scores = low_back(jnp.einsum('gqhe,gkhe->ghqk', queries, key_rows, precision=HIGH) * scaling)
    scores = jnp.where(allowed, scores, MASKED)
    maximum = lax.optimization_barrier(jnp.max(scores, axis=-1, keepdims=True))
    exponent = jnp.exp(scores - maximum)
    probability = low(exponent / lax.optimization_barrier(jnp.sum(exponent, axis=-1, keepdims=True)))
    context = jnp.einsum('ghqk,gkhe->gqhe', probability, values, precision=HIGH)
    context = low(low_back(context.reshape(seq_count, length, model_width)))
    attn_out = jnp.einsum('gte,ed->gtd', context, output_weight, precision=HIGH) + output_bias
    normed_two = low(layer_norm(inputs, second_gain, second_bias))
    hidden = low_back(jnp.einsum('gtd,df->gtf', normed_two, up_weight, precision=HIGH) + up_bias)
    active = low(jax.nn.gelu(hidden, approximate=False))
    mlp_out = jnp.einsum('gtf,fd->gtd', active, down_weight, precision=HIGH) + down_bias
    return inputs + attn_out + mlp_out

def whole_layer(inputs, params, seg_start):
    seq_count = inputs.shape[0]
    pair_count = 2
    stacked = inputs.reshape(seq_count // pair_count, pair_count, inputs.shape[1], inputs.shape[2])
    starts = seg_start.reshape(seq_count // pair_count, pair_count, seg_start.shape[1])
    step_fn = jax.checkpoint(forward_group)

    def scan_step(state_in, element):
        return (state_in, step_fn(params, element[0], element[1]))
    unused, results = lax.scan(scan_step, jnp.zeros((), jnp.float32), (stacked, starts))
    return results.reshape(inputs.shape)

def reference(inputs, seg_start, cotangent, project_weight, project_bias, output_weight, output_bias, up_weight, up_bias, down_weight, down_bias, first_gain, first_bias, second_gain, second_bias):
    params = tuple((tensor.astype(jnp.float32) for tensor in (project_weight, project_bias, output_weight, output_bias, up_weight, up_bias, down_weight, down_bias, first_gain, first_bias, second_gain, second_bias)))
    start_ids = seg_start.astype(jnp.int32)
    result, pullback = jax.vjp(lambda rows_in, weights: whole_layer(rows_in, weights, start_ids), inputs.astype(jnp.float32), params)
    input_grad, grads = pullback(cotangent.astype(jnp.float32))
    return (result.astype(jnp.bfloat16), input_grad, grads[0], grads[1], grads[2], grads[3], grads[4], grads[5], grads[6], grads[7], grads[8], grads[9], grads[10], grads[11])
```

```python
import math

import jax
import jax.numpy as jnp
import numpy as np
from jax import lax
from jax.sharding import PartitionSpec as P

HD = 64
ROT = 16
EPS = 1e-05
MASKED = -1e30
BF = jnp.bfloat16
F32 = jnp.float32


def normalize(rows_in):
    average = jnp.mean(rows_in, axis=-1, keepdims=True)
    centred = rows_in - average
    spread = jnp.mean(centred * centred, axis=-1, keepdims=True)
    root = lax.rsqrt(spread + EPS)
    return centred * root, root


def dot(a, b, dims=((1,), (0,))):
    return lax.dot_general(a, b, (dims, ((), ())), preferred_element_type=F32)


def pack_project(b):
    half = b.shape[0] // 2
    return jnp.concatenate(
        [b[:, :128], jnp.concatenate([b[:half, 128:], b[half:, 128:]], axis=1)], axis=0
    )


def unpack_project(p):
    rest = p[128:192]
    return jnp.concatenate(
        [p[:128], jnp.concatenate([rest[:, :64], rest[:, 64:]], axis=0)], axis=1
    )


def pack_up(b):
    return jnp.concatenate([b[:, :128], b[:, 128:]], axis=0)


def unpack_up(p):
    return jnp.concatenate([p[:128], p[128:256]], axis=1)


def xor_order(stacked, key):
    return [
        lax.dynamic_index_in_dim(stacked, g ^ key, keepdims=False) for g in range(stacked.shape[0])
    ]


def rotary_tables(positions):
    lane = np.arange(2 * HD) % HD
    frequency = np.where(lane < ROT, 10000.0 ** (-(lane % (ROT // 2)) * 2.0 / ROT), 0.0)
    angles = positions[:, None].astype(F32) * jnp.asarray(frequency, F32)[None, :]
    return jnp.cos(angles), jnp.sin(angles)


def rotate(tensor, cosine, sine):
    half = ROT // 2
    swapped = jnp.concatenate(
        [-tensor[:, half:ROT], tensor[:, :half], tensor[:, ROT:]], axis=1
    )
    return tensor * cosine + swapped * sine


def mlp_half(normed, cot, slots, key, up_shift):
    blocks = xor_order(slots, key)
    up = jnp.concatenate([unpack_up(b[:256]) for b in blocks], axis=0)
    down = jnp.concatenate([b[256:] for b in blocks], axis=1)
    hidden = dot(normed, up) + up_shift[None, :]
    cdf = 0.5 * (1.0 + lax.erf(hidden * math.sqrt(0.5)))
    active = (hidden * cdf).astype(BF)
    slope = cdf + hidden * jnp.exp(-0.5 * hidden * hidden) * (1.0 / math.sqrt(2 * math.pi))
    out = dot(active, down)
    d_hidden = (dot(cot, down, ((1,), (1,))) * slope).astype(BF)
    down_grad = dot(active, cot, ((0,), (0,)))
    up_grad = dot(normed, d_hidden, ((0,), (0,)))
    up_shift_grad = jnp.sum(d_hidden.astype(F32), axis=0)
    d_second = dot(d_hidden, up, ((1,), (1,)))
    grads = jnp.stack(
        [
            jnp.concatenate(
                [pack_up(up_grad[128 * g : 128 * g + 128]), down_grad[:, 128 * g : 128 * g + 128]],
                axis=0,
            )
            for g in range(4)
        ]
    )
    return out, d_second, jnp.stack(xor_order(grads, key)), up_shift_grad


def att_head(normed, cot, slots, key, shift, cosine, sine, starts):
    blocks = xor_order(slots, key)
    project = jnp.concatenate([unpack_project(b[:192]) for b in blocks], axis=0)
    mix = jnp.concatenate([b[192:] for b in blocks], axis=1)
    cosine, sine = cosine[:, :HD], sine[:, :HD]
    projected = dot(normed, project) + shift[None, :]
    q = rotate(projected[:, :HD], cosine, sine).astype(BF)
    k = rotate(projected[:, HD : 2 * HD], cosine, sine).astype(BF)
    v = projected[:, 2 * HD :].astype(BF)
    scaling = HD**-0.5
    count = q.shape[0]
    place = jnp.arange(count, dtype=jnp.int32)
    allowed = (place[None, :] >= starts[:, None]) & (place[:, None] >= place[None, :])
    scores = jnp.where(allowed, dot(q, k, ((1,), (1,))) * scaling, MASKED)
    exponent = jnp.exp(scores - jnp.max(scores, axis=-1, keepdims=True))
    probability = exponent / jnp.sum(exponent, axis=-1, keepdims=True)
    prob_low = probability.astype(BF)
    context = dot(prob_low, v).astype(BF)
    out = dot(context, mix)
    mix_grad = dot(context, cot, ((0,), (0,)))
    d_context = dot(cot, mix, ((1,), (1,))).astype(BF)
    d_prob = dot(d_context, v, ((1,), (1,)))
    d_scores = probability * (d_prob - jnp.sum(d_prob * probability, axis=-1, keepdims=True))
    d_scores = d_scores.astype(BF)
    d_q = dot(d_scores, k) * scaling
    d_k = dot(d_scores, q, ((0,), (0,))) * scaling
    d_v = dot(prob_low, d_context, ((0,), (0,)))
    d_projected = jnp.concatenate(
        [rotate(d_q, cosine, -sine), rotate(d_k, cosine, -sine), d_v], axis=1
    ).astype(BF)
    project_grad = dot(normed, d_projected, ((0,), (0,)))
    shift_grad = jnp.sum(d_projected.astype(F32), axis=0)
    d_first = dot(d_projected, project, ((1,), (1,)))
    grads = jnp.stack(
        [
            jnp.concatenate(
                [
                    pack_project(project_grad[128 * g : 128 * g + 128]),
                    mix_grad[:, 128 * g : 128 * g + 128],
                ],
                axis=0,
            )
            for g in range(4)
        ]
    )
    return out, d_first, jnp.stack(xor_order(grads, key)), shift_grad


def on_device(
    inputs,
    seg_start,
    cotangent,
    project_weight,
    project_bias,
    output_weight,
    output_bias,
    up_weight,
    up_bias,
    down_weight,
    down_bias,
    first_gain,
    first_bias,
    second_gain,
    second_bias,
):
    rows, cols = lax.axis_size("row"), lax.axis_size("col")
    per = cols // rows
    r, c = lax.axis_index("row"), lax.axis_index("col")
    both = ("row", "col")
    count, width = inputs.shape[1], inputs.shape[2]
    paired = per == 2

    def flip(value, bit):
        return lax.ppermute(value, "row", [(i, i ^ bit) for i in range(rows)])

    def home(i, k):
        rr, cc = divmod(i, cols)
        z, y = divmod(cc, per)
        return z * cols + (rr ^ k) * per + y

    everyone = range(rows * cols)

    def spread(block):
        parts = [
            lax.ppermute(block, both, [(i, home(i, k)) for i in everyone]) for k in range(rows)
        ]
        own = jnp.stack(parts)
        return own, lax.ppermute(own, "col", [(i, i ^ 1) for i in range(cols)])

    def bring_other(grads):
        return lax.ppermute(grads, "col", [(i, i ^ 1) for i in range(cols)])

    def collect(grads):
        parts = [
            lax.ppermute(grads[k], both, [(home(i, k), i) for i in everyone]) for k in range(rows)
        ]
        return sum(p.astype(F32) for p in parts)

    def slot_of(i):
        rr, cc = divmod(i, cols)
        return (cc // per) * cols + (cc % per) * rows + rr

    def fetch(block):
        moved = lax.ppermute(block, both, [(i, slot_of(i)) for i in everyone])
        whole = lax.all_gather(moved, "col", axis=0)
        return whole.reshape((per, rows) + block.shape)

    def fetch_columns(block):
        whole = fetch(block).transpose(1, 2, 0, 3).reshape(rows, block.shape[0], 2, -1)
        return whole.transpose(2, 0, 1, 3)

    def fetch_rows(block):
        whole = fetch(block).transpose(1, 0, 2, 3).reshape(rows, 2, -1, block.shape[1])
        return whole.transpose(1, 0, 2, 3)

    def deliver(blocks):
        flat = blocks.reshape((cols,) + blocks.shape[2:]).astype(BF)
        mine = lax.psum_scatter(flat, "col", scatter_dimension=0, tiled=False)
        return lax.ppermute(mine, both, [(slot_of(i), i) for i in everyone]).astype(F32)

    def deliver_columns(halves):
        deep = halves.shape[2]
        whole = halves.transpose(1, 2, 0, 3).reshape(rows, deep, per, -1)
        return deliver(whole.transpose(2, 0, 1, 3))

    def deliver_rows(halves):
        wide = halves.shape[3]
        whole = halves.transpose(1, 0, 2, 3).reshape(rows, per, -1, wide)
        return deliver(whole.transpose(1, 0, 2, 3))

    act = jnp.stack([inputs[0], cotangent[0]])
    act_two = jnp.stack([act, flip(act, 2)])
    act_far = flip(act_two, 1)
    act_all = jnp.stack([act_two[0], act_far[0], act_two[1], act_far[1]])
    act_all = jnp.stack(xor_order(act_all, r), axis=1)
    x_all = act_all[0].reshape(-1, width)
    cot_all = act_all[1].reshape(-1, width)

    if paired:
        key, y = c // per, c % per
        mlp_slots = spread(jnp.concatenate([pack_up(up_weight), down_weight], axis=0))
        att_slots = spread(jnp.concatenate([pack_project(project_weight), output_weight], axis=0))
    else:
        key, y = jnp.int32(0), jnp.int32(0)
        ups, downs = fetch_columns(up_weight), fetch_rows(down_weight)
        projects, mixes = fetch_columns(project_weight), fetch_rows(output_weight)
        mlp_slots = [
            jnp.stack(
                [jnp.concatenate([pack_up(ups[h, g]), downs[h, g]], axis=0) for g in range(rows)]
            )
            for h in range(2)
        ]
        att_slots = [
            jnp.stack(
                [
                    jnp.concatenate([pack_project(projects[h, g]), mixes[h, g]], axis=0)
                    for g in range(rows)
                ]
            )
            for h in range(2)
        ]

    seg_own = seg_start[0]
    small = jnp.concatenate(
        [
            first_gain,
            first_bias,
            second_gain,
            second_bias,
            output_bias,
            down_bias,
            project_bias,
            up_bias,
            (seg_own // 32).astype(BF),
            (seg_own % 32).astype(BF),
        ]
    )
    every = lax.all_to_all(
        jnp.broadcast_to(small[None], (rows * cols, small.shape[0])), both, 0, 0, tiled=True
    )
    part = first_gain.shape[0]
    norms = every[:, : 6 * part].reshape(-1, 6, part).transpose(1, 0, 2).reshape(6, -1).astype(F32)
    lengths = (project_bias.shape[0], up_bias.shape[0])
    begin = 6 * part
    mine = lax.dynamic_slice_in_dim(every, r * cols, cols, axis=0)
    project_shift = mine[:, begin : begin + lengths[0]].reshape(2, -1).astype(F32)
    begin += lengths[0]
    up_shift = mine[:, begin : begin + lengths[1]].reshape(2, -1).astype(F32)
    begin += lengths[1]
    project_shift = jnp.where(y == 0, project_shift, project_shift[::-1])
    up_shift = jnp.where(y == 0, up_shift, up_shift[::-1])
    segs = every.reshape(rows, cols, -1)[:, :, begin:]
    segs = lax.dynamic_index_in_dim(segs, c, axis=1, keepdims=False).astype(jnp.int32)
    starts = (segs[:, :count] * 32 + segs[:, count:]).reshape(-1)
    cosine, sine = rotary_tables(jnp.arange(rows * count, dtype=jnp.int32) - starts)

    xhat, root = normalize(x_all.astype(F32))
    normed_one = (xhat * norms[0] + norms[1]).astype(BF)
    normed_two = (xhat * norms[2] + norms[3]).astype(BF)

    out_oth, d2_oth, mlp_send, ub_oth = mlp_half(normed_two, cot_all, mlp_slots[1], key, up_shift[1])
    out_own, d2_own, mlp_keep, ub_own = mlp_half(normed_two, cot_all, mlp_slots[0], key, up_shift[0])
    out_a, d1_oth, att_send, pb_oth = att_head(
        normed_one, cot_all, att_slots[1], key, project_shift[1], cosine, sine, starts
    )
    out_b, d1_own, att_keep, pb_own = att_head(
        normed_one, cot_all, att_slots[0], key, project_shift[0], cosine, sine, starts
    )
    d_first, d_second = d1_oth + d1_own, d2_oth + d2_own
    out_part = out_oth + out_own + out_a + out_b
    e_part = d_first * norms[0] + d_second * norms[2]

    if paired:
        mlp_done = collect((mlp_keep + bring_other(mlp_send.astype(BF)).astype(F32)).astype(BF))
        att_done = collect((att_keep + bring_other(att_send.astype(BF)).astype(F32)).astype(BF))
        project_done, mix_done = unpack_project(att_done[:192]), att_done[192:]
        up_done, down_done = unpack_up(mlp_done[:256]), mlp_done[256:]
    else:
        att_grads, mlp_grads = jnp.stack([att_keep, att_send]), jnp.stack([mlp_keep, mlp_send])
        every_pair = [(h, g) for h in range(2) for g in range(rows)]

        def regroup(parts):
            return jnp.stack(parts).reshape((2, rows) + parts[0].shape)

        project_done = deliver_columns(
            regroup([unpack_project(att_grads[h, g][:192]) for h, g in every_pair])
        )
        mix_done = deliver_rows(regroup([att_grads[h, g][192:] for h, g in every_pair]))
        up_done = deliver_columns(
            regroup([unpack_up(mlp_grads[h, g][:256]) for h, g in every_pair])
        )
        down_done = deliver_rows(regroup([mlp_grads[h, g][256:] for h, g in every_pair]))

    oe = jnp.stack([out_part, e_part]).reshape(2, rows, count, width)
    chunk = [lax.dynamic_index_in_dim(oe, r ^ j, axis=1, keepdims=False) for j in range(4)]
    near = flip(jnp.stack([chunk[1], chunk[3]]).astype(BF), 1).astype(F32)
    mine_sum, far_sum = chunk[0] + near[0], chunk[2] + near[1]
    total = mine_sum + flip(far_sum.astype(BF), 2).astype(F32)
    x_own = inputs[0].astype(F32)
    cot_own = cotangent[0].astype(F32)
    output = (x_own + total[0] + norms[4] + norms[5]).astype(BF)[None]
    e_all = total[1]
    xhat_own, root_own = normalize(x_own)
    input_grad = cot_own + root_own * (
        e_all
        - jnp.mean(e_all, axis=-1, keepdims=True)
        - xhat_own * jnp.mean(e_all * xhat_own, axis=-1, keepdims=True)
    )

    everywhere = jnp.stack(
        [
            jnp.sum(d_first * xhat, axis=0),
            jnp.sum(d_first, axis=0),
            jnp.sum(d_second * xhat, axis=0),
            jnp.sum(d_second, axis=0),
            jnp.sum(cot_own, axis=0),
        ]
    )
    everywhere = everywhere.reshape(5, rows * cols, part).transpose(1, 0, 2).reshape(rows * cols, -1)

    def by_half(own, other):
        first = jnp.where(y == 0, own, other)
        second = jnp.where(y == 0, other, own)
        return jnp.concatenate([first, second]).reshape(cols, -1)

    local = jnp.concatenate([by_half(pb_own, pb_oth), by_half(ub_own, ub_oth)], axis=1)
    local = lax.dynamic_update_slice(
        jnp.zeros((rows * cols, local.shape[1]), F32), local, (r * cols, 0)
    )
    sums = lax.all_to_all(
        jnp.concatenate([everywhere, local], axis=1), both, 0, 0, tiled=True
    ).sum(axis=0)
    pieces = [sums[i * part : (i + 1) * part] for i in range(5)]
    project_shift_grad = sums[5 * part : 5 * part + lengths[0]]
    up_shift_grad = sums[5 * part + lengths[0] :]
    return (
        output,
        input_grad[None],
        project_done,
        project_shift_grad,
        mix_done,
        pieces[4],
        up_done,
        up_shift_grad,
        down_done,
        pieces[4],
        pieces[0],
        pieces[1],
        pieces[2],
        pieces[3],
    )


def solution(mesh):
    return jax.shard_map(
        on_device,
        mesh=mesh,
        in_specs=(
            P("col", "row", None),
            P("col", "row"),
            P("col", "row", None),
            P("row", "col"),
            P(("row", "col")),
            P("col", "row"),
            P(("row", "col")),
            P("row", "col"),
            P(("row", "col")),
            P("col", "row"),
            P(("row", "col")),
            P(("row", "col")),
            P(("row", "col")),
            P(("row", "col")),
            P(("row", "col")),
        ),
        out_specs=(
            P("col", "row", None),
            P("col", "row", None),
            P("row", "col"),
            P(("row", "col")),
            P("col", "row"),
            P(("row", "col")),
            P("row", "col"),
            P(("row", "col")),
            P("col", "row"),
            P(("row", "col")),
            P(("row", "col")),
            P(("row", "col")),
            P(("row", "col")),
            P(("row", "col")),
        ),
        check_vma=False,
    )
```

```python
import functools
import math

import jax
import jax.numpy as jnp
import numpy as np
from jax import lax
from jax.experimental import pallas as pl
from jax.experimental.pallas import tpu as pltpu
from jax.sharding import PartitionSpec as P

HD = 64
ROT = 16
EPS = 1e-05
MASKED = -1e30
BF = jnp.bfloat16
F32 = jnp.float32


def normalize(rows_in):
    average = jnp.mean(rows_in, axis=-1, keepdims=True)
    centred = rows_in - average
    spread = jnp.mean(centred * centred, axis=-1, keepdims=True)
    root = lax.rsqrt(spread + EPS)
    return centred * root, root


def dot(a, b, dims=((1,), (0,))):
    return lax.dot_general(a, b, (dims, ((), ())), preferred_element_type=F32)


def pack_project(b):
    half = b.shape[0] // 2
    return jnp.concatenate(
        [b[:, :128], jnp.concatenate([b[:half, 128:], b[half:, 128:]], axis=1)], axis=0
    )


def unpack_project(p):
    rest = p[128:192]
    return jnp.concatenate(
        [p[:128], jnp.concatenate([rest[:, :64], rest[:, 64:]], axis=0)], axis=1
    )


def pack_up(b):
    return jnp.concatenate([b[:, :128], b[:, 128:]], axis=0)


def unpack_up(p):
    return jnp.concatenate([p[:128], p[128:256]], axis=1)


def xor_order(stacked, key):
    return [
        lax.dynamic_index_in_dim(stacked, g ^ key, keepdims=False) for g in range(stacked.shape[0])
    ]


def rotary_tables(positions):
    lane = np.arange(2 * HD) % HD
    frequency = np.where(lane < ROT, 10000.0 ** (-(lane % (ROT // 2)) * 2.0 / ROT), 0.0)
    angles = positions[:, None].astype(F32) * jnp.asarray(frequency, F32)[None, :]
    return jnp.cos(angles), jnp.sin(angles)


VMEM_LIMIT = 50 * 1024 * 1024


def roll(value, shift):
    return pltpu.roll(value, shift, 1)


def lanes_of(shape):
    return lax.broadcasted_iota(jnp.int32, shape, 1)


def mlp_kernel(
    where_ref,
    x_ref,
    cot_ref,
    across_ref,
    far_ref,
    own_ref,
    oth_ref,
    norms_ref,
    shift_ref,
    n1_ref,
    xhat_ref,
    call_ref,
    out_ref,
    e_ref,
    send_ref,
    keep_ref,
    small_ref,
    up_s,
    down_s,
    n2_s,
    act_s,
    dh_s,
    ug_s,
    dg_s,
):
    r, key = where_ref[0], where_ref[1]
    count = x_ref.shape[0]
    gains = norms_ref[...]
    sources = (
        (x_ref, cot_ref),
        (far_ref.at[0, 0], far_ref.at[0, 1]),
        (across_ref.at[0], across_ref.at[1]),
        (far_ref.at[1, 0], far_ref.at[1, 1]),
    )
    for j, (rows_in, grad_in) in enumerate(sources):
        at = pl.ds(pl.multiple_of((r ^ j) * count, count), count)
        hat, unused = normalize(rows_in[...].astype(F32))
        xhat_ref[at, :] = hat.astype(BF)
        n1_ref[at, :] = (hat * gains[0:1] + gains[1:2]).astype(BF)
        n2_s[at, :] = (hat * gains[2:3] + gains[3:4]).astype(BF)
        call_ref[at, :] = grad_in[...]
    for k in range(4):
        g = pl.multiple_of((key ^ k) * 128, 128)
        for h, ref in enumerate((own_ref, oth_ref)):
            up_s[pl.ds(g, 128), h * 256 : h * 256 + 128] = ref[k, 0:128]
            up_s[pl.ds(g, 128), h * 256 + 128 : h * 256 + 256] = ref[k, 128:256]
            down_s[h * 256 : h * 256 + 256, pl.ds(g, 128)] = ref[k, 256:512]
    up, down = up_s[...], down_s[...]
    shift = shift_ref[...]
    sums = [jnp.zeros((1, up.shape[1]), F32)] * 3
    for t in range(4):
        at = slice(t * count, t * count + count)
        hidden = dot(n2_s[at, :], up) + shift
        cdf = 0.5 + 0.5 * lax.erf(hidden * math.sqrt(0.5))
        active = (hidden * cdf).astype(BF)
        slope = cdf + hidden * jnp.exp(-0.5 * hidden * hidden) * (1.0 / math.sqrt(2 * math.pi))
        act_s[at, :] = active
        out_ref[at, :] = dot(active, down)
        d_hidden = (dot(call_ref[at, :], down, ((1,), (1,))) * slope).astype(BF)
        dh_s[at, :] = d_hidden
        d_second = dot(d_hidden, up, ((1,), (1,)))
        e_ref[at, :] = d_second * gains[2:3]
        sums[0] += jnp.sum(d_hidden.astype(F32), axis=0, keepdims=True)
        sums[1] += jnp.sum(d_second * xhat_ref[at, :].astype(F32), axis=0, keepdims=True)
        sums[2] += jnp.sum(d_second, axis=0, keepdims=True)
    sums.append(jnp.sum(cot_ref[...].astype(F32), axis=0, keepdims=True))
    for i, row in enumerate(sums):
        small_ref[i : i + 1, :] = row
    small_ref[4:8, :] = jnp.zeros((4, small_ref.shape[1]), F32)
    ug_s[...] = dot(n2_s[...], dh_s[...], ((0,), (0,)))
    dg_s[...] = dot(act_s[...], call_ref[...], ((0,), (0,)))
    for k in range(4):
        g = pl.multiple_of((key ^ k) * 128, 128)
        for h, ref in enumerate((keep_ref, send_ref)):
            ref[k, 0:128] = ug_s[pl.ds(g, 128), h * 256 : h * 256 + 128].astype(ref.dtype)
            ref[k, 128:256] = ug_s[pl.ds(g, 128), h * 256 + 128 : h * 256 + 256].astype(ref.dtype)
            ref[k, 256:512] = dg_s[h * 256 : h * 256 + 256, pl.ds(g, 128)].astype(ref.dtype)


def run_mlp(where, x, cot, across, far, own, oth, norms, shift):
    count, width = x.shape
    tall = 4 * count
    wide = shift.shape[1]
    shape = jax.ShapeDtypeStruct
    return pl.pallas_call(
        mlp_kernel,
        out_shape=(
            shape((tall, width), BF),
            shape((tall, width), BF),
            shape((tall, width), BF),
            shape((tall, width), F32),
            shape((tall, width), F32),
            shape(own.shape, BF),
            shape(own.shape, F32),
            shape((8, wide), F32),
        ),
        in_specs=[pl.BlockSpec(memory_space=pltpu.SMEM)]
        + [pl.BlockSpec(memory_space=pltpu.VMEM)] * 8,
        out_specs=[pl.BlockSpec(memory_space=pltpu.VMEM)] * 8,
        scratch_shapes=[
            pltpu.VMEM((width, wide), BF),
            pltpu.VMEM((wide, width), BF),
            pltpu.VMEM((tall, width), BF),
            pltpu.VMEM((tall, wide), BF),
            pltpu.VMEM((tall, wide), BF),
            pltpu.VMEM((width, wide), F32),
            pltpu.VMEM((wide, width), F32),
        ],
        compiler_params=pltpu.CompilerParams(vmem_limit_bytes=VMEM_LIMIT),
        cost_estimate=pl.CostEstimate(
            flops=12 * tall * width * wide, bytes_accessed=20 * tall * width, transcendentals=0
        ),
        name="feed_forward",
    )(where, x, cot, across, far, own, oth, norms, shift)


def att_kernel(
    last,
    where_ref,
    n1_ref,
    xhat_ref,
    cot_ref,
    slots_ref,
    shift_ref,
    cos_ref,
    sin_ref,
    starts_ref,
    norms_ref,
    out_in,
    e_in,
    *refs,
):
    if last:
        near_ref, rest_ref, grads_ref, small_ref = refs[:4]
    else:
        out_ref, e_ref, grads_ref, small_ref = refs[:4]
    w_s, mix_s, q_s, qh_s, k_s, v_s, ctx_s, dctx_s, dq_s, dt_s, dp_s, pg_s, mg_s, out_s, e_s = refs[4:]
    r, key = where_ref[0], where_ref[1]
    tall = n1_ref.shape[0]
    count = tall // 4
    scaling = HD**-0.5
    mix_s[64:128, :] = jnp.zeros((64, mix_s.shape[1]), BF)
    low = lanes_of((64, 128)) < 64
    for k in range(4):
        g = pl.multiple_of((key ^ k) * 128, 128)
        w_s[pl.ds(g, 128), 0:128] = slots_ref[k, 0:128]
        rest = slots_ref[k, 128:192].astype(F32)
        w_s[pl.ds(g, 64), 128:256] = jnp.where(low, rest, 0.0).astype(BF)
        w_s[pl.ds(g + 64, 64), 128:256] = jnp.where(low, roll(rest, 64), 0.0).astype(BF)
        mix_s[0:64, pl.ds(g, 128)] = slots_ref[k, 192:256]
    w, mix = w_s[...], mix_s[...]
    shift = shift_ref[...]
    lane = lanes_of((count, 128))
    left = lane < 64
    first, second = lane % 64 < ROT // 2, lane % 64 < ROT
    for t in range(4):
        at = slice(t * count, t * count + count)
        projected = dot(n1_ref[at, :], w) + shift
        qk = projected[:, :128]
        sine = sin_ref[at, :]
        minus = jnp.where(first, -sine, 0.0)
        plus = jnp.where(first, 0.0, jnp.where(second, sine, 0.0))
        qk = qk * cos_ref[at, :] + roll(qk, 120) * minus + roll(qk, 8) * plus
        turned = roll(qk, 64)
        q_s[at, :] = jnp.where(left, qk, 0.0).astype(BF)
        k_s[at, :] = jnp.where(left, turned, 0.0).astype(BF)
        qh_s[at, :] = jnp.where(left, 0.0, turned).astype(BF)
        v_s[at, :] = projected[:, 128:].astype(BF)
        dctx_s[at, :] = dot(cot_ref[at, :], mix, ((1,), (1,))).astype(BF)
    dt_s[...] = jnp.zeros(dt_s.shape, F32)
    for t in range(4):
        at = slice(t * count, t * count + count)
        keys = (t + 1) * count
        q, d_context = q_s[at, :], dctx_s[at, :]
        kk, vv = k_s[0:keys, :], v_s[0:keys, :]
        scores = dot(q, kk, ((1,), (1,))) * scaling
        place = lax.broadcasted_iota(jnp.int32, (count, keys), 1)
        row = lax.broadcasted_iota(jnp.int32, (count, 1), 0) + t * count
        allowed = (place >= starts_ref[at, :]) & (place <= row)
        scores = jnp.where(allowed, scores, MASKED)
        exponent = jnp.exp(scores - jnp.max(scores, axis=-1, keepdims=True))
        probability = exponent * (1.0 / jnp.sum(exponent, axis=-1, keepdims=True))
        prob_low = probability.astype(BF)
        ctx_s[at, :] = dot(prob_low, vv).astype(BF)
        d_prob = dot(d_context, vv, ((1,), (1,)))
        weight = jnp.sum(d_prob * probability, axis=-1, keepdims=True)
        d_scores = (probability * (d_prob - weight)).astype(BF)
        dq_s[at, :] = dot(d_scores, kk)
        dt_s[0:128, 0:keys] += dot(qh_s[at, :], d_scores, ((0,), (0,)))
        dt_s[128:256, 0:keys] += dot(d_context, prob_low, ((0,), (0,)))
    sums = [jnp.zeros((1, n1_ref.shape[1]), F32)] * 2
    shift_sum = jnp.zeros((1, 256), F32)
    gain = norms_ref[0:1, :]
    for t in range(4):
        at = slice(t * count, t * count + count)
        turned = jnp.transpose(dt_s[:, at])
        qk = (dq_s[at, :] + turned[:, :128]) * scaling
        sine = sin_ref[at, :]
        minus = jnp.where(first, sine, 0.0)
        plus = jnp.where(first, 0.0, jnp.where(second, -sine, 0.0))
        qk = qk * cos_ref[at, :] + roll(qk, 120) * minus + roll(qk, 8) * plus
        dp_s[at, 0:128] = qk.astype(BF)
        dp_s[at, 128:256] = turned[:, 128:].astype(BF)
        d_projected = dp_s[at, :]
        shift_sum += jnp.sum(d_projected.astype(F32), axis=0, keepdims=True)
        d_first = dot(d_projected, w, ((1,), (1,)))
        sums[0] += jnp.sum(d_first * xhat_ref[at, :].astype(F32), axis=0, keepdims=True)
        sums[1] += jnp.sum(d_first, axis=0, keepdims=True)
        e = e_in[at, :] + d_first * gain
        out = out_in[at, :] + dot(ctx_s[at, :], mix)
        if last:
            out_s[at, :] = out
            e_s[at, :] = e
        else:
            out_ref[at, :] = out
            e_ref[at, :] = e
    small_ref[...] = jnp.zeros(small_ref.shape, F32)
    small_ref[0:1, :] = sums[0]
    small_ref[1:2, :] = sums[1]
    small_ref[2:3, 0:256] = shift_sum
    pg_s[...] = dot(n1_ref[...], dp_s[...], ((0,), (0,)))
    mg_s[...] = dot(ctx_s[...], cot_ref[...], ((0,), (0,)))
    for k in range(4):
        g = pl.multiple_of((key ^ k) * 128, 128)
        grads_ref[k, 0:128] = pg_s[pl.ds(g, 128), 0:128].astype(grads_ref.dtype)
        top, bottom = pg_s[pl.ds(g, 64), 128:256], pg_s[pl.ds(g + 64, 64), 128:256]
        grads_ref[k, 128:192] = jnp.where(low, top, roll(bottom, 64)).astype(grads_ref.dtype)
        grads_ref[k, 192:256] = mg_s[0:64, pl.ds(g, 128)].astype(grads_ref.dtype)
    if last:
        for j in range(4):
            at = pl.ds(pl.multiple_of((r ^ j) * count, count), count)
            target = near_ref if j % 2 else rest_ref
            target[j // 2, 0] = out_s[at, :].astype(target.dtype)
            target[j // 2, 1] = e_s[at, :].astype(target.dtype)


def run_att(last, where, n1, xhat, cot, slots, shift, cosine, sine, starts, norms, out, e):
    tall, width = n1.shape
    count = tall // 4
    shape = jax.ShapeDtypeStruct
    if last:
        results = (shape((2, 2, count, width), BF), shape((2, 2, count, width), F32))
    else:
        results = (shape(out.shape, F32), shape(e.shape, F32))
    return pl.pallas_call(
        functools.partial(att_kernel, last),
        out_shape=results + (shape(slots.shape, F32 if last else BF), shape((8, width), F32)),
        in_specs=[pl.BlockSpec(memory_space=pltpu.SMEM)]
        + [pl.BlockSpec(memory_space=pltpu.VMEM)] * 11,
        out_specs=[pl.BlockSpec(memory_space=pltpu.VMEM)] * 4,
        scratch_shapes=[
            pltpu.VMEM((width, 256), BF),
            pltpu.VMEM((128, width), BF),
            pltpu.VMEM((tall, 128), BF),
            pltpu.VMEM((tall, 128), BF),
            pltpu.VMEM((tall, 128), BF),
            pltpu.VMEM((tall, 128), BF),
            pltpu.VMEM((tall, 128), BF),
            pltpu.VMEM((tall, 128), BF),
            pltpu.VMEM((tall, 128), F32),
            pltpu.VMEM((256, tall), F32),
            pltpu.VMEM((tall, 256), BF),
            pltpu.VMEM((width, 256), F32),
            pltpu.VMEM((128, width), F32),
            pltpu.VMEM((tall, width) if last else (8, 128), F32),
            pltpu.VMEM((tall, width) if last else (8, 128), F32),
        ],
        compiler_params=pltpu.CompilerParams(vmem_limit_bytes=VMEM_LIMIT),
        cost_estimate=pl.CostEstimate(
            flops=24 * tall * width * 128, bytes_accessed=24 * tall * width, transcendentals=0
        ),
        name="attention_last" if last else "attention_first",
    )(where, n1, xhat, cot, slots, shift, cosine, sine, starts, norms, out, e)


def on_device(
    inputs,
    seg_start,
    cotangent,
    project_weight,
    project_bias,
    output_weight,
    output_bias,
    up_weight,
    up_bias,
    down_weight,
    down_bias,
    first_gain,
    first_bias,
    second_gain,
    second_bias,
):
    rows, cols = lax.axis_size("row"), lax.axis_size("col")
    per = cols // rows
    r, c = lax.axis_index("row"), lax.axis_index("col")
    both = ("row", "col")
    count, width = inputs.shape[1], inputs.shape[2]
    paired = per == 2

    def flip(value, bit):
        return lax.ppermute(value, "row", [(i, i ^ bit) for i in range(rows)])

    def home(i, k):
        rr, cc = divmod(i, cols)
        z, y = divmod(cc, per)
        return z * cols + (rr ^ k) * per + y

    everyone = range(rows * cols)

    def spread(block):
        parts = [
            lax.ppermute(block, both, [(i, home(i, k)) for i in everyone]) for k in range(rows)
        ]
        own = jnp.stack(parts)
        return own, lax.ppermute(own, "col", [(i, i ^ 1) for i in range(cols)])

    def bring_other(grads):
        return lax.ppermute(grads, "col", [(i, i ^ 1) for i in range(cols)])

    def collect(grads):
        parts = [
            lax.ppermute(grads[k], both, [(home(i, k), i) for i in everyone]) for k in range(rows)
        ]
        return sum(p.astype(F32) for p in parts)

    def slot_of(i):
        rr, cc = divmod(i, cols)
        return (cc // per) * cols + (cc % per) * rows + rr

    def fetch(block):
        moved = lax.ppermute(block, both, [(i, slot_of(i)) for i in everyone])
        whole = lax.all_gather(moved, "col", axis=0)
        return whole.reshape((per, rows) + block.shape)

    def fetch_columns(block):
        whole = fetch(block).transpose(1, 2, 0, 3).reshape(rows, block.shape[0], 2, -1)
        return whole.transpose(2, 0, 1, 3)

    def fetch_rows(block):
        whole = fetch(block).transpose(1, 0, 2, 3).reshape(rows, 2, -1, block.shape[1])
        return whole.transpose(1, 0, 2, 3)

    def deliver(blocks):
        flat = blocks.reshape((cols,) + blocks.shape[2:]).astype(BF)
        mine = lax.psum_scatter(flat, "col", scatter_dimension=0, tiled=False)
        return lax.ppermute(mine, both, [(slot_of(i), i) for i in everyone]).astype(F32)

    def deliver_columns(halves):
        deep = halves.shape[2]
        whole = halves.transpose(1, 2, 0, 3).reshape(rows, deep, per, -1)
        return deliver(whole.transpose(2, 0, 1, 3))

    def deliver_rows(halves):
        wide = halves.shape[3]
        whole = halves.transpose(1, 0, 2, 3).reshape(rows, per, -1, wide)
        return deliver(whole.transpose(1, 0, 2, 3))

    x_own, cot_own = inputs[0], cotangent[0]
    act = jnp.stack([x_own, cot_own])
    across = flip(act, 2)
    far = flip(jnp.stack([act, across]), 1)

    if paired:
        key, y = c // per, c % per
        mlp_slots = spread(jnp.concatenate([pack_up(up_weight), down_weight], axis=0))
        att_slots = spread(jnp.concatenate([pack_project(project_weight), output_weight], axis=0))
    else:
        key, y = jnp.int32(0), jnp.int32(0)
        ups, downs = fetch_columns(up_weight), fetch_rows(down_weight)
        projects, mixes = fetch_columns(project_weight), fetch_rows(output_weight)
        mlp_slots = [
            jnp.stack(
                [jnp.concatenate([pack_up(ups[h, g]), downs[h, g]], axis=0) for g in range(rows)]
            )
            for h in range(2)
        ]
        att_slots = [
            jnp.stack(
                [
                    jnp.concatenate([pack_project(projects[h, g]), mixes[h, g]], axis=0)
                    for g in range(rows)
                ]
            )
            for h in range(2)
        ]

    seg_own = seg_start[0]
    small = jnp.concatenate(
        [
            first_gain,
            first_bias,
            second_gain,
            second_bias,
            output_bias,
            down_bias,
            project_bias,
            up_bias,
            (seg_own // 32).astype(BF),
            (seg_own % 32).astype(BF),
        ]
    )
    every = lax.all_to_all(
        jnp.broadcast_to(small[None], (rows * cols, small.shape[0])), both, 0, 0, tiled=True
    )
    part = first_gain.shape[0]
    norms = every[:, : 6 * part].reshape(-1, 6, part).transpose(1, 0, 2).reshape(6, -1).astype(F32)
    lengths = (project_bias.shape[0], up_bias.shape[0])
    begin = 6 * part
    mine = lax.dynamic_slice_in_dim(every, r * cols, cols, axis=0)
    project_shift = mine[:, begin : begin + lengths[0]].reshape(2, -1).astype(F32)
    begin += lengths[0]
    up_shift = mine[:, begin : begin + lengths[1]].reshape(2, -1).astype(F32)
    begin += lengths[1]
    project_shift = jnp.where(y == 0, project_shift, project_shift[::-1])
    up_shift = jnp.where(y == 0, up_shift, up_shift[::-1])
    segs = every.reshape(rows, cols, -1)[:, :, begin:]
    segs = lax.dynamic_index_in_dim(segs, c, axis=1, keepdims=False).astype(jnp.int32)
    starts = (segs[:, :count] * 32 + segs[:, count:]).reshape(-1)
    cosine, sine = rotary_tables(jnp.arange(rows * count, dtype=jnp.int32) - starts)

    where = jnp.stack([r, key]).astype(jnp.int32)
    n1, xhat, cot_all, out, e, mlp_send, mlp_keep, mlp_small = run_mlp(
        where, x_own, cot_own, across, far, mlp_slots[0], mlp_slots[1], norms, up_shift.reshape(1, -1)
    )
    project_shift = jnp.pad(project_shift, ((0, 0), (0, HD)))
    shared = (cosine, sine, starts[:, None], norms)
    out, e, att_send, small_oth = run_att(
        False, where, n1, xhat, cot_all, att_slots[1], project_shift[1:], *shared, out, e
    )
    near, rest, att_keep, small_own = run_att(
        True, where, n1, xhat, cot_all, att_slots[0], project_shift[:1], *shared, out, e
    )
    ub_own, ub_oth = mlp_small[0, : up_shift.shape[1]], mlp_small[0, up_shift.shape[1] :]
    pb_own, pb_oth = small_own[2, : 3 * HD], small_oth[2, : 3 * HD]

    if paired:
        mlp_done = collect((mlp_keep + bring_other(mlp_send).astype(F32)).astype(BF))
        att_done = collect((att_keep + bring_other(att_send).astype(F32)).astype(BF))
        project_done, mix_done = unpack_project(att_done[:192]), att_done[192:]
        up_done, down_done = unpack_up(mlp_done[:256]), mlp_done[256:]
    else:
        att_grads, mlp_grads = jnp.stack([att_keep, att_send.astype(F32)]), jnp.stack([mlp_keep, mlp_send.astype(F32)])
        every_pair = [(h, g) for h in range(2) for g in range(rows)]

        def regroup(parts):
            return jnp.stack(parts).reshape((2, rows) + parts[0].shape)

        project_done = deliver_columns(
            regroup([unpack_project(att_grads[h, g][:192]) for h, g in every_pair])
        )
        mix_done = deliver_rows(regroup([att_grads[h, g][192:] for h, g in every_pair]))
        up_done = deliver_columns(
            regroup([unpack_up(mlp_grads[h, g][:256]) for h, g in every_pair])
        )
        down_done = deliver_rows(regroup([mlp_grads[h, g][256:] for h, g in every_pair]))

    mine = rest + flip(near, 1).astype(F32)
    total = mine[0] + flip(mine[1].astype(BF), 2).astype(F32)
    x_own, cot_own = x_own.astype(F32), cot_own.astype(F32)
    output = (x_own + total[0] + norms[4] + norms[5]).astype(BF)[None]
    e_all = total[1]
    xhat_own, root_own = normalize(x_own)
    input_grad = cot_own + root_own * (
        e_all
        - jnp.mean(e_all, axis=-1, keepdims=True)
        - xhat_own * jnp.mean(e_all * xhat_own, axis=-1, keepdims=True)
    )

    everywhere = jnp.concatenate([small_own[:2] + small_oth[:2], mlp_small[1:4]])
    everywhere = everywhere.reshape(5, rows * cols, part).transpose(1, 0, 2).reshape(rows * cols, -1)

    def by_half(own, other):
        first = jnp.where(y == 0, own, other)
        second = jnp.where(y == 0, other, own)
        return jnp.concatenate([first, second]).reshape(cols, -1)

    local = jnp.concatenate([by_half(pb_own, pb_oth), by_half(ub_own, ub_oth)], axis=1)
    local = lax.dynamic_update_slice(
        jnp.zeros((rows * cols, local.shape[1]), F32), local, (r * cols, 0)
    )
    sums = lax.all_to_all(
        jnp.concatenate([everywhere, local], axis=1), both, 0, 0, tiled=True
    ).sum(axis=0)
    pieces = [sums[i * part : (i + 1) * part] for i in range(5)]
    project_shift_grad = sums[5 * part : 5 * part + lengths[0]]
    up_shift_grad = sums[5 * part + lengths[0] :]
    return (
        output,
        input_grad[None],
        project_done,
        project_shift_grad,
        mix_done,
        pieces[4],
        up_done,
        up_shift_grad,
        down_done,
        pieces[4],
        pieces[0],
        pieces[1],
        pieces[2],
        pieces[3],
    )


def solution(mesh):
    return jax.shard_map(
        on_device,
        mesh=mesh,
        in_specs=(
            P("col", "row", None),
            P("col", "row"),
            P("col", "row", None),
            P("row", "col"),
            P(("row", "col")),
            P("col", "row"),
            P(("row", "col")),
            P("row", "col"),
            P(("row", "col")),
            P("col", "row"),
            P(("row", "col")),
            P(("row", "col")),
            P(("row", "col")),
            P(("row", "col")),
            P(("row", "col")),
        ),
        out_specs=(
            P("col", "row", None),
            P("col", "row", None),
            P("row", "col"),
            P(("row", "col")),
            P("col", "row"),
            P(("row", "col")),
            P("row", "col"),
            P(("row", "col")),
            P("col", "row"),
            P(("row", "col")),
            P(("row", "col")),
            P(("row", "col")),
            P(("row", "col")),
            P(("row", "col")),
        ),
        check_vma=False,
    )
```

```python
import functools
import math

import jax
import jax.numpy as jnp
import numpy as np
from jax import lax
from jax.experimental import pallas as pl
from jax.experimental.pallas import tpu as pltpu
from jax.sharding import PartitionSpec as P

HD = 64
ROT = 16
EPS = 1e-05
MASKED = -1e30
BF = jnp.bfloat16
F32 = jnp.float32


def normalize(rows_in):
    average = jnp.mean(rows_in, axis=-1, keepdims=True)
    centred = rows_in - average
    spread = jnp.mean(centred * centred, axis=-1, keepdims=True)
    root = lax.rsqrt(spread + EPS)
    return centred * root, root


def dot(a, b, dims=((1,), (0,))):
    return lax.dot_general(a, b, (dims, ((), ())), preferred_element_type=F32)


def pack_att(project, mix):
    return jnp.concatenate([project.T, mix], axis=0)


def pack_mlp(up, down):
    return jnp.concatenate([up[:, :128], up[:, 128:], down], axis=0)


def unpack_up(p):
    return jnp.concatenate([p[:128], p[128:256]], axis=1)


def rotary_tables(positions):
    lane = np.arange(2 * HD) % HD
    frequency = np.where(lane < ROT, 10000.0 ** (-(lane % (ROT // 2)) * 2.0 / ROT), 0.0)
    angles = positions[:, None].astype(F32) * jnp.asarray(frequency, F32)[None, :]
    return jnp.cos(angles), jnp.sin(angles)


VMEM_LIMIT = 24 << 20


def roll(value, shift):
    return pltpu.roll(value, shift, 1)


def lanes_of(shape):
    return lax.broadcasted_iota(jnp.int32, shape, 1)


VMEM = pl.BlockSpec(memory_space=pltpu.VMEM)
SMEM = pl.BlockSpec(memory_space=pltpu.SMEM)
SHAPE = jax.ShapeDtypeStruct
LINES = 8


def call(kernel, name, work, operands, results, scratch):
    return pl.pallas_call(
        kernel,
        out_shape=results,
        in_specs=[SMEM] + [VMEM] * (len(operands) - 1),
        out_specs=[VMEM] * len(results),
        scratch_shapes=[pltpu.VMEM(size, dtype) for size, dtype in scratch],
        compiler_params=pltpu.CompilerParams(vmem_limit_bytes=VMEM_LIMIT),
        cost_estimate=pl.CostEstimate(flops=work, bytes_accessed=work // 400, transcendentals=0),
        name=name,
    )(*operands)


def fetch_in(sources, held, sems):
    copies = [
        pltpu.make_async_copy(source, target, sems.at[i])
        for i, (source, target) in enumerate(zip(sources, held))
    ]
    for copy in copies:
        copy.start()
    for copy in copies:
        copy.wait()


def prepare_kernel(paired, *refs):
    sources, (small_ref, *packs), held = refs[:13], refs[13 : 14 + 2 * paired], refs[14 + 2 * paired :]
    line, sems = held[13], held[14]
    fetch_in(sources, held, sems)
    seg_ref, project_ref, mix_ref, up_ref, down_ref, *vectors = held[:13]
    if paired:
        att, mlp = packs
        att[0:192, :] = project_ref[...]
        att[192:256, :] = mix_ref[...]
        mlp[0:128, :] = up_ref[:, 0:128]
        mlp[128:256, :] = up_ref[:, 128:256]
        mlp[256:512, :] = down_ref[...]
    line[...] = jnp.zeros(line.shape, F32)
    part = vectors[0].shape[1]
    for i in range(6):
        line[0:1, i * part : (i + 1) * part] = vectors[i][...].astype(F32)
    line[1:2, 0 : vectors[6].shape[1]] = vectors[6][...].astype(F32)
    line[2:3, 0 : vectors[7].shape[1]] = vectors[7][...].astype(F32)
    seg = seg_ref[...]
    blocks = seg.shape[1] // 128
    for i in range(blocks):
        piece = seg[:, i * 128 : (i + 1) * 128]
        line[3 + i : 4 + i, :] = (piece >> 5).astype(F32)
        line[3 + blocks + i : 4 + blocks + i, :] = (piece & 31).astype(F32)
    full = line[...].astype(BF)
    for i in range(small_ref.shape[0]):
        small_ref[i] = full


def run_local(kernel, name, work, sources, results, scratch):
    return pl.pallas_call(
        kernel,
        out_shape=results,
        in_specs=[pl.BlockSpec(memory_space=pl.ANY)] * len(sources),
        out_specs=[VMEM] * len(results),
        scratch_shapes=[pltpu.VMEM(v.shape, v.dtype) for v in sources]
        + scratch
        + [pltpu.SemaphoreType.DMA((len(sources),))],
        compiler_params=pltpu.CompilerParams(vmem_limit_bytes=60 << 20),
        cost_estimate=pl.CostEstimate(flops=work, bytes_accessed=1 << 20, transcendentals=0),
        name=name,
    )(*sources)


def layout_kernel(rows, cols, sizes, where_ref, every_ref, norms_ref, project_ref, up_ref, starts_ref):
    c, y, group = where_ref[2], where_ref[3], where_ref[4]
    part, project, up = sizes
    copies = every_ref.shape[0]

    def spread_out(block, lane_of, row_of, wide):
        lane = lax.broadcasted_iota(jnp.int32, (128, wide), 0)
        place = lax.broadcasted_iota(jnp.int32, (128, wide), 1)
        picked = dot(block, jnp.where(lane == lane_of(place), 1.0, 0.0).astype(BF))
        device = lax.broadcasted_iota(jnp.int32, (copies, wide), 0)
        place = lax.broadcasted_iota(jnp.int32, (copies, wide), 1)
        return jnp.sum(jnp.where(device == row_of(place), picked, 0.0), axis=0, keepdims=True)

    def line(i):
        return every_ref[:, i, :]

    wide = norms_ref.shape[1]
    rows_of = [line(i) for i in range(LINES)]
    for i in range(6):
        norms_ref[i : i + 1, :] = spread_out(
            rows_of[0], lambda n: i * part + n % part, lambda n: n // part, wide
        )
    norms_ref[6:8, :] = jnp.zeros((2, wide), F32)
    half = cols // 2
    for h in range(2):
        begin = group * cols + (h ^ y) * half
        project_ref[h : h + 1, :] = spread_out(
            rows_of[1],
            lambda n: n % project,
            lambda n: jnp.where(n < half * project, begin + n // project, -1),
            256,
        )
        up_ref[:, h * 256 : h * 256 + 256] = spread_out(
            rows_of[2], lambda n: n % up, lambda n: begin + n // up, 256
        )
    device = lax.broadcasted_iota(jnp.int32, (copies, 128), 0)
    eye = lax.broadcasted_iota(jnp.int32, (128, 128), 0) == lanes_of((128, 128))
    count = starts_ref.shape[0] // rows
    blocks = count // 128
    for g in range(rows):
        here = device == g * cols + c
        for b in range(blocks):
            coarse, fine = rows_of[3 + b].astype(F32), rows_of[3 + blocks + b].astype(F32)
            value = jnp.sum(jnp.where(here, coarse * 32.0 + fine, 0.0), axis=0, keepdims=True)
            column = jnp.sum(jnp.where(eye, value, 0.0), axis=1, keepdims=True)
            begin = g * count + b * 128
            starts_ref[begin : begin + 128, :] = column.astype(jnp.int32)


def mlp_kernel(
    where_ref,
    n2_ref,
    xhat_ref,
    cot_ref,
    own_ref,
    oth_ref,
    norms_ref,
    shift_ref,
    out_ref,
    e_ref,
    send_ref,
    keep_ref,
    small_ref,
    up_s,
    down_s,
    act_s,
    dh_s,
    ug_s,
    dg_s,
):
    r, key = where_ref[0], where_ref[1]
    count = n2_ref.shape[0] // 4
    gain = norms_ref[2:3, :]
    for k in range(4):
        g = pl.multiple_of((key ^ k) * 128, 128)
        for h, ref in enumerate((own_ref, oth_ref)):
            b = ref.shape[1] - 512
            up_s[pl.ds(g, 128), h * 256 : h * 256 + 128] = ref[k, b : b + 128]
            up_s[pl.ds(g, 128), h * 256 + 128 : h * 256 + 256] = ref[k, b + 128 : b + 256]
            down_s[h * 256 : h * 256 + 256, pl.ds(g, 128)] = ref[k, b + 256 : b + 512]
    up, down = up_s[...], down_s[...]
    shift = shift_ref[...]
    sums = [jnp.zeros((1, up.shape[1]), F32)] * 3
    for t in range(4):
        at = slice(t * count, t * count + count)
        hidden = dot(n2_ref[at, :], up) + shift
        cdf = 0.5 + 0.5 * lax.erf(hidden * math.sqrt(0.5))
        active = (hidden * cdf).astype(BF)
        slope = cdf + hidden * jnp.exp(-0.5 * hidden * hidden) * (1.0 / math.sqrt(2 * math.pi))
        act_s[at, :] = active
        out_ref[at, :] = dot(active, down).astype(BF)
        d_hidden = (dot(cot_ref[at, :], down, ((1,), (1,))) * slope).astype(BF)
        dh_s[at, :] = d_hidden
        d_second = dot(d_hidden, up, ((1,), (1,)))
        e_ref[at, :] = (d_second * gain).astype(BF)
        sums[0] += jnp.sum(d_hidden.astype(F32), axis=0, keepdims=True)
        sums[1] += jnp.sum(d_second * xhat_ref[at, :].astype(F32), axis=0, keepdims=True)
        sums[2] += jnp.sum(d_second, axis=0, keepdims=True)
    mine = cot_ref[pl.ds(pl.multiple_of(r * count, count), count), :]
    sums.append(jnp.sum(mine.astype(F32), axis=0, keepdims=True))
    for i, row in enumerate(sums):
        small_ref[i : i + 1, :] = row
    small_ref[4:8, :] = jnp.zeros((4, small_ref.shape[1]), F32)
    ug_s[...] = dot(n2_ref[...], dh_s[...], ((0,), (0,)))
    dg_s[...] = dot(act_s[...], cot_ref[...], ((0,), (0,)))
    for k in range(4):
        g = pl.multiple_of((key ^ k) * 128, 128)
        for h, ref in enumerate((keep_ref, send_ref)):
            ref[k, 0:128] = ug_s[pl.ds(g, 128), h * 256 : h * 256 + 128].astype(ref.dtype)
            ref[k, 128:256] = ug_s[pl.ds(g, 128), h * 256 + 128 : h * 256 + 256].astype(ref.dtype)
            ref[k, 256:512] = dg_s[h * 256 : h * 256 + 256, pl.ds(g, 128)].astype(ref.dtype)


def run_mlp(where, n2, xhat, cot, own, oth, norms, shift):
    tall, width = n2.shape
    wide = shift.shape[1]
    return call(
        mlp_kernel,
        "feed_forward",
        1 << 35,
        (where, n2, xhat, cot, own, oth, norms, shift),
        (
            SHAPE((tall, width), BF),
            SHAPE((tall, width), BF),
            SHAPE(oth.shape, BF),
            SHAPE(oth.shape, F32),
            SHAPE((8, wide), F32),
        ),
        (
            ((width, wide), BF),
            ((wide, width), BF),
            ((tall, wide), BF),
            ((tall, wide), BF),
            ((width, wide), F32),
            ((wide, width), F32),
        ),
    )


def head(key, n1_ref, cot_ref, slots_ref, shift, cos_ref, sin_ref, starts_ref, w, mix, ctx, dp, grads_ref, scratch):
    q_s, qh_s, k_s, v_s, dctx_s, dq_s, dt_s, pg_s, mg_s = scratch
    tall = n1_ref.shape[0]
    count = tall // 4
    scaling = HD**-0.5
    w[192:256, :] = jnp.zeros((64, w.shape[1]), BF)
    mix[64:128, :] = jnp.zeros((64, mix.shape[1]), BF)
    for k in range(4):
        g = pl.multiple_of((key ^ k) * 128, 128)
        w[0:192, pl.ds(g, 128)] = slots_ref[k, 0:192]
        mix[0:64, pl.ds(g, 128)] = slots_ref[k, 192:256]
    lane = lanes_of((count, 128))
    left = lane < 64
    first, second = lane % 64 < ROT // 2, lane % 64 < ROT

    def turn(qk, at, sign):
        sine = sin_ref[at, :] * sign
        minus = jnp.where(first, -sine, 0.0)
        plus = jnp.where(first, 0.0, jnp.where(second, sine, 0.0))
        return qk * cos_ref[at, :] + roll(qk, 120) * minus + roll(qk, 8) * plus

    for t in range(4):
        at = slice(t * count, t * count + count)
        projected = dot(n1_ref[at, :], w[...], ((1,), (1,))) + shift
        qk = turn(projected[:, :128], at, 1.0)
        turned = roll(qk, 64)
        q_s[at, :] = jnp.where(left, qk, 0.0).astype(BF)
        k_s[at, :] = jnp.where(left, turned, 0.0).astype(BF)
        qh_s[at, :] = jnp.where(left, 0.0, turned).astype(BF)
        v_s[at, :] = projected[:, 128:].astype(BF)
        dctx_s[at, :] = dot(cot_ref[at, :], mix[...], ((1,), (1,))).astype(BF)
    dt_s[...] = jnp.zeros(dt_s.shape, F32)
    for t in range(4):
        at = slice(t * count, t * count + count)
        keys = (t + 1) * count
        q, d_context = q_s[at, :], dctx_s[at, :]
        kk, vv = k_s[0:keys, :], v_s[0:keys, :]
        scores = dot(q, kk, ((1,), (1,))) * scaling
        place = lax.broadcasted_iota(jnp.int32, (count, keys), 1)
        row = lax.broadcasted_iota(jnp.int32, (count, 1), 0) + t * count
        allowed = (place >= starts_ref[at, :]) & (place <= row)
        scores = jnp.where(allowed, scores, MASKED)
        exponent = jnp.exp(scores - jnp.max(scores, axis=-1, keepdims=True))
        probability = exponent * (1.0 / jnp.sum(exponent, axis=-1, keepdims=True))
        prob_low = probability.astype(BF)
        ctx[at, :] = dot(prob_low, vv).astype(BF)
        d_prob = dot(d_context, vv, ((1,), (1,)))
        weight = jnp.sum(d_prob * probability, axis=-1, keepdims=True)
        d_scores = (probability * (d_prob - weight)).astype(BF)
        dq_s[at, :] = dot(d_scores, kk)
        dt_s[0:128, 0:keys] += dot(qh_s[at, :], d_scores, ((0,), (0,)))
        dt_s[128:256, 0:keys] += dot(d_context, prob_low, ((0,), (0,)))
    shift_sum = jnp.zeros((1, 256), F32)
    for t in range(4):
        at = slice(t * count, t * count + count)
        turned = jnp.transpose(dt_s[:, at])
        qk = turn((dq_s[at, :] + turned[:, :128]) * scaling, at, -1.0)
        dp[at, 0:128] = qk.astype(BF)
        dp[at, 128:256] = turned[:, 128:].astype(BF)
        shift_sum += jnp.sum(dp[at, :].astype(F32), axis=0, keepdims=True)
    pg_s[...] = dot(dp[...], n1_ref[...], ((0,), (0,)))
    mg_s[...] = dot(ctx[...], cot_ref[...], ((0,), (0,)))
    for k in range(4):
        g = pl.multiple_of((key ^ k) * 128, 128)
        grads_ref[k, 0:192] = pg_s[0:192, pl.ds(g, 128)].astype(grads_ref.dtype)
        grads_ref[k, 192:256] = mg_s[0:64, pl.ds(g, 128)].astype(grads_ref.dtype)
    return shift_sum


def head_scratch(tall, width):
    return (
        ((tall, 128), BF),
        ((tall, 128), BF),
        ((tall, 128), BF),
        ((tall, 128), BF),
        ((tall, 128), BF),
        ((tall, 128), F32),
        ((256, tall), F32),
        ((256, width), F32),
        ((128, width), F32),
    )


def first_kernel(
    where_ref,
    x0_ref,
    x1_ref,
    x2_ref,
    x3_ref,
    cot0_ref,
    cot1_ref,
    cot2_ref,
    cot3_ref,
    slots_ref,
    shift_ref,
    cos_ref,
    sin_ref,
    starts_ref,
    norms_ref,
    n1_ref,
    n2_ref,
    xhat_ref,
    cot_ref,
    w_ref,
    mix_ref,
    ctx_ref,
    dp_ref,
    grads_ref,
    small_ref,
    *scratch,
):
    r, key = where_ref[0], where_ref[1]
    count = x0_ref.shape[0]
    norms = norms_ref[...]
    grads_in = (cot0_ref, cot1_ref, cot2_ref, cot3_ref)
    for j, source in enumerate((x0_ref, x1_ref, x2_ref, x3_ref)):
        at = pl.ds(pl.multiple_of((r ^ j) * count, count), count)
        hat, unused = normalize(source[...].astype(F32))
        xhat_ref[at, :] = hat.astype(BF)
        n1_ref[at, :] = (hat * norms[0:1] + norms[1:2]).astype(BF)
        n2_ref[at, :] = (hat * norms[2:3] + norms[3:4]).astype(BF)
        cot_ref[at, :] = grads_in[j][...]
    small_ref[...] = jnp.zeros(small_ref.shape, F32)
    small_ref[0:1, 0:256] = head(
        key,
        n1_ref,
        cot_ref,
        slots_ref,
        shift_ref[0:1, :],
        cos_ref,
        sin_ref,
        starts_ref,
        w_ref,
        mix_ref,
        ctx_ref,
        dp_ref,
        grads_ref,
        scratch,
    )


def run_first(where, chunks, slots, shift, cosine, sine, starts, norms):
    count, width = chunks[0].shape
    tall = 4 * count
    return call(
        first_kernel,
        "attention_first",
        1 << 35,
        (where, *chunks, slots, shift, cosine, sine, starts, norms),
        (
            SHAPE((tall, width), BF),
            SHAPE((tall, width), BF),
            SHAPE((tall, width), BF),
            SHAPE((tall, width), BF),
            SHAPE((256, width), BF),
            SHAPE((128, width), BF),
            SHAPE((tall, 128), BF),
            SHAPE((tall, 256), BF),
            SHAPE((4, 256, 128), F32),
            SHAPE((8, width), F32),
        ),
        head_scratch(tall, width),
    )


def second_kernel(
    where_ref,
    n1_ref,
    cot_ref,
    slots_ref,
    shift_ref,
    cos_ref,
    sin_ref,
    starts_ref,
    w_ref,
    mix_ref,
    ctx_ref,
    dp_ref,
    grads_ref,
    small_ref,
    *scratch,
):
    small_ref[...] = jnp.zeros(small_ref.shape, F32)
    small_ref[0:1, 0:256] = head(
        where_ref[1],
        n1_ref,
        cot_ref,
        slots_ref,
        shift_ref[1:2, :],
        cos_ref,
        sin_ref,
        starts_ref,
        w_ref,
        mix_ref,
        ctx_ref,
        dp_ref,
        grads_ref,
        scratch,
    )


def run_second(where, n1, cot, slots, shift, cosine, sine, starts):
    tall, width = n1.shape
    return call(
        second_kernel,
        "attention_second",
        1 << 35,
        (where, n1, cot, slots, shift, cosine, sine, starts),
        (
            SHAPE((256, width), BF),
            SHAPE((128, width), BF),
            SHAPE((tall, 128), BF),
            SHAPE((tall, 256), BF),
            SHAPE((4, 256, 128), BF),
            SHAPE((8, width), F32),
        ),
        head_scratch(tall, width),
    )


def join_kernel(
    where_ref,
    xhat_ref,
    norms_ref,
    w_a,
    mix_a,
    ctx_a,
    dp_a,
    w_b,
    mix_b,
    ctx_b,
    dp_b,
    out_in,
    e_in,
    near_ref,
    rest_ref,
    small_ref,
):
    r = where_ref[0]
    count = xhat_ref.shape[0] // 4
    sums = [jnp.zeros((1, xhat_ref.shape[1]), F32)] * 2
    gain = norms_ref[0:1, :]
    for j in range(4):
        at = pl.ds(pl.multiple_of((r ^ j) * count, count), count)
        d_first = dot(dp_a[at, :], w_a[...]) + dot(dp_b[at, :], w_b[...])
        sums[0] += jnp.sum(d_first * xhat_ref[at, :].astype(F32), axis=0, keepdims=True)
        sums[1] += jnp.sum(d_first, axis=0, keepdims=True)
        out = dot(ctx_a[at, :], mix_a[...]) + dot(ctx_b[at, :], mix_b[...])
        target = near_ref if j % 2 else rest_ref
        target[j // 2, 0] = (out_in[at, :].astype(F32) + out).astype(target.dtype)
        target[j // 2, 1] = (e_in[at, :].astype(F32) + d_first * gain).astype(target.dtype)
    small_ref[...] = jnp.zeros(small_ref.shape, F32)
    small_ref[0:1, :] = sums[0]
    small_ref[1:2, :] = sums[1]


def run_join(where, xhat, norms, first, second, out, e):
    tall, width = xhat.shape
    count = tall // 4
    return call(
        join_kernel,
        "join",
        1 << 35,
        (where, xhat, norms, *first, *second, out, e),
        (
            SHAPE((2, 2, count, width), BF),
            SHAPE((2, 2, count, width), F32),
            SHAPE((8, width), F32),
        ),
        (),
    )


def merge_kernel(unused, att_keep, att_come, mlp_keep, mlp_come, *outs):
    for k in range(4):
        outs[k][0:256, :] = (att_keep[k] + att_come[k].astype(F32)).astype(BF)
        outs[k][256:768, :] = (mlp_keep[k] + mlp_come[k].astype(F32)).astype(BF)


def collect_kernel(unused, a_ref, b_ref, c_ref, d_ref, project_ref, mix_ref, up_ref, down_ref):
    def total(begin, end):
        refs = (a_ref, b_ref, c_ref, d_ref)
        return sum(ref[begin:end, :].astype(F32) for ref in refs)

    project_ref[...] = total(0, 192)
    mix_ref[...] = total(192, 256)
    up_ref[:, 0:128] = total(256, 384)
    up_ref[:, 128:256] = total(384, 512)
    down_ref[...] = total(512, 768)


def on_device(
    inputs,
    seg_start,
    cotangent,
    project_weight,
    project_bias,
    output_weight,
    output_bias,
    up_weight,
    up_bias,
    down_weight,
    down_bias,
    first_gain,
    first_bias,
    second_gain,
    second_bias,
):
    rows, cols = lax.axis_size("row"), lax.axis_size("col")
    per = cols // rows
    r, c = lax.axis_index("row"), lax.axis_index("col")
    both = ("row", "col")
    count, width = inputs.shape[1], inputs.shape[2]
    paired = per == 2

    def flip(value, bit):
        return lax.ppermute(value, "row", [(i, i ^ bit) for i in range(rows)])

    def group_of(i):
        return (i % 2) * 2 + i // 2

    def home(i, k):
        rr, cc = divmod(i, cols)
        z, y = divmod(cc, per)
        return group_of(z) * cols + (rr ^ k) * per + y

    everyone = range(rows * cols)

    def beside(value):
        return lax.ppermute(value, "col", [(i, i ^ 1) for i in range(cols)])

    def spread(block):
        return [lax.ppermute(block, both, [(i, home(i, k)) for i in everyone]) for k in range(rows)]

    def bring(blocks):
        return [
            lax.ppermute(b, both, [(home(i, k), i) for i in everyone]) for k, b in enumerate(blocks)
        ]

    def slot_of(i):
        rr, cc = divmod(i, cols)
        return group_of(cc // per) * cols + (cc % per) * rows + rr

    def fetch(block):
        moved = lax.ppermute(block, both, [(i, slot_of(i)) for i in everyone])
        whole = lax.all_gather(moved, "col", axis=0)
        return whole.reshape((per, rows) + block.shape)

    def fetch_columns(block):
        whole = fetch(block).transpose(1, 2, 0, 3).reshape(rows, block.shape[0], 2, -1)
        return whole.transpose(2, 0, 1, 3)

    def fetch_rows(block):
        whole = fetch(block).transpose(1, 0, 2, 3).reshape(rows, 2, -1, block.shape[1])
        return whole.transpose(1, 0, 2, 3)

    def deliver(blocks):
        flat = blocks.reshape((cols,) + blocks.shape[2:]).astype(BF)
        mine = lax.psum_scatter(flat, "col", scatter_dimension=0, tiled=False)
        return lax.ppermute(mine, both, [(slot_of(i), i) for i in everyone]).astype(F32)

    def deliver_columns(halves):
        deep = halves.shape[2]
        whole = halves.transpose(1, 2, 0, 3).reshape(rows, deep, per, -1)
        return deliver(whole.transpose(2, 0, 1, 3))

    def deliver_rows(halves):
        wide = halves.shape[3]
        whole = halves.transpose(1, 0, 2, 3).reshape(rows, per, -1, wide)
        return deliver(whole.transpose(1, 0, 2, 3))

    if paired:
        key, y = c // per, c % per
    else:
        key, y = jnp.int32(0), jnp.int32(0)
    group = group_of(r)
    where = jnp.stack([r, key, c, y, group]).astype(jnp.int32)
    part, project_len, up_len = first_gain.shape[0], project_bias.shape[0], up_bias.shape[0]
    copies = rows * cols
    x_own, cot_own = inputs[0], cotangent[0]
    x_across, cot_across = flip(x_own, 2), flip(cot_own, 2)
    x_far, cot_far = flip(x_own, 1), flip(cot_own, 1)
    chunks = (x_own, x_far, x_across, flip(x_across, 1))
    chunks += (cot_own, cot_far, cot_across, flip(cot_across, 1))
    vectors = (
        first_gain,
        first_bias,
        second_gain,
        second_bias,
        output_bias,
        down_bias,
        project_bias,
        up_bias,
    )
    results = [SHAPE((copies, LINES, 128), BF)]
    if paired:
        results += [SHAPE((256, 128), BF), SHAPE((512, 128), BF)]
    small, *packs = run_local(
        functools.partial(prepare_kernel, paired),
        "prepare",
        1 << 20,
        (seg_start, project_weight.T, output_weight, up_weight, down_weight)
        + tuple(v[None] for v in vectors),
        results,
        [pltpu.VMEM((LINES, 128), F32)],
    )
    every = lax.all_to_all(small, both, 0, 0, tiled=True)
    if paired:
        att_own, mlp_own = jnp.stack(spread(packs[0])), jnp.stack(spread(packs[1]))
        att_slots = att_own, beside(att_own)
        mlp_slots = mlp_own, beside(mlp_own)
    else:
        ups, downs = fetch_columns(up_weight), fetch_rows(down_weight)
        projects, mixes = fetch_columns(project_weight), fetch_rows(output_weight)
        mlp_slots = [
            jnp.stack(
                [pack_mlp(ups[h, g], downs[h, g]) for g in range(rows)]
            )
            for h in range(2)
        ]
        att_slots = [
            jnp.stack(
                [pack_att(projects[h, g], mixes[h, g]) for g in range(rows)]
            )
            for h in range(2)
        ]

    norms, project_shift, up_shift, starts = call(
        functools.partial(layout_kernel, rows, cols, (part, project_len, up_len)),
        "layout",
        1 << 24,
        (where, every),
        (
            SHAPE((8, width), F32),
            SHAPE((2, 256), F32),
            SHAPE((1, 512), F32),
            SHAPE((rows * count, 1), jnp.int32),
        ),
        (),
    )
    cosine, sine = rotary_tables(jnp.arange(rows * count, dtype=jnp.int32) - starts[:, 0])

    n1, n2, xhat, cot_all, *first, att_keep, small_own = run_first(
        where, chunks, att_slots[0], project_shift, cosine, sine, starts, norms
    )
    *second, att_send, small_oth = run_second(
        where, n1, cot_all, att_slots[1], project_shift, cosine, sine, starts
    )
    out, e, mlp_send, mlp_keep, mlp_small = run_mlp(
        where, n2, xhat, cot_all, mlp_slots[0], mlp_slots[1], norms, up_shift
    )
    near, rest, small_join = run_join(where, xhat, norms, first, second, out, e)
    ub_own, ub_oth = mlp_small[0, :256], mlp_small[0, 256:]
    pb_own, pb_oth = small_own[0, : 3 * HD], small_oth[0, : 3 * HD]

    mine = rest + flip(near, 1).astype(F32)
    total = mine[0] + flip(mine[1].astype(BF), 2).astype(F32)
    x_own, cot_own = inputs[0].astype(F32), cotangent[0].astype(F32)
    output = (x_own + total[0] + norms[4] + norms[5]).astype(BF)[None]
    e_all = total[1]
    xhat_own, root_own = normalize(x_own)
    input_grad = cot_own + root_own * (
        e_all
        - jnp.mean(e_all, axis=-1, keepdims=True)
        - xhat_own * jnp.mean(e_all * xhat_own, axis=-1, keepdims=True)
    )

    if paired:
        blocks = call(
            merge_kernel,
            "merge",
            1 << 26,
            (where, att_keep, beside(att_send), mlp_keep, beside(mlp_send)),
            (SHAPE((768, 128), BF),) * 4,
            (),
        )
    else:
        att_grads, mlp_grads = jnp.stack([att_keep, att_send.astype(F32)]), jnp.stack([mlp_keep, mlp_send.astype(F32)])
        every_pair = [(h, g) for h in range(2) for g in range(rows)]

        def regroup(parts):
            return jnp.stack(parts).reshape((2, rows) + parts[0].shape)

        project_done = deliver_columns(
            regroup([att_grads[h, g][:192].T for h, g in every_pair])
        )
        mix_done = deliver_rows(regroup([att_grads[h, g][192:] for h, g in every_pair]))
        up_done = deliver_columns(
            regroup([unpack_up(mlp_grads[h, g][:256]) for h, g in every_pair])
        )
        down_done = deliver_rows(regroup([mlp_grads[h, g][256:] for h, g in every_pair]))

    everywhere = jnp.concatenate([small_join[:2], mlp_small[1:4]])
    everywhere = everywhere.reshape(5, rows * cols, part).transpose(1, 0, 2).reshape(rows * cols, -1)

    def by_half(own, other):
        first = jnp.where(y == 0, own, other)
        second = jnp.where(y == 0, other, own)
        return jnp.concatenate([first, second]).reshape(cols, -1)

    local = jnp.concatenate([by_half(pb_own, pb_oth), by_half(ub_own, ub_oth)], axis=1)
    local = lax.dynamic_update_slice(
        jnp.zeros((rows * cols, local.shape[1]), F32), local, (group * cols, 0)
    )
    small = jnp.concatenate([everywhere, local], axis=1)
    if paired:
        small, blocks = lax.optimization_barrier((small, blocks))
    sums = lax.all_to_all(small, both, 0, 0, tiled=True).sum(axis=0)
    if paired:
        project_done, mix_done, up_done, down_done = call(
            collect_kernel,
            "collect",
            1 << 26,
            (where, *bring(blocks)),
            (
                SHAPE(project_weight.shape[::-1], F32),
                SHAPE(output_weight.shape, F32),
                SHAPE(up_weight.shape, F32),
                SHAPE(down_weight.shape, F32),
            ),
            (),
        )
        project_done = project_done.T
    pieces = [sums[i * part : (i + 1) * part] for i in range(5)]
    project_shift_grad = sums[5 * part : 5 * part + project_len]
    up_shift_grad = sums[5 * part + project_len :]
    return (
        output,
        input_grad[None],
        project_done,
        project_shift_grad,
        mix_done,
        pieces[4],
        up_done,
        up_shift_grad,
        down_done,
        pieces[4],
        pieces[0],
        pieces[1],
        pieces[2],
        pieces[3],
    )


def solution(mesh):
    return jax.shard_map(
        on_device,
        mesh=mesh,
        in_specs=(
            P("col", "row", None),
            P("col", "row"),
            P("col", "row", None),
            P("row", "col"),
            P(("row", "col")),
            P("col", "row"),
            P(("row", "col")),
            P("row", "col"),
            P(("row", "col")),
            P("col", "row"),
            P(("row", "col")),
            P(("row", "col")),
            P(("row", "col")),
            P(("row", "col")),
            P(("row", "col")),
        ),
        out_specs=(
            P("col", "row", None),
            P("col", "row", None),
            P("row", "col"),
            P(("row", "col")),
            P("col", "row"),
            P(("row", "col")),
            P("row", "col"),
            P(("row", "col")),
            P("col", "row"),
            P(("row", "col")),
            P(("row", "col")),
            P(("row", "col")),
            P(("row", "col")),
            P(("row", "col")),
        ),
        check_vma=False,
    )
```

```python
import functools
import math

import jax
import jax.numpy as jnp
import numpy as np
from jax import lax
from jax.experimental import pallas as pl
from jax.experimental.pallas import tpu as pltpu
from jax.sharding import PartitionSpec as P

HD = 64
ROT = 16
EPS = 1e-05
MASKED = -1e30
BF = jnp.bfloat16
F32 = jnp.float32


def normalize(rows_in):
    average = jnp.mean(rows_in, axis=-1, keepdims=True)
    centred = rows_in - average
    spread = jnp.mean(centred * centred, axis=-1, keepdims=True)
    root = lax.rsqrt(spread + EPS)
    return centred * root, root


def dot(a, b, dims=((1,), (0,))):
    return lax.dot_general(a, b, (dims, ((), ())), preferred_element_type=F32)


def pack_att(project, mix):
    return jnp.concatenate([project.T, mix], axis=0)


def pack_mlp(up, down):
    return jnp.concatenate([up[:, :128], up[:, 128:], down], axis=0)


def unpack_up(p):
    return jnp.concatenate([p[:128], p[128:256]], axis=1)


def rotary_tables(positions):
    lane = np.arange(2 * HD) % HD
    frequency = np.where(lane < ROT, 10000.0 ** (-(lane % (ROT // 2)) * 2.0 / ROT), 0.0)
    angles = positions[:, None].astype(F32) * jnp.asarray(frequency, F32)[None, :]
    return jnp.cos(angles), jnp.sin(angles)


VMEM_LIMIT = 14 << 20


def roll(value, shift):
    return pltpu.roll(value, shift, 1)


def lanes_of(shape):
    return lax.broadcasted_iota(jnp.int32, shape, 1)


VMEM = pl.BlockSpec(memory_space=pltpu.VMEM)
SMEM = pl.BlockSpec(memory_space=pltpu.SMEM)
SHAPE = jax.ShapeDtypeStruct
LINES = 8


ANY = pl.BlockSpec(memory_space=pl.ANY)
HBM = pl.BlockSpec(memory_space=pltpu.HBM)


def call_streamed(kernel, name, work, operands, results):
    def body(*refs):
        count = len(operands)
        sources, outs, held, sems = refs[:count], refs[count:-count - 1], refs[-count - 1 : -1], refs[-1]
        wait_all(start_all(list(zip(sources, held)), sems))
        kernel(*held, *outs)

    return pl.pallas_call(
        body,
        out_shape=results,
        in_specs=[HBM] * len(operands),
        out_specs=[VMEM] * len(results),
        scratch_shapes=[pltpu.VMEM(v.shape, v.dtype) for v in operands]
        + [pltpu.SemaphoreType.DMA((len(operands),))],
        compiler_params=pltpu.CompilerParams(vmem_limit_bytes=12 << 20),
        cost_estimate=pl.CostEstimate(flops=work, bytes_accessed=work // 400, transcendentals=0),
        name=name,
    )(*operands)


def call(kernel, name, work, operands, results, scratch, far=(), copies=0, held=(), limit=VMEM_LIMIT):
    places = [HBM if any(v is w for w in far) else VMEM for v in operands[1:]]
    return pl.pallas_call(
        kernel,
        out_shape=results,
        in_specs=[SMEM] + places,
        out_specs=[VMEM] * len(results),
        scratch_shapes=[pltpu.VMEM(size, dtype) for size, dtype in scratch]
        + [pltpu.SemaphoreType.DMA((copies,))] * (copies > 0)
        + [v for size, dtype in held for v in (pltpu.VMEM(size, dtype), pltpu.SemaphoreType.DMA(size[:1]))],
        compiler_params=pltpu.CompilerParams(vmem_limit_bytes=limit),
        cost_estimate=pl.CostEstimate(flops=work, bytes_accessed=work // 400, transcendentals=0),
        name=name,
    )(*operands)


def start_all(moves, sems):
    copies = [
        pltpu.make_async_copy(source, target, sems.at[i]) for i, (source, target) in enumerate(moves)
    ]
    for copy in copies:
        copy.start()
    return copies


def wait_all(copies):
    for copy in copies:
        copy.wait()


def prepare_kernel(paired, *refs):
    sources, (small_ref, act_ref, *packs) = refs[:15], refs[15 : 17 + paired]
    *held, line, sems = refs[17 + paired :]
    moves = list(zip(sources[2:], held[2:]))
    moves += [(sources[0], act_ref.at[0]), (sources[1], act_ref.at[1])]
    copies = start_all(moves, sems)
    line[...] = jnp.zeros(line.shape, F32)
    wait_all(copies)
    unused, unused, seg_ref, project_ref, mix_ref, up_ref, down_ref, *vectors = held
    if paired:
        pack = packs[0]
        pack[0:192, :] = project_ref[...]
        pack[192:256, :] = mix_ref[...]
        pack[256:384, :] = up_ref[:, 0:128]
        pack[384:512, :] = up_ref[:, 128:256]
        pack[512:768, :] = down_ref[...]
    part = vectors[0].shape[1]
    for i in range(6):
        line[0:1, i * part : (i + 1) * part] = vectors[i][...].astype(F32)
    line[1:2, 0 : vectors[6].shape[1]] = vectors[6][...].astype(F32)
    line[2:3, 0 : vectors[7].shape[1]] = vectors[7][...].astype(F32)
    seg = seg_ref[...]
    blocks = seg.shape[1] // 128
    for i in range(blocks):
        piece = seg[:, i * 128 : (i + 1) * 128]
        line[3 + i : 4 + i, :] = (piece >> 5).astype(F32)
        line[3 + blocks + i : 4 + blocks + i, :] = (piece & 31).astype(F32)
    full = line[...].astype(BF)
    for i in range(small_ref.shape[0]):
        small_ref[i] = full


def run_local(kernel, name, work, sources, results, scratch):
    return pl.pallas_call(
        kernel,
        out_shape=results,
        in_specs=[HBM] * len(sources),
        out_specs=[VMEM] * len(results),
        scratch_shapes=[pltpu.VMEM(v.shape, v.dtype) for v in sources]
        + scratch
        + [pltpu.SemaphoreType.DMA((len(sources),))],
        compiler_params=pltpu.CompilerParams(vmem_limit_bytes=60 << 20),
        cost_estimate=pl.CostEstimate(flops=work, bytes_accessed=1 << 20, transcendentals=0),
        name=name,
    )(*sources)


def layout_kernel(rows, cols, sizes, where_ref, every_ref, norms_ref, project_ref, up_ref, starts_ref):
    c, y, group = where_ref[2], where_ref[3], where_ref[4]
    part, project, up = sizes
    copies = every_ref.shape[0]

    def spread_out(block, lane_of, row_of, wide):
        lane = lax.broadcasted_iota(jnp.int32, (128, wide), 0)
        place = lax.broadcasted_iota(jnp.int32, (128, wide), 1)
        picked = dot(block, jnp.where(lane == lane_of(place), 1.0, 0.0).astype(BF))
        device = lax.broadcasted_iota(jnp.int32, (copies, wide), 0)
        place = lax.broadcasted_iota(jnp.int32, (copies, wide), 1)
        return jnp.sum(jnp.where(device == row_of(place), picked, 0.0), axis=0, keepdims=True)

    def line(i):
        return every_ref[:, i, :]

    wide = norms_ref.shape[1]
    rows_of = [line(i) for i in range(LINES)]
    for i in range(6):
        norms_ref[i : i + 1, :] = spread_out(
            rows_of[0], lambda n: i * part + n % part, lambda n: n // part, wide
        )
    norms_ref[6:8, :] = jnp.zeros((2, wide), F32)
    half = cols // 2
    for h in range(2):
        begin = group * cols + (h ^ y) * half
        project_ref[h : h + 1, :] = spread_out(
            rows_of[1],
            lambda n: n % project,
            lambda n: jnp.where(n < half * project, begin + n // project, -1),
            256,
        )
        up_ref[:, h * 256 : h * 256 + 256] = spread_out(
            rows_of[2], lambda n: n % up, lambda n: begin + n // up, 256
        )
    device = lax.broadcasted_iota(jnp.int32, (copies, 128), 0)
    eye = lax.broadcasted_iota(jnp.int32, (128, 128), 0) == lanes_of((128, 128))
    count = starts_ref.shape[0] // rows
    blocks = count // 128
    for g in range(rows):
        here = device == g * cols + c
        for b in range(blocks):
            coarse, fine = rows_of[3 + b].astype(F32), rows_of[3 + blocks + b].astype(F32)
            value = jnp.sum(jnp.where(here, coarse * 32.0 + fine, 0.0), axis=0, keepdims=True)
            column = jnp.sum(jnp.where(eye, value, 0.0), axis=1, keepdims=True)
            begin = g * count + b * 128
            starts_ref[begin : begin + 128, :] = column.astype(jnp.int32)


def mlp_kernel(
    where_ref,
    n2_ref,
    xhat_ref,
    cot_ref,
    own0_ref,
    own1_ref,
    own2_ref,
    own3_ref,
    oth_ref,
    norms_ref,
    shift_ref,
    out_ref,
    e_ref,
    send_ref,
    keep_ref,
    small_ref,
    up_s,
    down_s,
    act_s,
    dh_s,
    ug_s,
    dg_s,
    sems,
):
    r, key = where_ref[0], where_ref[1]
    count = n2_ref.shape[0] // 4
    gain = norms_ref[2:3, :]
    owns, others = (own0_ref, own1_ref, own2_ref, own3_ref), [oth_ref.at[k] for k in range(4)]
    moves = []
    for k in range(4):
        g = pl.multiple_of((key ^ k) * 128, 128)
        for h, ref in enumerate((owns[k], others[k])):
            b = ref.shape[0] - 512
            left, right = pl.ds(h * 256, 128), pl.ds(h * 256 + 128, 128)
            moves += [
                (ref.at[pl.ds(b, 128)], up_s.at[pl.ds(g, 128), left]),
                (ref.at[pl.ds(b + 128, 128)], up_s.at[pl.ds(g, 128), right]),
                (ref.at[pl.ds(b + 256, 256)], down_s.at[pl.ds(h * 256, 256), pl.ds(g, 128)]),
            ]
    wait_all(start_all(moves, sems))
    up, down = up_s[...], down_s[...]
    shift = shift_ref[...]
    shift_sum = jnp.zeros((1, up.shape[1]), F32)
    for t in range(4):
        at = slice(t * count, t * count + count)
        hidden = dot(n2_ref[at, :], up) + shift
        cdf = 0.5 + 0.5 * lax.erf(hidden * math.sqrt(0.5))
        active = (hidden * cdf).astype(BF)
        slope = cdf + hidden * jnp.exp(-0.5 * hidden * hidden) * (1.0 / math.sqrt(2 * math.pi))
        act_s[at, :] = active
        out_ref[at, :] = dot(active, down).astype(BF)
        d_hidden = (dot(cot_ref[at, :], down, ((1,), (1,))) * slope).astype(BF)
        dh_s[at, :] = d_hidden
        e_ref[at, :] = (dot(d_hidden, up, ((1,), (1,))) * gain).astype(BF)
        shift_sum += jnp.sum(d_hidden.astype(F32), axis=0, keepdims=True)
    mine = cot_ref[pl.ds(pl.multiple_of(r * count, count), count), :]
    product = dot(dh_s[...], xhat_ref[...], ((0,), (0,)))
    weights = jnp.transpose(up.astype(F32))
    across = jnp.transpose(jnp.broadcast_to(shift_sum, (8, up.shape[1])))[:, 0:1]
    small_ref[...] = jnp.zeros(small_ref.shape, F32)
    small_ref[0:1, :] = shift_sum
    small_ref[1:2, :] = jnp.sum(weights * product, axis=0, keepdims=True)
    small_ref[2:3, :] = jnp.sum(weights * across, axis=0, keepdims=True)
    small_ref[3:4, :] = jnp.sum(mine.astype(F32), axis=0, keepdims=True)
    ug_s[...] = jnp.transpose(product * gain + across * norms_ref[3:4, :])
    dg_s[...] = dot(act_s[...], cot_ref[...], ((0,), (0,)))
    for k in range(4):
        g = pl.multiple_of((key ^ k) * 128, 128)
        for h, ref in enumerate((keep_ref, send_ref)):
            ref[k, 0:128] = ug_s[pl.ds(g, 128), h * 256 : h * 256 + 128].astype(ref.dtype)
            ref[k, 128:256] = ug_s[pl.ds(g, 128), h * 256 + 128 : h * 256 + 256].astype(ref.dtype)
            ref[k, 256:512] = dg_s[h * 256 : h * 256 + 256, pl.ds(g, 128)].astype(ref.dtype)


def run_mlp(where, n2, xhat, cot, own, oth, norms, shift):
    tall, width = n2.shape
    wide = shift.shape[1]
    return call(
        mlp_kernel,
        "feed_forward",
        1 << 35,
        (where, n2, xhat, cot, *own, *oth, norms, shift),
        (
            SHAPE((tall, width), BF),
            SHAPE((tall, width), BF),
            SHAPE((4, 512, 128), BF),
            SHAPE((4, 512, 128), F32),
            SHAPE((8, wide), F32),
        ),
        (
            ((width, wide), BF),
            ((wide, width), BF),
            ((tall, wide), BF),
            ((tall, wide), BF),
            ((width, wide), F32),
            ((wide, width), F32),
        ),
        (*own, *oth),
        24,
    )


def head(key, n1_ref, xhat_ref, cot_ref, norms_ref, shift, cos_ref, sin_ref, starts_ref, w, mix, ctx, dp, grads_ref, scratch):
    q_s, qh_s, k_s, v_s, dctx_s, dq_s, dt_s, pg_s, mg_s, unused = scratch
    tall = n1_ref.shape[0]
    count = tall // 4
    scaling = HD**-0.5
    lane = lanes_of((count, 128))
    left = lane < 64
    first, second = lane % 64 < ROT // 2, lane % 64 < ROT

    def turn(qk, at, sign):
        sine = sin_ref[at, :] * sign
        minus = jnp.where(first, -sine, 0.0)
        plus = jnp.where(first, 0.0, jnp.where(second, sine, 0.0))
        return qk * cos_ref[at, :] + roll(qk, 120) * minus + roll(qk, 8) * plus

    for t in range(4):
        at = slice(t * count, t * count + count)
        projected = dot(n1_ref[at, :], w[...], ((1,), (1,))) + shift
        qk = turn(projected[:, :128], at, 1.0)
        turned = roll(qk, 64)
        q_s[at, :] = jnp.where(left, qk, 0.0).astype(BF)
        k_s[at, :] = jnp.where(left, turned, 0.0).astype(BF)
        qh_s[at, :] = jnp.where(left, 0.0, turned).astype(BF)
        v_s[at, :] = projected[:, 128:].astype(BF)
        dctx_s[at, :] = dot(cot_ref[at, :], mix[...], ((1,), (1,))).astype(BF)
    dt_s[...] = jnp.zeros(dt_s.shape, F32)
    for t in range(4):
        at = slice(t * count, t * count + count)
        keys = (t + 1) * count
        q, d_context = q_s[at, :], dctx_s[at, :]
        kk, vv = k_s[0:keys, :], v_s[0:keys, :]
        scores = dot(q, kk, ((1,), (1,))) * scaling
        place = lax.broadcasted_iota(jnp.int32, (count, keys), 1)
        row = lax.broadcasted_iota(jnp.int32, (count, 1), 0) + t * count
        allowed = (place >= starts_ref[at, :]) & (place <= row)
        scores = jnp.where(allowed, scores, MASKED)
        exponent = jnp.exp(scores - jnp.max(scores, axis=-1, keepdims=True))
        probability = exponent * (1.0 / jnp.sum(exponent, axis=-1, keepdims=True))
        prob_low = probability.astype(BF)
        ctx[at, :] = dot(prob_low, vv).astype(BF)
        d_prob = dot(d_context, vv, ((1,), (1,)))
        weight = jnp.sum(d_prob * probability, axis=-1, keepdims=True)
        d_scores = (probability * (d_prob - weight)).astype(BF)
        dq_s[at, :] = dot(d_scores, kk)
        dt_s[0:128, 0:keys] += dot(qh_s[at, :], d_scores, ((0,), (0,)))
        dt_s[128:256, 0:keys] += dot(d_context, prob_low, ((0,), (0,)))
    shift_sum = jnp.zeros((1, 256), F32)
    for t in range(4):
        at = slice(t * count, t * count + count)
        turned = jnp.transpose(dt_s[:, at])
        qk = turn((dq_s[at, :] + turned[:, :128]) * scaling, at, -1.0)
        dp[at, 0:128] = qk.astype(BF)
        dp[at, 128:256] = turned[:, 128:].astype(BF)
        shift_sum += jnp.sum(dp[at, :].astype(F32), axis=0, keepdims=True)
    product = dot(dp[...], xhat_ref[...], ((0,), (0,)))
    weights = w[...].astype(F32)
    across = jnp.transpose(jnp.broadcast_to(shift_sum, (8, 256)))[:, 0:1]
    gain_sum = jnp.sum(weights * product, axis=0, keepdims=True)
    bias_sum = jnp.sum(weights * across, axis=0, keepdims=True)
    pg_s[...] = product * norms_ref[0:1, :] + across * norms_ref[1:2, :]
    mg_s[...] = dot(ctx[...], cot_ref[...], ((0,), (0,)))
    for k in range(4):
        g = pl.multiple_of((key ^ k) * 128, 128)
        grads_ref[k, 0:192] = pg_s[0:192, pl.ds(g, 128)].astype(grads_ref.dtype)
        grads_ref[k, 192:256] = mg_s[0:64, pl.ds(g, 128)].astype(grads_ref.dtype)
    return shift_sum, gain_sum, bias_sum


def fetch_head(key, slots, w, mix, sems):
    moves = []
    for k in range(4):
        g = pl.multiple_of((key ^ k) * 128, 128)
        moves += [
            (slots[k].at[pl.ds(0, 192)], w.at[pl.ds(0, 192), pl.ds(g, 128)]),
            (slots[k].at[pl.ds(192, 64)], mix.at[pl.ds(0, 64), pl.ds(g, 128)]),
        ]
    copies = start_all(moves, sems)
    w[192:256, :] = jnp.zeros((64, w.shape[1]), BF)
    mix[64:128, :] = jnp.zeros((64, mix.shape[1]), BF)
    return copies


def head_scratch(tall, width):
    return (
        ((tall, 128), BF),
        ((tall, 128), BF),
        ((tall, 128), BF),
        ((tall, 128), BF),
        ((tall, 128), BF),
        ((tall, 128), F32),
        ((256, tall), F32),
        ((256, width), F32),
        ((128, width), F32),
    )


def first_kernel(
    where_ref,
    act0_ref,
    act1_ref,
    act2_ref,
    act3_ref,
    slot0_ref,
    slot1_ref,
    slot2_ref,
    slot3_ref,
    shift_ref,
    cos_ref,
    sin_ref,
    starts_ref,
    norms_ref,
    n1_ref,
    n2_ref,
    xhat_ref,
    cot_ref,
    w_ref,
    mix_ref,
    ctx_ref,
    dp_ref,
    grads_ref,
    small_ref,
    *scratch,
):
    r, key = where_ref[0], where_ref[1]
    *scratch, act_s, act_sems = scratch
    count = act0_ref.shape[1]
    norms = norms_ref[...]
    moves = [(act0_ref, act_s.at[0]), (act1_ref, act_s.at[1])]
    moves += [(act2_ref, act_s.at[2]), (act3_ref, act_s.at[3])]
    fetched = start_all(moves, act_sems)
    copies = fetch_head(key, (slot0_ref, slot1_ref, slot2_ref, slot3_ref), w_ref, mix_ref, scratch[-1])
    for j in range(4):
        fetched[j].wait()
        source = act_s.at[j]
        at = pl.ds(pl.multiple_of((r ^ j) * count, count), count)
        hat, unused = normalize(source[0].astype(F32))
        xhat_ref[at, :] = hat.astype(BF)
        n1_ref[at, :] = (hat * norms[0:1] + norms[1:2]).astype(BF)
        n2_ref[at, :] = (hat * norms[2:3] + norms[3:4]).astype(BF)
        cot_ref[at, :] = source[1]
    wait_all(copies)
    small_ref[...] = jnp.zeros(small_ref.shape, F32)
    small_ref[0:1, 0:256], small_ref[1:2, :], small_ref[2:3, :] = head(
        key,
        n1_ref,
        xhat_ref,
        cot_ref,
        norms_ref,
        shift_ref[0:1, :],
        cos_ref,
        sin_ref,
        starts_ref,
        w_ref,
        mix_ref,
        ctx_ref,
        dp_ref,
        grads_ref,
        scratch,
    )


def run_first(where, chunks, slots, shift, cosine, sine, starts, norms):
    count, width = chunks[0].shape[1:]
    tall = 4 * count
    return call(
        first_kernel,
        "attention_first",
        1 << 35,
        (where, *chunks, *slots, shift, cosine, sine, starts, norms),
        (
            SHAPE((tall, width), BF),
            SHAPE((tall, width), BF),
            SHAPE((tall, width), BF),
            SHAPE((tall, width), BF),
            SHAPE((256, width), BF),
            SHAPE((128, width), BF),
            SHAPE((tall, 128), BF),
            SHAPE((tall, 256), BF),
            SHAPE((4, 256, 128), F32),
            SHAPE((8, width), F32),
        ),
        head_scratch(tall, width),
        (*slots, *chunks),
        8,
        (((4, 2, count, width), BF),),
        14 << 20,
    )


def second_kernel(
    where_ref,
    n1_ref,
    xhat_ref,
    cot_ref,
    slots_ref,
    shift_ref,
    cos_ref,
    sin_ref,
    starts_ref,
    norms_ref,
    w_ref,
    mix_ref,
    ctx_ref,
    dp_ref,
    grads_ref,
    small_ref,
    *scratch,
):
    wait_all(fetch_head(where_ref[1], [slots_ref.at[k] for k in range(4)], w_ref, mix_ref, scratch[-1]))
    small_ref[...] = jnp.zeros(small_ref.shape, F32)
    small_ref[0:1, 0:256], small_ref[1:2, :], small_ref[2:3, :] = head(
        where_ref[1],
        n1_ref,
        xhat_ref,
        cot_ref,
        norms_ref,
        shift_ref[1:2, :],
        cos_ref,
        sin_ref,
        starts_ref,
        w_ref,
        mix_ref,
        ctx_ref,
        dp_ref,
        grads_ref,
        scratch,
    )


def run_second(where, n1, xhat, cot, slots, shift, cosine, sine, starts, norms):
    tall, width = n1.shape
    return call(
        second_kernel,
        "attention_second",
        1 << 35,
        (where, n1, xhat, cot, *slots, shift, cosine, sine, starts, norms),
        (
            SHAPE((256, width), BF),
            SHAPE((128, width), BF),
            SHAPE((tall, 128), BF),
            SHAPE((tall, 256), BF),
            SHAPE((4, 256, 128), BF),
            SHAPE((8, width), F32),
        ),
        head_scratch(tall, width),
        slots,
        8,
    )


def join_kernel(
    where_ref,
    norms_ref,
    w_a,
    mix_a,
    ctx_a,
    dp_a,
    w_b,
    mix_b,
    ctx_b,
    dp_b,
    out_in,
    e_in,
    near_ref,
    rest_ref,
):
    r = where_ref[0]
    count = ctx_a.shape[0] // 4
    gain = norms_ref[0:1, :]
    for j in range(4):
        at = pl.ds(pl.multiple_of((r ^ j) * count, count), count)
        d_first = dot(dp_a[at, :], w_a[...]) + dot(dp_b[at, :], w_b[...])
        out = dot(ctx_a[at, :], mix_a[...]) + dot(ctx_b[at, :], mix_b[...])
        target = near_ref if j % 2 else rest_ref
        target[j // 2, 0] = (out_in[at, :].astype(F32) + out).astype(target.dtype)
        target[j // 2, 1] = (e_in[at, :].astype(F32) + d_first * gain).astype(target.dtype)


def run_join(where, norms, first, second, out, e):
    tall, width = out.shape
    count = tall // 4
    return call(
        join_kernel,
        "join",
        1 << 24,
        (where, norms, *first, *second, out, e),
        (
            SHAPE((2, 2, count, width), BF),
            SHAPE((2, 2, count, width), F32),
        ),
        (),
    )


def add_kernel(rest_ref, come_ref, mine_ref, onward_ref):
    for i in range(2):
        mine_ref[i] = rest_ref[0, i] + come_ref[0, i].astype(F32)
        onward_ref[i] = (rest_ref[1, i] + come_ref[1, i].astype(F32)).astype(BF)


def finish_kernel(x_ref, cot_ref, mine_ref, come_ref, norms_ref, output_ref, grad_ref):
    x = x_ref[...].astype(F32)
    out = mine_ref[0] + come_ref[0].astype(F32)
    output_ref[...] = (x + out + norms_ref[4:5, :] + norms_ref[5:6, :]).astype(BF)
    e = mine_ref[1] + come_ref[1].astype(F32)
    xhat, root = normalize(x)
    centred = e - jnp.mean(e, axis=-1, keepdims=True)
    along = xhat * jnp.mean(e * xhat, axis=-1, keepdims=True)
    grad_ref[...] = cot_ref[...].astype(F32) + root * (centred - along)


def share_kernel(cols, sizes, where_ref, mlp_ref, own_ref, oth_ref, out_ref):
    y, group = where_ref[3], where_ref[4]
    part, project, up = sizes
    copies = out_ref.shape[0]

    def cut(row, device_of, lane_of):
        wide = row.shape[1]
        place = lax.broadcasted_iota(jnp.int32, (copies, wide), 1)
        device = lax.broadcasted_iota(jnp.int32, (copies, wide), 0)
        kept = jnp.where(device == device_of(place), row, 0.0)
        place = lax.broadcasted_iota(jnp.int32, (wide, 128), 0)
        lane = lax.broadcasted_iota(jnp.int32, (wide, 128), 1)
        chosen = jnp.where(lane == lane_of(place), 1.0, 0.0)
        return jnp.dot(kept, chosen, precision=lax.Precision.HIGHEST, preferred_element_type=F32)

    rows = [own_ref[i : i + 1, :] + oth_ref[i : i + 1, :] for i in (1, 2)]
    rows += [mlp_ref[i : i + 1, :] for i in (1, 2, 3)]
    total = jnp.zeros((copies, 128), F32)
    for i, row in enumerate(rows):
        total += cut(row, lambda n: n // part, lambda n: i * part + n % part)
    out_ref[...] = jnp.zeros(out_ref.shape, F32)
    out_ref[:, 0, :] = total
    half = cols // 2
    heads, hidden = jnp.zeros((copies, 128), F32), jnp.zeros((copies, 128), F32)
    for h, ref in enumerate((own_ref, oth_ref)):
        begin = group * cols + (h ^ y) * half
        heads += cut(
            ref[0:1, 0:256],
            lambda n: jnp.where(n < half * project, begin + n // project, -1),
            lambda n: n % project,
        )
        hidden += cut(
            mlp_ref[0:1, h * 256 : h * 256 + 256], lambda n: begin + n // up, lambda n: n % up
        )
    out_ref[:, 1, :] = heads
    out_ref[:, 2, :] = hidden


def small_kernel(unused, sums_ref, *outs):
    total = jnp.sum(sums_ref[...], axis=0)
    part = outs[0].shape[1]
    for i in range(5):
        outs[i][...] = total[0:1, i * part : (i + 1) * part]
    outs[5][...] = total[1:2, 0 : outs[5].shape[1]]
    outs[6][...] = total[2:3, 0 : outs[6].shape[1]]


def merge_kernel(att_keep, att_come, mlp_keep, mlp_come, *outs):
    for k in range(4):
        outs[k][0:256, :] = (att_keep[k] + att_come[k].astype(F32)).astype(BF)
        outs[k][256:768, :] = (mlp_keep[k] + mlp_come[k].astype(F32)).astype(BF)


def collect_kernel(a_ref, b_ref, c_ref, d_ref, project_ref, mix_ref, up_ref, down_ref):
    def total(begin, end):
        refs = (a_ref, b_ref, c_ref, d_ref)
        return sum(ref[begin:end, :].astype(F32) for ref in refs)

    project_ref[...] = total(0, 192)
    mix_ref[...] = total(192, 256)
    up_ref[:, 0:128] = total(256, 384)
    up_ref[:, 128:256] = total(384, 512)
    down_ref[...] = total(512, 768)


def on_device(
    inputs,
    seg_start,
    cotangent,
    project_weight,
    project_bias,
    output_weight,
    output_bias,
    up_weight,
    up_bias,
    down_weight,
    down_bias,
    first_gain,
    first_bias,
    second_gain,
    second_bias,
):
    rows, cols = lax.axis_size("row"), lax.axis_size("col")
    per = cols // rows
    r, c = lax.axis_index("row"), lax.axis_index("col")
    both = ("row", "col")
    count, width = inputs.shape[1], inputs.shape[2]
    paired = per == 2

    def flip(value, bit):
        return lax.ppermute(value, "row", [(i, i ^ bit) for i in range(rows)])

    def group_of(i):
        return (i % 2) * 2 + i // 2

    def home(i, k):
        rr, cc = divmod(i, cols)
        z, y = divmod(cc, per)
        return group_of(z) * cols + (rr ^ k) * per + y

    everyone = range(rows * cols)

    def beside(value):
        return lax.ppermute(value, "col", [(i, i ^ 1) for i in range(cols)])

    def spread(block):
        return [lax.ppermute(block, both, [(i, home(i, k)) for i in everyone]) for k in range(rows)]

    def bring(blocks):
        return [
            lax.ppermute(b, both, [(home(i, k), i) for i in everyone]) for k, b in enumerate(blocks)
        ]

    def slot_of(i):
        rr, cc = divmod(i, cols)
        return group_of(cc // per) * cols + (cc % per) * rows + rr

    def fetch(block):
        moved = lax.ppermute(block, both, [(i, slot_of(i)) for i in everyone])
        whole = lax.all_gather(moved, "col", axis=0)
        return whole.reshape((per, rows) + block.shape)

    def fetch_columns(block):
        whole = fetch(block).transpose(1, 2, 0, 3).reshape(rows, block.shape[0], 2, -1)
        return whole.transpose(2, 0, 1, 3)

    def fetch_rows(block):
        whole = fetch(block).transpose(1, 0, 2, 3).reshape(rows, 2, -1, block.shape[1])
        return whole.transpose(1, 0, 2, 3)

    def deliver(blocks):
        flat = blocks.reshape((cols,) + blocks.shape[2:]).astype(BF)
        mine = lax.psum_scatter(flat, "col", scatter_dimension=0, tiled=False)
        return lax.ppermute(mine, both, [(slot_of(i), i) for i in everyone]).astype(F32)

    def deliver_columns(halves):
        deep = halves.shape[2]
        whole = halves.transpose(1, 2, 0, 3).reshape(rows, deep, per, -1)
        return deliver(whole.transpose(2, 0, 1, 3))

    def deliver_rows(halves):
        wide = halves.shape[3]
        whole = halves.transpose(1, 0, 2, 3).reshape(rows, per, -1, wide)
        return deliver(whole.transpose(1, 0, 2, 3))

    if paired:
        key, y = c // per, c % per
    else:
        key, y = jnp.int32(0), jnp.int32(0)
    group = group_of(r)
    where = jnp.stack([r, key, c, y, group]).astype(jnp.int32)
    part, project_len, up_len = first_gain.shape[0], project_bias.shape[0], up_bias.shape[0]
    copies = rows * cols
    x_own, cot_own = inputs[0], cotangent[0]
    vectors = (
        first_gain,
        first_bias,
        second_gain,
        second_bias,
        output_bias,
        down_bias,
        project_bias,
        up_bias,
    )
    results = [SHAPE((copies, LINES, 128), BF), SHAPE((2, count, width), BF)]
    small, act, *packs = run_local(
        functools.partial(prepare_kernel, paired),
        "prepare",
        1 << 20,
        (x_own, cot_own, seg_start, project_weight.T, output_weight, up_weight, down_weight)
        + tuple(v[None] for v in vectors),
        results + [SHAPE((768, 128), BF)] * paired,
        [pltpu.VMEM((LINES, 128), F32)],
    )
    across, far = flip(act, 2), flip(act, 1)
    every = lax.all_to_all(small, both, 0, 0, tiled=True)
    if paired:
        own = spread(packs[0])
        mlp_slots = own, (beside(jnp.stack([v[256:] for v in own])),)
        att_slots = own, (beside(jnp.stack([v[:256] for v in own])),)
        every, across = lax.optimization_barrier((every, across))
    else:
        ups, downs = fetch_columns(up_weight), fetch_rows(down_weight)
        projects, mixes = fetch_columns(project_weight), fetch_rows(output_weight)
        mlp_slots = [
            jnp.stack(
                [pack_mlp(ups[h, g], downs[h, g]) for g in range(rows)]
            )
            for h in range(2)
        ]
        att_slots = [
            jnp.stack(
                [pack_att(projects[h, g], mixes[h, g]) for g in range(rows)]
            )
            for h in range(2)
        ]

    chunks = (act, far, across, flip(across, 1))
    norms, project_shift, up_shift, starts = call(
        functools.partial(layout_kernel, rows, cols, (part, project_len, up_len)),
        "layout",
        1 << 35,
        (where, every),
        (
            SHAPE((8, width), F32),
            SHAPE((2, 256), F32),
            SHAPE((1, 512), F32),
            SHAPE((rows * count, 1), jnp.int32),
        ),
        (),
    )
    if paired:
        pass
    cosine, sine = rotary_tables(jnp.arange(rows * count, dtype=jnp.int32) - starts[:, 0])

    if not paired:
        att_slots = list(att_slots[0]), (att_slots[1],)
        mlp_slots = list(mlp_slots[0]), (mlp_slots[1],)
    n1, n2, xhat, cot_all, *first, att_keep, small_own = run_first(
        where, chunks, att_slots[0], project_shift, cosine, sine, starts, norms
    )
    out, e, mlp_send, mlp_keep, mlp_small = run_mlp(
        where, n2, xhat, cot_all, mlp_slots[0], mlp_slots[1], norms, up_shift
    )
    n1, out = lax.optimization_barrier((n1, out))
    *second, att_send, small_oth = run_second(
        where, n1, xhat, cot_all, att_slots[1], project_shift, cosine, sine, starts, norms
    )
    near, rest = run_join(where, norms, first, second, out, e)

    (small,) = call(
        functools.partial(share_kernel, cols, (part, project_len, up_len)),
        "share_small",
        1 << 24,
        (where, mlp_small, small_own, small_oth),
        (SHAPE((copies, LINES, 128), F32),),
        (),
    )
    if paired:
        near, small, mlp_come, att_come = lax.optimization_barrier(
            (near, small, beside(mlp_send), beside(att_send))
        )

    if paired:
        blocks = call_streamed(
            merge_kernel,
            "merge",
            1 << 26,
            (att_keep, att_come, mlp_keep, mlp_come),
            (SHAPE((768, 128), BF),) * 4,
        )
        blocks = bring(blocks)
    shares = lax.all_to_all(small, both, 0, 0, tiled=True)

    mine, onward = call_streamed(
        add_kernel,
        "add_near",
        1 << 24,
        (rest, flip(near, 1)),
        (SHAPE((2, count, width), F32), SHAPE((2, count, width), BF)),
    )
    onward = flip(onward, 2)
    if paired:
        project_done, mix_done, up_done, down_done = call_streamed(
            collect_kernel,
            "collect",
            1 << 35,
            tuple(blocks),
            (
                SHAPE(project_weight.shape[::-1], F32),
                SHAPE(output_weight.shape, F32),
                SHAPE(up_weight.shape, F32),
                SHAPE(down_weight.shape, F32),
            ),
        )
        project_done, onward, shares = lax.optimization_barrier((project_done, onward, shares))
        project_done = project_done.T
    output, input_grad = call_streamed(
        finish_kernel,
        "finish",
        1 << 24,
        (x_own, cot_own, mine, onward, norms),
        (SHAPE((count, width), BF), SHAPE((count, width), F32)),
    )

    if paired:
        pass
    else:
        att_grads, mlp_grads = jnp.stack([att_keep, att_send.astype(F32)]), jnp.stack([mlp_keep, mlp_send.astype(F32)])
        every_pair = [(h, g) for h in range(2) for g in range(rows)]

        def regroup(parts):
            return jnp.stack(parts).reshape((2, rows) + parts[0].shape)

        project_done = deliver_columns(
            regroup([att_grads[h, g][:192].T for h, g in every_pair])
        )
        mix_done = deliver_rows(regroup([att_grads[h, g][192:] for h, g in every_pair]))
        up_done = deliver_columns(
            regroup([unpack_up(mlp_grads[h, g][:256]) for h, g in every_pair])
        )
        down_done = deliver_rows(regroup([mlp_grads[h, g][256:] for h, g in every_pair]))

    *pieces, project_shift_grad, up_shift_grad = [
        v[0]
        for v in call(
            small_kernel,
            "small_sums",
            1 << 24,
            (where, shares),
            (SHAPE((1, part), F32),) * 5
            + (SHAPE((1, project_len), F32), SHAPE((1, up_len), F32)),
            (),
        )
    ]
    return (
        output[None],
        input_grad[None],
        project_done,
        project_shift_grad,
        mix_done,
        pieces[4],
        up_done,
        up_shift_grad,
        down_done,
        pieces[4],
        pieces[0],
        pieces[1],
        pieces[2],
        pieces[3],
    )


def solution(mesh):
    return jax.shard_map(
        on_device,
        mesh=mesh,
        in_specs=(
            P("col", "row", None),
            P("col", "row"),
            P("col", "row", None),
            P("row", "col"),
            P(("row", "col")),
            P("col", "row"),
            P(("row", "col")),
            P("row", "col"),
            P(("row", "col")),
            P("col", "row"),
            P(("row", "col")),
            P(("row", "col")),
            P(("row", "col")),
            P(("row", "col")),
            P(("row", "col")),
        ),
        out_specs=(
            P("col", "row", None),
            P("col", "row", None),
            P("row", "col"),
            P(("row", "col")),
            P("col", "row"),
            P(("row", "col")),
            P("row", "col"),
            P(("row", "col")),
            P("col", "row"),
            P(("row", "col")),
            P(("row", "col")),
            P(("row", "col")),
            P(("row", "col")),
            P(("row", "col")),
        ),
        check_vma=False,
    )
```

```python
import functools
import math

import jax
import jax.numpy as jnp
import numpy as np
from jax import lax
from jax.experimental import pallas as pl
from jax.experimental.pallas import tpu as pltpu
from jax.sharding import PartitionSpec as P

HD = 64
ROT = 16
EPS = 1e-05
MASKED = -1e30
BF = jnp.bfloat16
F32 = jnp.float32


def normalize(rows_in):
    average = jnp.mean(rows_in, axis=-1, keepdims=True)
    centred = rows_in - average
    spread = jnp.mean(centred * centred, axis=-1, keepdims=True)
    root = lax.rsqrt(spread + EPS)
    return centred * root, root


def dot(a, b, dims=((1,), (0,))):
    return lax.dot_general(a, b, (dims, ((), ())), preferred_element_type=F32)


def pack_att(project, mix):
    return jnp.concatenate([project.T, mix], axis=0)


def pack_mlp(up, down):
    return jnp.concatenate([up[:, :128], up[:, 128:], down], axis=0)


def unpack_up(p):
    return jnp.concatenate([p[:128], p[128:256]], axis=1)


def rotary_tables(positions):
    lane = np.arange(2 * HD) % HD
    frequency = np.where(lane < ROT, 10000.0 ** (-(lane % (ROT // 2)) * 2.0 / ROT), 0.0)
    angles = positions[:, None].astype(F32) * jnp.asarray(frequency, F32)[None, :]
    return jnp.cos(angles), jnp.sin(angles)


VMEM_LIMIT = 14 << 20


def roll(value, shift):
    return pltpu.roll(value, shift, 1)


def lanes_of(shape):
    return lax.broadcasted_iota(jnp.int32, shape, 1)


VMEM = pl.BlockSpec(memory_space=pltpu.VMEM)
SMEM = pl.BlockSpec(memory_space=pltpu.SMEM)
SHAPE = jax.ShapeDtypeStruct
LINES = 8


ANY = pl.BlockSpec(memory_space=pl.ANY)
HBM = pl.BlockSpec(memory_space=pltpu.HBM)


def call_streamed(kernel, name, work, operands, results):
    def body(*refs):
        count = len(operands)
        sources, outs, held, sems = refs[:count], refs[count:-count - 1], refs[-count - 1 : -1], refs[-1]
        wait_all(start_all(list(zip(sources, held)), sems))
        kernel(*held, *outs)

    return pl.pallas_call(
        body,
        out_shape=results,
        in_specs=[HBM] * len(operands),
        out_specs=[VMEM] * len(results),
        scratch_shapes=[pltpu.VMEM(v.shape, v.dtype) for v in operands]
        + [pltpu.SemaphoreType.DMA((len(operands),))],
        compiler_params=pltpu.CompilerParams(vmem_limit_bytes=12 << 20),
        cost_estimate=pl.CostEstimate(flops=work, bytes_accessed=work // 400, transcendentals=0),
        name=name,
    )(*operands)


def call(kernel, name, work, operands, results, scratch, far=(), copies=0, held=(), limit=VMEM_LIMIT):
    places = [HBM if any(v is w for w in far) else VMEM for v in operands[1:]]
    return pl.pallas_call(
        kernel,
        out_shape=results,
        in_specs=[SMEM] + places,
        out_specs=[VMEM] * len(results),
        scratch_shapes=[pltpu.VMEM(size, dtype) for size, dtype in scratch]
        + [pltpu.SemaphoreType.DMA((copies,))] * (copies > 0)
        + [v for size, dtype in held for v in (pltpu.VMEM(size, dtype), pltpu.SemaphoreType.DMA(size[:1]))],
        compiler_params=pltpu.CompilerParams(vmem_limit_bytes=limit),
        cost_estimate=pl.CostEstimate(flops=work, bytes_accessed=work // 400, transcendentals=0),
        name=name,
    )(*operands)


def start_all(moves, sems):
    copies = [
        pltpu.make_async_copy(source, target, sems.at[i]) for i, (source, target) in enumerate(moves)
    ]
    for copy in copies:
        copy.start()
    return copies


def wait_all(copies):
    for copy in copies:
        copy.wait()


def prepare_kernel(paired, *refs):
    sources, (small_ref, act_ref, *packs) = refs[:15], refs[15 : 17 + paired]
    *held, line, sems = refs[17 + paired :]
    moves = list(zip(sources[2:], held[2:]))
    moves += [(sources[0], act_ref.at[0]), (sources[1], act_ref.at[1])]
    copies = start_all(moves, sems)
    line[...] = jnp.zeros(line.shape, F32)
    wait_all(copies)
    unused, unused, seg_ref, project_ref, mix_ref, up_ref, down_ref, *vectors = held
    if paired:
        pack = packs[0]
        pack[0:192, :] = project_ref[...]
        pack[192:256, :] = mix_ref[...]
        pack[256:384, :] = up_ref[:, 0:128]
        pack[384:512, :] = up_ref[:, 128:256]
        pack[512:768, :] = down_ref[...]
    part = vectors[0].shape[1]
    for i in range(6):
        line[0:1, i * part : (i + 1) * part] = vectors[i][...].astype(F32)
    line[1:2, 0 : vectors[6].shape[1]] = vectors[6][...].astype(F32)
    line[2:3, 0 : vectors[7].shape[1]] = vectors[7][...].astype(F32)
    seg = seg_ref[...]
    blocks = seg.shape[1] // 128
    for i in range(blocks):
        piece = seg[:, i * 128 : (i + 1) * 128]
        line[3 + i : 4 + i, :] = (piece >> 5).astype(F32)
        line[3 + blocks + i : 4 + blocks + i, :] = (piece & 31).astype(F32)
    full = line[...].astype(BF)
    for i in range(small_ref.shape[0]):
        small_ref[i] = full


def run_local(kernel, name, work, sources, results, scratch):
    return pl.pallas_call(
        kernel,
        out_shape=results,
        in_specs=[HBM] * len(sources),
        out_specs=[VMEM] * len(results),
        scratch_shapes=[pltpu.VMEM(v.shape, v.dtype) for v in sources]
        + scratch
        + [pltpu.SemaphoreType.DMA((len(sources),))],
        compiler_params=pltpu.CompilerParams(vmem_limit_bytes=60 << 20),
        cost_estimate=pl.CostEstimate(flops=work, bytes_accessed=1 << 20, transcendentals=0),
        name=name,
    )(*sources)


def layout_kernel(rows, cols, sizes, where_ref, every_ref, norms_ref, project_ref, up_ref, starts_ref):
    c, y, group = where_ref[2], where_ref[3], where_ref[4]
    part, project, up = sizes
    copies = every_ref.shape[0]

    def spread_out(block, lane_of, row_of, wide):
        lane = lax.broadcasted_iota(jnp.int32, (128, wide), 0)
        place = lax.broadcasted_iota(jnp.int32, (128, wide), 1)
        picked = dot(block, jnp.where(lane == lane_of(place), 1.0, 0.0).astype(BF))
        device = lax.broadcasted_iota(jnp.int32, (copies, wide), 0)
        place = lax.broadcasted_iota(jnp.int32, (copies, wide), 1)
        return jnp.sum(jnp.where(device == row_of(place), picked, 0.0), axis=0, keepdims=True)

    def line(i):
        return every_ref[:, i, :]

    wide = norms_ref.shape[1]
    rows_of = [line(i) for i in range(LINES)]
    for i in range(6):
        norms_ref[i : i + 1, :] = spread_out(
            rows_of[0], lambda n: i * part + n % part, lambda n: n // part, wide
        )
    norms_ref[6:8, :] = jnp.zeros((2, wide), F32)
    half = cols // 2
    for h in range(2):
        begin = group * cols + (h ^ y) * half
        project_ref[h : h + 1, :] = spread_out(
            rows_of[1],
            lambda n: n % project,
            lambda n: jnp.where(n < half * project, begin + n // project, -1),
            256,
        )
        up_ref[:, h * 256 : h * 256 + 256] = spread_out(
            rows_of[2], lambda n: n % up, lambda n: begin + n // up, 256
        )
    device = lax.broadcasted_iota(jnp.int32, (copies, 128), 0)
    eye = lax.broadcasted_iota(jnp.int32, (128, 128), 0) == lanes_of((128, 128))
    count = starts_ref.shape[0] // rows
    blocks = count // 128
    for g in range(rows):
        here = device == g * cols + c
        for b in range(blocks):
            coarse, fine = rows_of[3 + b].astype(F32), rows_of[3 + blocks + b].astype(F32)
            value = jnp.sum(jnp.where(here, coarse * 32.0 + fine, 0.0), axis=0, keepdims=True)
            column = jnp.sum(jnp.where(eye, value, 0.0), axis=1, keepdims=True)
            begin = g * count + b * 128
            starts_ref[begin : begin + 128, :] = column.astype(jnp.int32)


def mlp_kernel(
    where_ref,
    n2_ref,
    xhat_ref,
    cot_ref,
    own0_ref,
    own1_ref,
    own2_ref,
    own3_ref,
    oth_ref,
    norms_ref,
    shift_ref,
    w_a,
    mix_a,
    ctx_a,
    dp_a,
    w_b,
    mix_b,
    ctx_b,
    dp_b,
    near_ref,
    rest_ref,
    send_ref,
    keep_ref,
    small_ref,
    up_s,
    down_s,
    act_s,
    dh_s,
    ug_s,
    dg_s,
    sems,
):
    r, key = where_ref[0], where_ref[1]
    count = n2_ref.shape[0] // 4
    gain, first_gain = norms_ref[2:3, :], norms_ref[0:1, :]
    owns, others = (own0_ref, own1_ref, own2_ref, own3_ref), [oth_ref.at[k] for k in range(4)]
    moves = []
    for k in range(4):
        g = pl.multiple_of((key ^ k) * 128, 128)
        for h, ref in enumerate((owns[k], others[k])):
            b = ref.shape[0] - 512
            left, right = pl.ds(h * 256, 128), pl.ds(h * 256 + 128, 128)
            moves += [
                (ref.at[pl.ds(b, 128)], up_s.at[pl.ds(g, 128), left]),
                (ref.at[pl.ds(b + 128, 128)], up_s.at[pl.ds(g, 128), right]),
                (ref.at[pl.ds(b + 256, 256)], down_s.at[pl.ds(h * 256, 256), pl.ds(g, 128)]),
            ]
    wait_all(start_all(moves, sems))
    up, down = up_s[...], down_s[...]
    shift = shift_ref[...]
    shift_sum = jnp.zeros((1, up.shape[1]), F32)
    for j in range(4):
        at = pl.ds(pl.multiple_of((r ^ j) * count, count), count)
        target = near_ref if j % 2 else rest_ref
        hidden = dot(n2_ref[at, :], up) + shift
        cdf = 0.5 + 0.5 * lax.erf(hidden * math.sqrt(0.5))
        active = (hidden * cdf).astype(BF)
        slope = cdf + hidden * jnp.exp(-0.5 * hidden * hidden) * (1.0 / math.sqrt(2 * math.pi))
        act_s[at, :] = active
        out = dot(active, down) + dot(ctx_a[at, :], mix_a[...]) + dot(ctx_b[at, :], mix_b[...])
        target[j // 2, 0] = out.astype(target.dtype)
        d_hidden = (dot(cot_ref[at, :], down, ((1,), (1,))) * slope).astype(BF)
        dh_s[at, :] = d_hidden
        d_first = dot(dp_a[at, :], w_a[...]) + dot(dp_b[at, :], w_b[...])
        e = dot(d_hidden, up, ((1,), (1,))) * gain + d_first * first_gain
        target[j // 2, 1] = e.astype(target.dtype)
        shift_sum += jnp.sum(d_hidden.astype(F32), axis=0, keepdims=True)
    mine = cot_ref[pl.ds(pl.multiple_of(r * count, count), count), :]
    product = dot(dh_s[...], xhat_ref[...], ((0,), (0,)))
    weights = jnp.transpose(up.astype(F32))
    across = jnp.transpose(jnp.broadcast_to(shift_sum, (8, up.shape[1])))[:, 0:1]
    small_ref[...] = jnp.zeros(small_ref.shape, F32)
    small_ref[0:1, :] = shift_sum
    small_ref[1:2, :] = jnp.sum(weights * product, axis=0, keepdims=True)
    small_ref[2:3, :] = jnp.sum(weights * across, axis=0, keepdims=True)
    small_ref[3:4, :] = jnp.sum(mine.astype(F32), axis=0, keepdims=True)
    ug_s[...] = jnp.transpose(product * gain + across * norms_ref[3:4, :])
    dg_s[...] = dot(act_s[...], cot_ref[...], ((0,), (0,)))
    for k in range(4):
        g = pl.multiple_of((key ^ k) * 128, 128)
        for h, ref in enumerate((keep_ref, send_ref)):
            ref[k, 0:128] = ug_s[pl.ds(g, 128), h * 256 : h * 256 + 128].astype(ref.dtype)
            ref[k, 128:256] = ug_s[pl.ds(g, 128), h * 256 + 128 : h * 256 + 256].astype(ref.dtype)
            ref[k, 256:512] = dg_s[h * 256 : h * 256 + 256, pl.ds(g, 128)].astype(ref.dtype)


def run_mlp(where, n2, xhat, cot, own, oth, norms, shift, first, second):
    tall, width = n2.shape
    count = tall // 4
    wide = shift.shape[1]
    return call(
        mlp_kernel,
        "feed_forward",
        1 << 35,
        (where, n2, xhat, cot, *own, *oth, norms, shift, *first, *second),
        (
            SHAPE((2, 2, count, width), BF),
            SHAPE((2, 2, count, width), F32),
            SHAPE((4, 512, 128), BF),
            SHAPE((4, 512, 128), F32),
            SHAPE((8, wide), F32),
        ),
        (
            ((width, wide), BF),
            ((wide, width), BF),
            ((tall, wide), BF),
            ((tall, wide), BF),
            ((width, wide), F32),
            ((wide, width), F32),
        ),
        (*own, *oth),
        24,
    )


def cut_kernel(a_ref, b_ref, c_ref, d_ref, att_ref, mlp_ref):
    for k, ref in enumerate((a_ref, b_ref, c_ref, d_ref)):
        att_ref[k] = ref[0:256, :]
        mlp_ref[k] = ref[256:768, :]


def head(key, n1_ref, xhat_ref, cot_ref, norms_ref, shift, cos_ref, sin_ref, starts_ref, w, mix, ctx, dp, grads_ref, scratch):
    q_s, qh_s, k_s, v_s, dctx_s, dq_s, dt_s, pg_s, mg_s, unused = scratch
    tall = n1_ref.shape[0]
    count = tall // 4
    scaling = HD**-0.5
    lane = lanes_of((count, 128))
    left = lane < 64
    first, second = lane % 64 < ROT // 2, lane % 64 < ROT

    def turn(qk, at, sign):
        sine = sin_ref[at, :] * sign
        minus = jnp.where(first, -sine, 0.0)
        plus = jnp.where(first, 0.0, jnp.where(second, sine, 0.0))
        return qk * cos_ref[at, :] + roll(qk, 120) * minus + roll(qk, 8) * plus

    for t in range(4):
        at = slice(t * count, t * count + count)
        projected = dot(n1_ref[at, :], w[...], ((1,), (1,))) + shift
        qk = turn(projected[:, :128], at, 1.0)
        turned = roll(qk, 64)
        q_s[at, :] = jnp.where(left, qk * scaling, 0.0).astype(BF)
        k_s[at, :] = jnp.where(left, turned, 0.0).astype(BF)
        qh_s[at, :] = jnp.where(left, 0.0, turned).astype(BF)
        v_s[at, :] = projected[:, 128:].astype(BF)
        dctx_s[at, :] = dot(cot_ref[at, :], mix[...], ((1,), (1,))).astype(BF)
    dt_s[...] = jnp.zeros(dt_s.shape, F32)
    for t in range(4):
        at = slice(t * count, t * count + count)
        keys = (t + 1) * count
        q, d_context = q_s[at, :], dctx_s[at, :]
        kk, vv = k_s[0:keys, :], v_s[0:keys, :]
        scores = dot(q, kk, ((1,), (1,)))
        place = lax.broadcasted_iota(jnp.int32, (count, keys), 1)
        row = lax.broadcasted_iota(jnp.int32, (count, 1), 0) + t * count
        allowed = (place >= starts_ref[at, :]) & (place <= row)
        scores = jnp.where(allowed, scores, MASKED)
        exponent = jnp.exp(scores - jnp.max(scores, axis=-1, keepdims=True))
        probability = exponent * (1.0 / jnp.sum(exponent, axis=-1, keepdims=True))
        prob_low = probability.astype(BF)
        ctx[at, :] = dot(prob_low, vv).astype(BF)
        d_prob = dot(d_context, vv, ((1,), (1,)))
        weight = jnp.sum(d_prob * probability, axis=-1, keepdims=True)
        d_scores = (probability * (d_prob - weight)).astype(BF)
        dq_s[at, :] = dot(d_scores, kk)
        dt_s[0:128, 0:keys] += dot(qh_s[at, :], d_scores, ((0,), (0,)))
        dt_s[128:256, 0:keys] += dot(d_context, prob_low, ((0,), (0,)))
    shift_sum = jnp.zeros((1, 256), F32)
    for t in range(4):
        at = slice(t * count, t * count + count)
        turned = jnp.transpose(dt_s[:, at])
        qk = turn((dq_s[at, :] + turned[:, :128]) * scaling, at, -1.0)
        dp[at, 0:128] = qk.astype(BF)
        dp[at, 128:256] = turned[:, 128:].astype(BF)
        shift_sum += jnp.sum(dp[at, :].astype(F32), axis=0, keepdims=True)
    product = dot(dp[...], xhat_ref[...], ((0,), (0,)))
    weights = w[...].astype(F32)
    across = jnp.transpose(jnp.broadcast_to(shift_sum, (8, 256)))[:, 0:1]
    gain_sum = jnp.sum(weights * product, axis=0, keepdims=True)
    bias_sum = jnp.sum(weights * across, axis=0, keepdims=True)
    pg_s[...] = product * norms_ref[0:1, :] + across * norms_ref[1:2, :]
    mg_s[...] = dot(ctx[...], cot_ref[...], ((0,), (0,)))
    for k in range(4):
        g = pl.multiple_of((key ^ k) * 128, 128)
        grads_ref[k, 0:192] = pg_s[0:192, pl.ds(g, 128)].astype(grads_ref.dtype)
        grads_ref[k, 192:256] = mg_s[0:64, pl.ds(g, 128)].astype(grads_ref.dtype)
    return shift_sum, gain_sum, bias_sum


def fetch_head(key, slots, w, mix, sems):
    moves = []
    for k in range(4):
        g = pl.multiple_of((key ^ k) * 128, 128)
        moves += [
            (slots[k].at[pl.ds(0, 192)], w.at[pl.ds(0, 192), pl.ds(g, 128)]),
            (slots[k].at[pl.ds(192, 64)], mix.at[pl.ds(0, 64), pl.ds(g, 128)]),
        ]
    copies = start_all(moves, sems)
    w[192:256, :] = jnp.zeros((64, w.shape[1]), BF)
    mix[64:128, :] = jnp.zeros((64, mix.shape[1]), BF)
    return copies


def head_scratch(tall, width):
    return (
        ((tall, 128), BF),
        ((tall, 128), BF),
        ((tall, 128), BF),
        ((tall, 128), BF),
        ((tall, 128), BF),
        ((tall, 128), F32),
        ((256, tall), F32),
        ((256, width), F32),
        ((128, width), F32),
    )


def first_kernel(
    where_ref,
    act0_ref,
    act1_ref,
    act2_ref,
    act3_ref,
    slot0_ref,
    slot1_ref,
    slot2_ref,
    slot3_ref,
    shift_ref,
    cos_ref,
    sin_ref,
    starts_ref,
    norms_ref,
    n1_ref,
    n2_ref,
    xhat_ref,
    cot_ref,
    w_ref,
    mix_ref,
    ctx_ref,
    dp_ref,
    grads_ref,
    small_ref,
    *scratch,
):
    r, key = where_ref[0], where_ref[1]
    *scratch, act_s, act_sems = scratch
    count = act0_ref.shape[1]
    norms = norms_ref[...]
    moves = [(act0_ref, act_s.at[0]), (act1_ref, act_s.at[1])]
    moves += [(act2_ref, act_s.at[2]), (act3_ref, act_s.at[3])]
    fetched = start_all(moves, act_sems)
    copies = fetch_head(key, (slot0_ref, slot1_ref, slot2_ref, slot3_ref), w_ref, mix_ref, scratch[-1])
    for j in range(4):
        fetched[j].wait()
        source = act_s.at[j]
        at = pl.ds(pl.multiple_of((r ^ j) * count, count), count)
        hat, unused = normalize(source[0].astype(F32))
        xhat_ref[at, :] = hat.astype(BF)
        n1_ref[at, :] = (hat * norms[0:1] + norms[1:2]).astype(BF)
        n2_ref[at, :] = (hat * norms[2:3] + norms[3:4]).astype(BF)
        cot_ref[at, :] = source[1]
    wait_all(copies)
    small_ref[...] = jnp.zeros(small_ref.shape, F32)
    small_ref[0:1, 0:256], small_ref[1:2, :], small_ref[2:3, :] = head(
        key,
        n1_ref,
        xhat_ref,
        cot_ref,
        norms_ref,
        shift_ref[0:1, :],
        cos_ref,
        sin_ref,
        starts_ref,
        w_ref,
        mix_ref,
        ctx_ref,
        dp_ref,
        grads_ref,
        scratch,
    )


def run_first(where, chunks, slots, shift, cosine, sine, starts, norms):
    count, width = chunks[0].shape[1:]
    tall = 4 * count
    return call(
        first_kernel,
        "attention_first",
        1 << 35,
        (where, *chunks, *slots, shift, cosine, sine, starts, norms),
        (
            SHAPE((tall, width), BF),
            SHAPE((tall, width), BF),
            SHAPE((tall, width), BF),
            SHAPE((tall, width), BF),
            SHAPE((256, width), BF),
            SHAPE((128, width), BF),
            SHAPE((tall, 128), BF),
            SHAPE((tall, 256), BF),
            SHAPE((4, 256, 128), F32),
            SHAPE((8, width), F32),
        ),
        head_scratch(tall, width),
        (*slots, *chunks),
        8,
        (((4, 2, count, width), BF),),
        14 << 20,
    )


def second_kernel(
    where_ref,
    n1_ref,
    xhat_ref,
    cot_ref,
    slots_ref,
    shift_ref,
    cos_ref,
    sin_ref,
    starts_ref,
    norms_ref,
    w_ref,
    mix_ref,
    ctx_ref,
    dp_ref,
    grads_ref,
    small_ref,
    *scratch,
):
    wait_all(fetch_head(where_ref[1], [slots_ref.at[k] for k in range(4)], w_ref, mix_ref, scratch[-1]))
    small_ref[...] = jnp.zeros(small_ref.shape, F32)
    small_ref[0:1, 0:256], small_ref[1:2, :], small_ref[2:3, :] = head(
        where_ref[1],
        n1_ref,
        xhat_ref,
        cot_ref,
        norms_ref,
        shift_ref[1:2, :],
        cos_ref,
        sin_ref,
        starts_ref,
        w_ref,
        mix_ref,
        ctx_ref,
        dp_ref,
        grads_ref,
        scratch,
    )


def run_second(where, n1, xhat, cot, slots, shift, cosine, sine, starts, norms):
    tall, width = n1.shape
    return call(
        second_kernel,
        "attention_second",
        1 << 35,
        (where, n1, xhat, cot, *slots, shift, cosine, sine, starts, norms),
        (
            SHAPE((256, width), BF),
            SHAPE((128, width), BF),
            SHAPE((tall, 128), BF),
            SHAPE((tall, 256), BF),
            SHAPE((4, 256, 128), BF),
            SHAPE((8, width), F32),
        ),
        head_scratch(tall, width),
        slots,
        8,
    )


def add_kernel(rest_ref, come_ref, mine_ref, onward_ref):
    for i in range(2):
        mine_ref[i] = rest_ref[0, i] + come_ref[0, i].astype(F32)
        onward_ref[i] = (rest_ref[1, i] + come_ref[1, i].astype(F32)).astype(BF)


def finish_kernel(x_ref, cot_ref, mine_ref, come_ref, norms_ref, output_ref, grad_ref):
    x = x_ref[...].astype(F32)
    out = mine_ref[0] + come_ref[0].astype(F32)
    output_ref[...] = (x + out + norms_ref[4:5, :] + norms_ref[5:6, :]).astype(BF)
    e = mine_ref[1] + come_ref[1].astype(F32)
    xhat, root = normalize(x)
    centred = e - jnp.mean(e, axis=-1, keepdims=True)
    along = xhat * jnp.mean(e * xhat, axis=-1, keepdims=True)
    grad_ref[...] = cot_ref[...].astype(F32) + root * (centred - along)


def share_kernel(cols, sizes, where_ref, mlp_ref, own_ref, oth_ref, out_ref):
    y, group = where_ref[3], where_ref[4]
    part, project, up = sizes
    copies = out_ref.shape[0]

    def cut(row, device_of, lane_of):
        wide = row.shape[1]
        place = lax.broadcasted_iota(jnp.int32, (copies, wide), 1)
        device = lax.broadcasted_iota(jnp.int32, (copies, wide), 0)
        kept = jnp.where(device == device_of(place), row, 0.0)
        place = lax.broadcasted_iota(jnp.int32, (wide, 128), 0)
        lane = lax.broadcasted_iota(jnp.int32, (wide, 128), 1)
        chosen = jnp.where(lane == lane_of(place), 1.0, 0.0).astype(BF)
        high = kept.astype(BF)
        low = (kept - high.astype(F32)).astype(BF)
        return dot(high, chosen) + dot(low, chosen)

    rows = [own_ref[i : i + 1, :] + oth_ref[i : i + 1, :] for i in (1, 2)]
    rows += [mlp_ref[i : i + 1, :] for i in (1, 2, 3)]
    total = jnp.zeros((copies, 128), F32)
    for i, row in enumerate(rows):
        total += cut(row, lambda n: n // part, lambda n: i * part + n % part)
    out_ref[...] = jnp.zeros(out_ref.shape, F32)
    out_ref[:, 0, :] = total
    half = cols // 2
    heads, hidden = jnp.zeros((copies, 128), F32), jnp.zeros((copies, 128), F32)
    for h, ref in enumerate((own_ref, oth_ref)):
        begin = group * cols + (h ^ y) * half
        heads += cut(
            ref[0:1, 0:256],
            lambda n: jnp.where(n < half * project, begin + n // project, -1),
            lambda n: n % project,
        )
        hidden += cut(
            mlp_ref[0:1, h * 256 : h * 256 + 256], lambda n: begin + n // up, lambda n: n % up
        )
    out_ref[:, 1, :] = heads
    out_ref[:, 2, :] = hidden


def small_kernel(unused, sums_ref, *outs):
    total = jnp.sum(sums_ref[...], axis=0)
    part = outs[0].shape[1]
    for i in range(5):
        outs[i][...] = total[0:1, i * part : (i + 1) * part]
    outs[5][...] = outs[4][...]
    outs[6][...] = total[1:2, 0 : outs[6].shape[1]]
    outs[7][...] = total[2:3, 0 : outs[7].shape[1]]


def merge_kernel(keep, come, *outs):
    for k in range(4):
        outs[k][...] = (keep[k] + come[k].astype(F32)).astype(BF)


def collect_kernel(unused, *refs):
    att, mlp, (project_ref, mix_ref, up_ref, down_ref) = refs[:4], refs[4:8], refs[8:]

    def total(blocks, begin, end):
        return sum(ref[begin:end, :].astype(F32) for ref in blocks)

    project_ref[...] = total(att, 0, 192)
    mix_ref[...] = total(att, 192, 256)
    up_ref[:, 0:128] = total(mlp, 0, 128)
    up_ref[:, 128:256] = total(mlp, 128, 256)
    down_ref[...] = total(mlp, 256, 512)


def merge(name, keep, come):
    return call_streamed(
        merge_kernel, name, 1 << 26, (keep, come), (SHAPE(keep.shape[1:], BF),) * 4
    )


def on_device(
    inputs,
    seg_start,
    cotangent,
    project_weight,
    project_bias,
    output_weight,
    output_bias,
    up_weight,
    up_bias,
    down_weight,
    down_bias,
    first_gain,
    first_bias,
    second_gain,
    second_bias,
):
    rows, cols = lax.axis_size("row"), lax.axis_size("col")
    per = cols // rows
    r, c = lax.axis_index("row"), lax.axis_index("col")
    both = ("row", "col")
    count, width = inputs.shape[1], inputs.shape[2]
    paired = per == 2

    def flip(value, bit):
        return lax.ppermute(value, "row", [(i, i ^ bit) for i in range(rows)])

    def group_of(i):
        return (i % 2) * 2 + i // 2

    def home(i, k):
        rr, cc = divmod(i, cols)
        z, y = divmod(cc, per)
        return group_of(z) * cols + (rr ^ k) * per + y

    everyone = range(rows * cols)

    def beside(value):
        return lax.ppermute(value, "col", [(i, i ^ 1) for i in range(cols)])

    def spread(block):
        return [lax.ppermute(block, both, [(i, home(i, k)) for i in everyone]) for k in range(rows)]

    def bring(blocks):
        return [
            lax.ppermute(b, both, [(home(i, k), i) for i in everyone]) for k, b in enumerate(blocks)
        ]

    def slot_of(i):
        rr, cc = divmod(i, cols)
        return group_of(cc // per) * cols + (cc % per) * rows + rr

    def fetch(block):
        moved = lax.ppermute(block, both, [(i, slot_of(i)) for i in everyone])
        whole = lax.all_gather(moved, "col", axis=0)
        return whole.reshape((per, rows) + block.shape)

    def fetch_columns(block):
        whole = fetch(block).transpose(1, 2, 0, 3).reshape(rows, block.shape[0], 2, -1)
        return whole.transpose(2, 0, 1, 3)

    def fetch_rows(block):
        whole = fetch(block).transpose(1, 0, 2, 3).reshape(rows, 2, -1, block.shape[1])
        return whole.transpose(1, 0, 2, 3)

    def deliver(blocks):
        flat = blocks.reshape((cols,) + blocks.shape[2:]).astype(BF)
        mine = lax.psum_scatter(flat, "col", scatter_dimension=0, tiled=False)
        return lax.ppermute(mine, both, [(slot_of(i), i) for i in everyone]).astype(F32)

    def deliver_columns(halves):
        deep = halves.shape[2]
        whole = halves.transpose(1, 2, 0, 3).reshape(rows, deep, per, -1)
        return deliver(whole.transpose(2, 0, 1, 3))

    def deliver_rows(halves):
        wide = halves.shape[3]
        whole = halves.transpose(1, 0, 2, 3).reshape(rows, per, -1, wide)
        return deliver(whole.transpose(1, 0, 2, 3))

    if paired:
        key, y = c // per, c % per
    else:
        key, y = jnp.int32(0), jnp.int32(0)
    group = group_of(r)
    where = jnp.stack([r, key, c, y, group]).astype(jnp.int32)
    part, project_len, up_len = first_gain.shape[0], project_bias.shape[0], up_bias.shape[0]
    copies = rows * cols
    x_own, cot_own = inputs[0], cotangent[0]
    vectors = (
        first_gain,
        first_bias,
        second_gain,
        second_bias,
        output_bias,
        down_bias,
        project_bias,
        up_bias,
    )
    results = [SHAPE((copies, LINES, 128), BF), SHAPE((2, count, width), BF)]
    small, act, *packs = run_local(
        functools.partial(prepare_kernel, paired),
        "prepare",
        1 << 20,
        (x_own, cot_own, seg_start, project_weight.T, output_weight, up_weight, down_weight)
        + tuple(v[None] for v in vectors),
        results + [SHAPE((768, 128), BF)] * paired,
        [pltpu.VMEM((LINES, 128), F32)],
    )
    across, far = flip(act, 2), flip(act, 1)
    every = lax.all_to_all(small, both, 0, 0, tiled=True)
    if paired:
        own = spread(packs[0])
        own, across, every = lax.optimization_barrier((own, across, every))
        att_cut, mlp_cut = call_streamed(
            cut_kernel,
            "cut",
            1 << 31,
            tuple(own),
            (SHAPE((4, 256, 128), BF), SHAPE((4, 512, 128), BF)),
        )
        att_slots, mlp_slots = (own, (beside(att_cut),)), (own, (beside(mlp_cut),))
        every, across = lax.optimization_barrier((every, across))
    else:
        ups, downs = fetch_columns(up_weight), fetch_rows(down_weight)
        projects, mixes = fetch_columns(project_weight), fetch_rows(output_weight)
        mlp_slots = [
            jnp.stack(
                [pack_mlp(ups[h, g], downs[h, g]) for g in range(rows)]
            )
            for h in range(2)
        ]
        att_slots = [
            jnp.stack(
                [pack_att(projects[h, g], mixes[h, g]) for g in range(rows)]
            )
            for h in range(2)
        ]

    chunks = (act, far, across, flip(across, 1))
    norms, project_shift, up_shift, starts = call(
        functools.partial(layout_kernel, rows, cols, (part, project_len, up_len)),
        "layout",
        1 << 35,
        (where, every),
        (
            SHAPE((8, width), F32),
            SHAPE((2, 256), F32),
            SHAPE((1, 512), F32),
            SHAPE((rows * count, 1), jnp.int32),
        ),
        (),
    )
    if paired:
        pass
    cosine, sine = rotary_tables(jnp.arange(rows * count, dtype=jnp.int32) - starts[:, 0])

    if not paired:
        att_slots = list(att_slots[0]), (att_slots[1],)
        mlp_slots = list(mlp_slots[0]), (mlp_slots[1],)
    n1, n2, xhat, cot_all, *first, att_keep, small_own = run_first(
        where, chunks, att_slots[0], project_shift, cosine, sine, starts, norms
    )
    *second, att_send, small_oth = run_second(
        where, n1, xhat, cot_all, att_slots[1], project_shift, cosine, sine, starts, norms
    )
    near, rest, mlp_send, mlp_keep, mlp_small = run_mlp(
        where, n2, xhat, cot_all, mlp_slots[0], mlp_slots[1], norms, up_shift, first, second
    )

    (small,) = call(
        functools.partial(share_kernel, cols, (part, project_len, up_len)),
        "share_small",
        1 << 24,
        (where, mlp_small, small_own, small_oth),
        (SHAPE((copies, LINES, 128), F32),),
        (),
    )
    if paired:
        near, att_come = lax.optimization_barrier((near, beside(att_send)))
        mlp_come = beside(mlp_send)
        att_blocks = bring(merge("merge_att", att_keep, att_come))
        mlp_come, att_blocks = lax.optimization_barrier((mlp_come, att_blocks))
        small, att_blocks = lax.optimization_barrier((small, att_blocks))
        blocks = att_blocks + bring(merge("merge_mlp", mlp_keep, mlp_come))

    shares = lax.all_to_all(small, both, 0, 0, tiled=True)

    mine, onward = call_streamed(
        add_kernel,
        "add_near",
        1 << 24,
        (rest, flip(near, 1)),
        (SHAPE((2, count, width), F32), SHAPE((2, count, width), BF)),
    )
    if paired:
        onward, att_blocks = lax.optimization_barrier((onward, att_blocks))
        blocks[:4] = att_blocks
    onward = flip(onward, 2)
    output, input_grad = call_streamed(
        finish_kernel,
        "finish",
        1 << 24,
        (x_own, cot_own, mine, onward, norms),
        (SHAPE((count, width), BF), SHAPE((count, width), F32)),
    )

    if paired:
        pass
    else:
        att_grads, mlp_grads = jnp.stack([att_keep, att_send.astype(F32)]), jnp.stack([mlp_keep, mlp_send.astype(F32)])
        every_pair = [(h, g) for h in range(2) for g in range(rows)]

        def regroup(parts):
            return jnp.stack(parts).reshape((2, rows) + parts[0].shape)

        project_done = deliver_columns(
            regroup([att_grads[h, g][:192].T for h, g in every_pair])
        )
        mix_done = deliver_rows(regroup([att_grads[h, g][192:] for h, g in every_pair]))
        up_done = deliver_columns(
            regroup([unpack_up(mlp_grads[h, g][:256]) for h, g in every_pair])
        )
        down_done = deliver_rows(regroup([mlp_grads[h, g][256:] for h, g in every_pair]))

    *pieces, project_shift_grad, up_shift_grad = [
        v[0]
        for v in call(
            small_kernel,
            "small_sums",
            1 << 24,
            (where, shares),
            (SHAPE((1, part), F32),) * 6
            + (SHAPE((1, project_len), F32), SHAPE((1, up_len), F32)),
            (),
        )
    ]
    if paired:
        output, pieces, blocks = lax.optimization_barrier((output, pieces, blocks))
        project_done, mix_done, up_done, down_done = call(
            collect_kernel,
            "collect",
            1 << 26,
            (where, *blocks),
            (
                SHAPE(project_weight.shape[::-1], F32),
                SHAPE(output_weight.shape, F32),
                SHAPE(up_weight.shape, F32),
                SHAPE(down_weight.shape, F32),
            ),
            (),
        )
        project_done = project_done.T
    return (
        output[None],
        input_grad[None],
        project_done,
        project_shift_grad,
        mix_done,
        pieces[4],
        up_done,
        up_shift_grad,
        down_done,
        pieces[5],
        pieces[0],
        pieces[1],
        pieces[2],
        pieces[3],
    )


def solution(mesh):
    return jax.shard_map(
        on_device,
        mesh=mesh,
        in_specs=(
            P("col", "row", None),
            P("col", "row"),
            P("col", "row", None),
            P("row", "col"),
            P(("row", "col")),
            P("col", "row"),
            P(("row", "col")),
            P("row", "col"),
            P(("row", "col")),
            P("col", "row"),
            P(("row", "col")),
            P(("row", "col")),
            P(("row", "col")),
            P(("row", "col")),
            P(("row", "col")),
        ),
        out_specs=(
            P("col", "row", None),
            P("col", "row", None),
            P("row", "col"),
            P(("row", "col")),
            P("col", "row"),
            P(("row", "col")),
            P("row", "col"),
            P(("row", "col")),
            P("col", "row"),
            P(("row", "col")),
            P(("row", "col")),
            P(("row", "col")),
            P(("row", "col")),
            P(("row", "col")),
        ),
        check_vma=False,
    )
```

```python
import functools
import math

import jax
import jax.numpy as jnp
import numpy as np
from jax import lax
from jax.experimental import pallas as pl
from jax.experimental.pallas import tpu as pltpu
from jax.sharding import PartitionSpec as P

HD = 64
ROT = 16
EPS = 1e-05
MASKED = -1e30
BF = jnp.bfloat16
F32 = jnp.float32


def normalize(rows_in):
    average = jnp.mean(rows_in, axis=-1, keepdims=True)
    centred = rows_in - average
    spread = jnp.mean(centred * centred, axis=-1, keepdims=True)
    root = lax.rsqrt(spread + EPS)
    return centred * root, root


def dot(a, b, dims=((1,), (0,))):
    return lax.dot_general(a, b, (dims, ((), ())), preferred_element_type=F32)


def pack_att(project, mix):
    return jnp.concatenate([project.T, mix], axis=0)


def pack_mlp(up, down):
    return jnp.concatenate([up[:, :128], up[:, 128:], down], axis=0)


def unpack_up(p):
    return jnp.concatenate([p[:128], p[128:256]], axis=1)


def rotary_tables(positions):
    lane = np.arange(2 * HD) % HD
    frequency = np.where(lane < ROT, 10000.0 ** (-(lane % (ROT // 2)) * 2.0 / ROT), 0.0)
    angles = positions[:, None].astype(F32) * jnp.asarray(frequency, F32)[None, :]
    return jnp.cos(angles), jnp.sin(angles)


VMEM_LIMIT = 14 << 20


def roll(value, shift):
    return pltpu.roll(value, shift, 1)


def lanes_of(shape):
    return lax.broadcasted_iota(jnp.int32, shape, 1)


VMEM = pl.BlockSpec(memory_space=pltpu.VMEM)
SMEM = pl.BlockSpec(memory_space=pltpu.SMEM)
SHAPE = jax.ShapeDtypeStruct
LINES = 8


ANY = pl.BlockSpec(memory_space=pl.ANY)
HBM = pl.BlockSpec(memory_space=pltpu.HBM)


def call_streamed(kernel, name, work, operands, results):
    def body(*refs):
        count = len(operands)
        sources, outs, held, sems = refs[:count], refs[count:-count - 1], refs[-count - 1 : -1], refs[-1]
        wait_all(start_all(list(zip(sources, held)), sems))
        kernel(*held, *outs)

    return pl.pallas_call(
        body,
        out_shape=results,
        in_specs=[HBM] * len(operands),
        out_specs=[VMEM] * len(results),
        scratch_shapes=[pltpu.VMEM(v.shape, v.dtype) for v in operands]
        + [pltpu.SemaphoreType.DMA((len(operands),))],
        compiler_params=pltpu.CompilerParams(vmem_limit_bytes=12 << 20),
        cost_estimate=pl.CostEstimate(flops=work, bytes_accessed=work // 400, transcendentals=0),
        name=name,
    )(*operands)


def call(kernel, name, work, operands, results, scratch, far=(), copies=0, held=(), limit=VMEM_LIMIT):
    places = [HBM if any(v is w for w in far) else VMEM for v in operands[1:]]
    return pl.pallas_call(
        kernel,
        out_shape=results,
        in_specs=[SMEM] + places,
        out_specs=[VMEM] * len(results),
        scratch_shapes=[pltpu.VMEM(size, dtype) for size, dtype in scratch]
        + [pltpu.SemaphoreType.DMA((copies,))] * (copies > 0)
        + [v for size, dtype in held for v in (pltpu.VMEM(size, dtype), pltpu.SemaphoreType.DMA(size[:1]))],
        compiler_params=pltpu.CompilerParams(vmem_limit_bytes=limit),
        cost_estimate=pl.CostEstimate(flops=work, bytes_accessed=work // 400, transcendentals=0),
        name=name,
    )(*operands)


def start_all(moves, sems):
    copies = [
        pltpu.make_async_copy(source, target, sems.at[i]) for i, (source, target) in enumerate(moves)
    ]
    for copy in copies:
        copy.start()
    return copies


def wait_all(copies):
    for copy in copies:
        copy.wait()


def prepare_kernel(paired, *refs):
    sources, (small_ref, act_ref, *packs) = refs[:15], refs[15 : 17 + paired]
    *held, line, sems = refs[17 + paired :]
    moves = list(zip(sources[2:], held[2:]))
    moves += [(sources[0], act_ref.at[0]), (sources[1], act_ref.at[1])]
    copies = start_all(moves, sems)
    line[...] = jnp.zeros(line.shape, F32)
    wait_all(copies)
    unused, unused, seg_ref, project_ref, mix_ref, up_ref, down_ref, *vectors = held
    if paired:
        pack = packs[0]
        pack[0:192, :] = project_ref[...]
        pack[192:256, :] = mix_ref[...]
        pack[256:384, :] = up_ref[:, 0:128]
        pack[384:512, :] = up_ref[:, 128:256]
        pack[512:768, :] = down_ref[...]
    part = vectors[0].shape[1]
    for i in range(6):
        line[0:1, i * part : (i + 1) * part] = vectors[i][...].astype(F32)
    line[1:2, 0 : vectors[6].shape[1]] = vectors[6][...].astype(F32)
    line[2:3, 0 : vectors[7].shape[1]] = vectors[7][...].astype(F32)
    seg = seg_ref[...]
    blocks = seg.shape[1] // 128
    for i in range(blocks):
        piece = seg[:, i * 128 : (i + 1) * 128]
        line[3 + i : 4 + i, :] = (piece >> 5).astype(F32)
        line[3 + blocks + i : 4 + blocks + i, :] = (piece & 31).astype(F32)
    full = line[...].astype(BF)
    for i in range(small_ref.shape[0]):
        small_ref[i] = full


def run_local(kernel, name, work, sources, results, scratch):
    return pl.pallas_call(
        kernel,
        out_shape=results,
        in_specs=[HBM] * len(sources),
        out_specs=[VMEM] * len(results),
        scratch_shapes=[pltpu.VMEM(v.shape, v.dtype) for v in sources]
        + scratch
        + [pltpu.SemaphoreType.DMA((len(sources),))],
        compiler_params=pltpu.CompilerParams(vmem_limit_bytes=60 << 20),
        cost_estimate=pl.CostEstimate(flops=work, bytes_accessed=1 << 20, transcendentals=0),
        name=name,
    )(*sources)


def layout_kernel(rows, cols, sizes, where_ref, every_ref, norms_ref, project_ref, up_ref, starts_ref):
    c, y, group = where_ref[2], where_ref[3], where_ref[4]
    part, project, up = sizes
    copies = every_ref.shape[0]

    def spread_out(block, lane_of, row_of, wide):
        lane = lax.broadcasted_iota(jnp.int32, (128, wide), 0)
        place = lax.broadcasted_iota(jnp.int32, (128, wide), 1)
        picked = dot(block, jnp.where(lane == lane_of(place), 1.0, 0.0).astype(BF))
        device = lax.broadcasted_iota(jnp.int32, (copies, wide), 0)
        place = lax.broadcasted_iota(jnp.int32, (copies, wide), 1)
        return jnp.sum(jnp.where(device == row_of(place), picked, 0.0), axis=0, keepdims=True)

    def line(i):
        return every_ref[:, i, :]

    wide = norms_ref.shape[1]
    rows_of = [line(i) for i in range(LINES)]
    for i in range(6):
        norms_ref[i : i + 1, :] = spread_out(
            rows_of[0], lambda n: i * part + n % part, lambda n: n // part, wide
        )
    norms_ref[6:8, :] = jnp.zeros((2, wide), F32)
    half = cols // 2
    for h in range(2):
        begin = group * cols + (h ^ y) * half
        project_ref[h : h + 1, :] = spread_out(
            rows_of[1],
            lambda n: n % project,
            lambda n: jnp.where(n < half * project, begin + n // project, -1),
            256,
        )
        up_ref[:, h * 256 : h * 256 + 256] = spread_out(
            rows_of[2], lambda n: n % up, lambda n: begin + n // up, 256
        )
    device = lax.broadcasted_iota(jnp.int32, (copies, 128), 0)
    eye = lax.broadcasted_iota(jnp.int32, (128, 128), 0) == lanes_of((128, 128))
    count = starts_ref.shape[0] // rows
    blocks = count // 128
    for g in range(rows):
        here = device == g * cols + c
        for b in range(blocks):
            coarse, fine = rows_of[3 + b].astype(F32), rows_of[3 + blocks + b].astype(F32)
            value = jnp.sum(jnp.where(here, coarse * 32.0 + fine, 0.0), axis=0, keepdims=True)
            column = jnp.sum(jnp.where(eye, value, 0.0), axis=1, keepdims=True)
            begin = g * count + b * 128
            starts_ref[begin : begin + 128, :] = column.astype(jnp.int32)


def mlp_kernel(
    where_ref,
    n2_ref,
    xhat_ref,
    cot_ref,
    own0_ref,
    own1_ref,
    own2_ref,
    own3_ref,
    oth_ref,
    norms_ref,
    shift_ref,
    w_a,
    mix_a,
    ctx_a,
    dp_a,
    w_b,
    mix_b,
    ctx_b,
    dp_b,
    near_ref,
    rest_ref,
    send_ref,
    keep_ref,
    small_ref,
    up_s,
    down_s,
    act_s,
    dh_s,
    ug_s,
    dg_s,
    sems,
):
    r, key = where_ref[0], where_ref[1]
    count = n2_ref.shape[0] // 4
    gain, first_gain = norms_ref[2:3, :], norms_ref[0:1, :]
    owns, others = (own0_ref, own1_ref, own2_ref, own3_ref), [oth_ref.at[k] for k in range(4)]
    moves = []
    for k in range(4):
        g = pl.multiple_of((key ^ k) * 128, 128)
        for h, ref in enumerate((owns[k], others[k])):
            b = ref.shape[0] - 512
            left, right = pl.ds(h * 256, 128), pl.ds(h * 256 + 128, 128)
            moves += [
                (ref.at[pl.ds(b, 128)], up_s.at[pl.ds(g, 128), left]),
                (ref.at[pl.ds(b + 128, 128)], up_s.at[pl.ds(g, 128), right]),
                (ref.at[pl.ds(b + 256, 256)], down_s.at[pl.ds(h * 256, 256), pl.ds(g, 128)]),
            ]
    wait_all(start_all(moves, sems))
    up, down = up_s[...], down_s[...]
    shift = shift_ref[...]
    shift_sum = jnp.zeros((1, up.shape[1]), F32)
    for j in range(4):
        at = pl.ds(pl.multiple_of((r ^ j) * count, count), count)
        target = near_ref if j % 2 else rest_ref
        hidden = dot(n2_ref[at, :], up) + shift
        cdf = 0.5 + 0.5 * lax.erf(hidden * math.sqrt(0.5))
        active = (hidden * cdf).astype(BF)
        slope = cdf + hidden * jnp.exp(-0.5 * hidden * hidden) * (1.0 / math.sqrt(2 * math.pi))
        act_s[at, :] = active
        out = dot(active, down) + dot(ctx_a[at, :], mix_a[...]) + dot(ctx_b[at, :], mix_b[...])
        target[j // 2, 0] = out.astype(target.dtype)
        d_hidden = (dot(cot_ref[at, :], down, ((1,), (1,))) * slope).astype(BF)
        dh_s[at, :] = d_hidden
        d_first = dot(dp_a[at, :], w_a[...]) + dot(dp_b[at, :], w_b[...])
        e = dot(d_hidden, up, ((1,), (1,))) * gain + d_first * first_gain
        target[j // 2, 1] = e.astype(target.dtype)
        shift_sum += jnp.sum(d_hidden.astype(F32), axis=0, keepdims=True)
    mine = cot_ref[pl.ds(pl.multiple_of(r * count, count), count), :]
    product = dot(dh_s[...], xhat_ref[...], ((0,), (0,)))
    weights = jnp.transpose(up.astype(F32))
    across = jnp.transpose(jnp.broadcast_to(shift_sum, (8, up.shape[1])))[:, 0:1]
    small_ref[...] = jnp.zeros(small_ref.shape, F32)
    small_ref[0:1, :] = shift_sum
    small_ref[1:2, :] = jnp.sum(weights * product, axis=0, keepdims=True)
    small_ref[2:3, :] = jnp.sum(weights * across, axis=0, keepdims=True)
    small_ref[3:4, :] = jnp.sum(mine.astype(F32), axis=0, keepdims=True)
    ug_s[...] = jnp.transpose(product * gain + across * norms_ref[3:4, :])
    dg_s[...] = dot(act_s[...], cot_ref[...], ((0,), (0,)))
    for k in range(4):
        g = pl.multiple_of((key ^ k) * 128, 128)
        for h, ref in enumerate((keep_ref, send_ref)):
            ref[k, 0:128] = ug_s[pl.ds(g, 128), h * 256 : h * 256 + 128].astype(ref.dtype)
            ref[k, 128:256] = ug_s[pl.ds(g, 128), h * 256 + 128 : h * 256 + 256].astype(ref.dtype)
            ref[k, 256:512] = dg_s[h * 256 : h * 256 + 256, pl.ds(g, 128)].astype(ref.dtype)


def run_mlp(where, n2, xhat, cot, own, oth, norms, shift, first, second):
    tall, width = n2.shape
    count = tall // 4
    wide = shift.shape[1]
    return call(
        mlp_kernel,
        "feed_forward",
        1 << 35,
        (where, n2, xhat, cot, *own, *oth, norms, shift, *first, *second),
        (
            SHAPE((2, 2, count, width), BF),
            SHAPE((2, 2, count, width), F32),
            SHAPE((4, 512, 128), BF),
            SHAPE((4, 512, 128), F32),
            SHAPE((8, wide), F32),
        ),
        (
            ((width, wide), BF),
            ((wide, width), BF),
            ((tall, wide), BF),
            ((tall, wide), BF),
            ((width, wide), F32),
            ((wide, width), F32),
        ),
        (*own, *oth),
        24,
    )


def cut_kernel(a_ref, b_ref, c_ref, d_ref, att_ref, mlp_ref):
    for k, ref in enumerate((a_ref, b_ref, c_ref, d_ref)):
        att_ref[k] = ref[0:256, :]
        mlp_ref[k] = ref[256:768, :]


def head(key, n1_ref, xhat_ref, cot_ref, norms_ref, shift, cos_ref, sin_ref, starts_ref, w, mix, ctx, dp, grads_ref, scratch):
    q_s, qh_s, k_s, v_s, dctx_s, dq_s, dt_s, pg_s, mg_s, unused = scratch
    tall = n1_ref.shape[0]
    count = tall // 4
    scaling = HD**-0.5
    lane = lanes_of((count, 128))
    left = lane < 64
    first, second = lane % 64 < ROT // 2, lane % 64 < ROT

    def turn(qk, at, sign):
        sine = sin_ref[at, :] * sign
        minus = jnp.where(first, -sine, 0.0)
        plus = jnp.where(first, 0.0, jnp.where(second, sine, 0.0))
        return qk * cos_ref[at, :] + roll(qk, 120) * minus + roll(qk, 8) * plus

    for t in range(4):
        at = slice(t * count, t * count + count)
        projected = dot(n1_ref[at, :], w[...], ((1,), (1,))) + shift
        qk = turn(projected[:, :128], at, 1.0)
        turned = roll(qk, 64)
        q_s[at, :] = jnp.where(left, qk * scaling, 0.0).astype(BF)
        k_s[at, :] = jnp.where(left, turned, 0.0).astype(BF)
        qh_s[at, :] = jnp.where(left, 0.0, turned).astype(BF)
        v_s[at, :] = projected[:, 128:].astype(BF)
        dctx_s[at, :] = dot(cot_ref[at, :], mix[...], ((1,), (1,))).astype(BF)
    dt_s[...] = jnp.zeros(dt_s.shape, F32)
    for t in range(4):
        at = slice(t * count, t * count + count)
        keys = (t + 1) * count
        q, d_context = q_s[at, :], dctx_s[at, :]
        kk, vv = k_s[0:keys, :], v_s[0:keys, :]
        scores = dot(q, kk, ((1,), (1,)))
        place = lax.broadcasted_iota(jnp.int32, (count, keys), 1)
        row = lax.broadcasted_iota(jnp.int32, (count, 1), 0) + t * count
        allowed = (place >= starts_ref[at, :]) & (place <= row)
        scores = jnp.where(allowed, scores, MASKED)
        exponent = jnp.exp(scores - jnp.max(scores, axis=-1, keepdims=True))
        probability = exponent * (1.0 / jnp.sum(exponent, axis=-1, keepdims=True))
        prob_low = probability.astype(BF)
        ctx[at, :] = dot(prob_low, vv).astype(BF)
        d_prob = dot(d_context, vv, ((1,), (1,)))
        weight = jnp.sum(d_prob * probability, axis=-1, keepdims=True)
        d_scores = (probability * (d_prob - weight)).astype(BF)
        dq_s[at, :] = dot(d_scores, kk)
        dt_s[0:128, 0:keys] += dot(qh_s[at, :], d_scores, ((0,), (0,)))
        dt_s[128:256, 0:keys] += dot(d_context, prob_low, ((0,), (0,)))
    shift_sum = jnp.zeros((1, 256), F32)
    for t in range(4):
        at = slice(t * count, t * count + count)
        turned = jnp.transpose(dt_s[:, at])
        qk = turn((dq_s[at, :] + turned[:, :128]) * scaling, at, -1.0)
        dp[at, 0:128] = qk.astype(BF)
        dp[at, 128:256] = turned[:, 128:].astype(BF)
        shift_sum += jnp.sum(dp[at, :].astype(F32), axis=0, keepdims=True)
    product = dot(dp[...], xhat_ref[...], ((0,), (0,)))
    weights = w[...].astype(F32)
    across = jnp.transpose(jnp.broadcast_to(shift_sum, (8, 256)))[:, 0:1]
    gain_sum = jnp.sum(weights * product, axis=0, keepdims=True)
    bias_sum = jnp.sum(weights * across, axis=0, keepdims=True)
    pg_s[...] = product * norms_ref[0:1, :] + across * norms_ref[1:2, :]
    mg_s[...] = dot(ctx[...], cot_ref[...], ((0,), (0,)))
    for k in range(4):
        g = pl.multiple_of((key ^ k) * 128, 128)
        grads_ref[k, 0:192] = pg_s[0:192, pl.ds(g, 128)].astype(grads_ref.dtype)
        grads_ref[k, 192:256] = mg_s[0:64, pl.ds(g, 128)].astype(grads_ref.dtype)
    return shift_sum, gain_sum, bias_sum


def fetch_head(key, slots, w, mix, sems):
    moves = []
    for k in range(4):
        g = pl.multiple_of((key ^ k) * 128, 128)
        moves += [
            (slots[k].at[pl.ds(0, 192)], w.at[pl.ds(0, 192), pl.ds(g, 128)]),
            (slots[k].at[pl.ds(192, 64)], mix.at[pl.ds(0, 64), pl.ds(g, 128)]),
        ]
    copies = start_all(moves, sems)
    w[192:256, :] = jnp.zeros((64, w.shape[1]), BF)
    mix[64:128, :] = jnp.zeros((64, mix.shape[1]), BF)
    return copies


def head_scratch(tall, width):
    return (
        ((tall, 128), BF),
        ((tall, 128), BF),
        ((tall, 128), BF),
        ((tall, 128), BF),
        ((tall, 128), BF),
        ((tall, 128), F32),
        ((256, tall), F32),
        ((256, width), F32),
        ((128, width), F32),
    )


def first_kernel(
    where_ref,
    act0_ref,
    act1_ref,
    act2_ref,
    act3_ref,
    slot0_ref,
    slot1_ref,
    slot2_ref,
    slot3_ref,
    shift_ref,
    cos_ref,
    sin_ref,
    starts_ref,
    norms_ref,
    n1_ref,
    n2_ref,
    xhat_ref,
    cot_ref,
    w_ref,
    mix_ref,
    ctx_ref,
    dp_ref,
    grads_ref,
    small_ref,
    *scratch,
):
    r, key = where_ref[0], where_ref[1]
    *scratch, act_s, act_sems = scratch
    count = act0_ref.shape[1]
    norms = norms_ref[...]
    moves = [(act0_ref, act_s.at[0]), (act1_ref, act_s.at[1])]
    moves += [(act2_ref, act_s.at[2]), (act3_ref, act_s.at[3])]
    fetched = start_all(moves, act_sems)
    copies = fetch_head(key, (slot0_ref, slot1_ref, slot2_ref, slot3_ref), w_ref, mix_ref, scratch[-1])
    for j in range(4):
        fetched[j].wait()
        source = act_s.at[j]
        at = pl.ds(pl.multiple_of((r ^ j) * count, count), count)
        hat, unused = normalize(source[0].astype(F32))
        xhat_ref[at, :] = hat.astype(BF)
        n1_ref[at, :] = (hat * norms[0:1] + norms[1:2]).astype(BF)
        n2_ref[at, :] = (hat * norms[2:3] + norms[3:4]).astype(BF)
        cot_ref[at, :] = source[1]
    wait_all(copies)
    small_ref[...] = jnp.zeros(small_ref.shape, F32)
    small_ref[0:1, 0:256], small_ref[1:2, :], small_ref[2:3, :] = head(
        key,
        n1_ref,
        xhat_ref,
        cot_ref,
        norms_ref,
        shift_ref[0:1, :],
        cos_ref,
        sin_ref,
        starts_ref,
        w_ref,
        mix_ref,
        ctx_ref,
        dp_ref,
        grads_ref,
        scratch,
    )


def run_first(where, chunks, slots, shift, cosine, sine, starts, norms):
    count, width = chunks[0].shape[1:]
    tall = 4 * count
    return call(
        first_kernel,
        "attention_first",
        1 << 35,
        (where, *chunks, *slots, shift, cosine, sine, starts, norms),
        (
            SHAPE((tall, width), BF),
            SHAPE((tall, width), BF),
            SHAPE((tall, width), BF),
            SHAPE((tall, width), BF),
            SHAPE((256, width), BF),
            SHAPE((128, width), BF),
            SHAPE((tall, 128), BF),
            SHAPE((tall, 256), BF),
            SHAPE((4, 256, 128), F32),
            SHAPE((8, width), F32),
        ),
        head_scratch(tall, width),
        (*slots, *chunks),
        8,
        (((4, 2, count, width), BF),),
        14 << 20,
    )


def second_kernel(
    where_ref,
    n1_ref,
    xhat_ref,
    cot_ref,
    slots_ref,
    shift_ref,
    cos_ref,
    sin_ref,
    starts_ref,
    norms_ref,
    w_ref,
    mix_ref,
    ctx_ref,
    dp_ref,
    grads_ref,
    small_ref,
    *scratch,
):
    wait_all(fetch_head(where_ref[1], [slots_ref.at[k] for k in range(4)], w_ref, mix_ref, scratch[-1]))
    small_ref[...] = jnp.zeros(small_ref.shape, F32)
    small_ref[0:1, 0:256], small_ref[1:2, :], small_ref[2:3, :] = head(
        where_ref[1],
        n1_ref,
        xhat_ref,
        cot_ref,
        norms_ref,
        shift_ref[1:2, :],
        cos_ref,
        sin_ref,
        starts_ref,
        w_ref,
        mix_ref,
        ctx_ref,
        dp_ref,
        grads_ref,
        scratch,
    )


def run_second(where, n1, xhat, cot, slots, shift, cosine, sine, starts, norms):
    tall, width = n1.shape
    return call(
        second_kernel,
        "attention_second",
        1 << 35,
        (where, n1, xhat, cot, *slots, shift, cosine, sine, starts, norms),
        (
            SHAPE((256, width), BF),
            SHAPE((128, width), BF),
            SHAPE((tall, 128), BF),
            SHAPE((tall, 256), BF),
            SHAPE((4, 256, 128), BF),
            SHAPE((8, width), F32),
        ),
        head_scratch(tall, width),
        slots,
        8,
    )


def add_kernel(rest_ref, come_ref, mine_ref, onward_ref):
    for i in range(2):
        mine_ref[i] = rest_ref[0, i] + come_ref[0, i].astype(F32)
        onward_ref[i] = (rest_ref[1, i] + come_ref[1, i].astype(F32)).astype(BF)


def finish_kernel(x_ref, cot_ref, mine_ref, come_ref, norms_ref, output_ref, grad_ref):
    x = x_ref[...].astype(F32)
    out = mine_ref[0] + come_ref[0].astype(F32)
    output_ref[...] = (x + out + norms_ref[4:5, :] + norms_ref[5:6, :]).astype(BF)
    e = mine_ref[1] + come_ref[1].astype(F32)
    xhat, root = normalize(x)
    centred = e - jnp.mean(e, axis=-1, keepdims=True)
    along = xhat * jnp.mean(e * xhat, axis=-1, keepdims=True)
    grad_ref[...] = cot_ref[...].astype(F32) + root * (centred - along)


def share_kernel(cols, sizes, where_ref, mlp_ref, own_ref, oth_ref, out_ref):
    y, group = where_ref[3], where_ref[4]
    part, project, up = sizes
    copies = out_ref.shape[0]

    def cut(row, device_of, lane_of):
        wide = row.shape[1]
        place = lax.broadcasted_iota(jnp.int32, (copies, wide), 1)
        device = lax.broadcasted_iota(jnp.int32, (copies, wide), 0)
        kept = jnp.where(device == device_of(place), row, 0.0)
        place = lax.broadcasted_iota(jnp.int32, (wide, 128), 0)
        lane = lax.broadcasted_iota(jnp.int32, (wide, 128), 1)
        chosen = jnp.where(lane == lane_of(place), 1.0, 0.0).astype(BF)
        high = kept.astype(BF)
        low = (kept - high.astype(F32)).astype(BF)
        return dot(high, chosen) + dot(low, chosen)

    rows = [own_ref[i : i + 1, :] + oth_ref[i : i + 1, :] for i in (1, 2)]
    rows += [mlp_ref[i : i + 1, :] for i in (1, 2, 3)]
    total = jnp.zeros((copies, 128), F32)
    for i, row in enumerate(rows):
        total += cut(row, lambda n: n // part, lambda n: i * part + n % part)
    out_ref[...] = jnp.zeros(out_ref.shape, F32)
    out_ref[:, 0, :] = total
    half = cols // 2
    heads, hidden = jnp.zeros((copies, 128), F32), jnp.zeros((copies, 128), F32)
    for h, ref in enumerate((own_ref, oth_ref)):
        begin = group * cols + (h ^ y) * half
        heads += cut(
            ref[0:1, 0:256],
            lambda n: jnp.where(n < half * project, begin + n // project, -1),
            lambda n: n % project,
        )
        hidden += cut(
            mlp_ref[0:1, h * 256 : h * 256 + 256], lambda n: begin + n // up, lambda n: n % up
        )
    out_ref[:, 1, :] = heads
    out_ref[:, 2, :] = hidden


def small_kernel(sums_ref, *outs):
    total = jnp.sum(sums_ref[...], axis=0)
    part = outs[0].shape[1]
    for i in range(5):
        outs[i][...] = total[0:1, i * part : (i + 1) * part]
    outs[5][...] = outs[4][...]
    outs[6][...] = total[1:2, 0 : outs[6].shape[1]]
    outs[7][...] = total[2:3, 0 : outs[7].shape[1]]


def merge_kernel(keep, come, *outs):
    for k in range(4):
        outs[k][...] = (keep[k] + come[k].astype(F32)).astype(BF)


def collect_kernel(unused, *refs):
    att, mlp, (project_ref, mix_ref, up_ref, down_ref) = refs[:4], refs[4:8], refs[8:]

    def total(blocks, begin, end):
        return sum(ref[begin:end, :].astype(F32) for ref in blocks)

    project_ref[...] = total(att, 0, 192)
    mix_ref[...] = total(att, 192, 256)
    up_ref[:, 0:128] = total(mlp, 0, 128)
    up_ref[:, 128:256] = total(mlp, 128, 256)
    down_ref[...] = total(mlp, 256, 512)


def merge(name, keep, come):
    return call_streamed(
        merge_kernel, name, 1 << 26, (keep, come), (SHAPE(keep.shape[1:], BF),) * 4
    )


def on_device(
    inputs,
    seg_start,
    cotangent,
    project_weight,
    project_bias,
    output_weight,
    output_bias,
    up_weight,
    up_bias,
    down_weight,
    down_bias,
    first_gain,
    first_bias,
    second_gain,
    second_bias,
):
    rows, cols = lax.axis_size("row"), lax.axis_size("col")
    per = cols // rows
    r, c = lax.axis_index("row"), lax.axis_index("col")
    both = ("row", "col")
    count, width = inputs.shape[1], inputs.shape[2]
    paired = per == 2

    def flip(value, bit):
        return lax.ppermute(value, "row", [(i, i ^ bit) for i in range(rows)])

    def group_of(i):
        return (i % 2) * 2 + i // 2

    def home(i, k):
        rr, cc = divmod(i, cols)
        z, y = divmod(cc, per)
        return group_of(z) * cols + (rr ^ k) * per + y

    everyone = range(rows * cols)

    def beside(value):
        return lax.ppermute(value, "col", [(i, i ^ 1) for i in range(cols)])

    def spread(block):
        return [lax.ppermute(block, both, [(i, home(i, k)) for i in everyone]) for k in range(rows)]

    def bring(blocks):
        return [
            lax.ppermute(b, both, [(home(i, k), i) for i in everyone]) for k, b in enumerate(blocks)
        ]

    def slot_of(i):
        rr, cc = divmod(i, cols)
        return group_of(cc // per) * cols + (cc % per) * rows + rr

    def fetch(block):
        moved = lax.ppermute(block, both, [(i, slot_of(i)) for i in everyone])
        whole = lax.all_gather(moved, "col", axis=0)
        return whole.reshape((per, rows) + block.shape)

    def fetch_columns(block):
        whole = fetch(block).transpose(1, 2, 0, 3).reshape(rows, block.shape[0], 2, -1)
        return whole.transpose(2, 0, 1, 3)

    def fetch_rows(block):
        whole = fetch(block).transpose(1, 0, 2, 3).reshape(rows, 2, -1, block.shape[1])
        return whole.transpose(1, 0, 2, 3)

    def deliver(blocks):
        flat = blocks.reshape((cols,) + blocks.shape[2:]).astype(BF)
        mine = lax.psum_scatter(flat, "col", scatter_dimension=0, tiled=False)
        return lax.ppermute(mine, both, [(slot_of(i), i) for i in everyone]).astype(F32)

    def deliver_columns(halves):
        deep = halves.shape[2]
        whole = halves.transpose(1, 2, 0, 3).reshape(rows, deep, per, -1)
        return deliver(whole.transpose(2, 0, 1, 3))

    def deliver_rows(halves):
        wide = halves.shape[3]
        whole = halves.transpose(1, 0, 2, 3).reshape(rows, per, -1, wide)
        return deliver(whole.transpose(1, 0, 2, 3))

    if paired:
        key, y = c // per, c % per
    else:
        key, y = jnp.int32(0), jnp.int32(0)
    group = group_of(r)
    where = jnp.stack([r, key, c, y, group]).astype(jnp.int32)
    part, project_len, up_len = first_gain.shape[0], project_bias.shape[0], up_bias.shape[0]
    copies = rows * cols
    x_own, cot_own = inputs[0], cotangent[0]
    vectors = (
        first_gain,
        first_bias,
        second_gain,
        second_bias,
        output_bias,
        down_bias,
        project_bias,
        up_bias,
    )
    results = [SHAPE((copies, LINES, 128), BF), SHAPE((2, count, width), BF)]
    small, act, *packs = run_local(
        functools.partial(prepare_kernel, paired),
        "prepare",
        1 << 20,
        (x_own, cot_own, seg_start, project_weight.T, output_weight, up_weight, down_weight)
        + tuple(v[None] for v in vectors),
        results + [SHAPE((768, 128), BF)] * paired,
        [pltpu.VMEM((LINES, 128), F32)],
    )
    across, far = flip(act, 2), flip(act, 1)
    every = lax.all_to_all(small, both, 0, 0, tiled=True)
    if paired:
        own = spread(packs[0])
        own, across, every = lax.optimization_barrier((own, across, every))
        att_cut, mlp_cut = call_streamed(
            cut_kernel,
            "cut",
            1 << 31,
            tuple(own),
            (SHAPE((4, 256, 128), BF), SHAPE((4, 512, 128), BF)),
        )
        att_slots, mlp_slots = (own, (beside(att_cut),)), (own, (beside(mlp_cut),))
        every, across = lax.optimization_barrier((every, across))
    else:
        ups, downs = fetch_columns(up_weight), fetch_rows(down_weight)
        projects, mixes = fetch_columns(project_weight), fetch_rows(output_weight)
        mlp_slots = [
            jnp.stack(
                [pack_mlp(ups[h, g], downs[h, g]) for g in range(rows)]
            )
            for h in range(2)
        ]
        att_slots = [
            jnp.stack(
                [pack_att(projects[h, g], mixes[h, g]) for g in range(rows)]
            )
            for h in range(2)
        ]

    chunks = (act, far, across, flip(across, 1))
    norms, project_shift, up_shift, starts = call(
        functools.partial(layout_kernel, rows, cols, (part, project_len, up_len)),
        "layout",
        1 << 35,
        (where, every),
        (
            SHAPE((8, width), F32),
            SHAPE((2, 256), F32),
            SHAPE((1, 512), F32),
            SHAPE((rows * count, 1), jnp.int32),
        ),
        (),
    )
    if paired:
        pass
    cosine, sine = rotary_tables(jnp.arange(rows * count, dtype=jnp.int32) - starts[:, 0])

    if not paired:
        att_slots = list(att_slots[0]), (att_slots[1],)
        mlp_slots = list(mlp_slots[0]), (mlp_slots[1],)
    n1, n2, xhat, cot_all, *first, att_keep, small_own = run_first(
        where, chunks, att_slots[0], project_shift, cosine, sine, starts, norms
    )
    *second, att_send, small_oth = run_second(
        where, n1, xhat, cot_all, att_slots[1], project_shift, cosine, sine, starts, norms
    )
    near, rest, mlp_send, mlp_keep, mlp_small = run_mlp(
        where, n2, xhat, cot_all, mlp_slots[0], mlp_slots[1], norms, up_shift, first, second
    )

    (small,) = call(
        functools.partial(share_kernel, cols, (part, project_len, up_len)),
        "share_small",
        1 << 24,
        (where, mlp_small, small_own, small_oth),
        (SHAPE((copies, LINES, 128), F32),),
        (),
    )
    if paired:
        near, att_come = lax.optimization_barrier((near, beside(att_send)))
        mlp_come = beside(mlp_send)
        att_blocks = bring(merge("merge_att", att_keep, att_come))
        mlp_come, att_blocks = lax.optimization_barrier((mlp_come, att_blocks))
        small, att_blocks = lax.optimization_barrier((small, att_blocks))
        blocks = att_blocks + bring(merge("merge_mlp", mlp_keep, mlp_come))

    shares = lax.all_to_all(small, both, 0, 0, tiled=True)

    mine, onward = call_streamed(
        add_kernel,
        "add_near",
        1 << 24,
        (rest, flip(near, 1)),
        (SHAPE((2, count, width), F32), SHAPE((2, count, width), BF)),
    )
    if paired:
        onward, att_blocks = lax.optimization_barrier((onward, att_blocks))
        blocks[:4] = att_blocks
    onward = flip(onward, 2)
    output, input_grad = call_streamed(
        finish_kernel,
        "finish",
        1 << 24,
        (x_own, cot_own, mine, onward, norms),
        (SHAPE((count, width), BF), SHAPE((count, width), F32)),
    )

    if paired:
        pass
    else:
        att_grads, mlp_grads = jnp.stack([att_keep, att_send.astype(F32)]), jnp.stack([mlp_keep, mlp_send.astype(F32)])
        every_pair = [(h, g) for h in range(2) for g in range(rows)]

        def regroup(parts):
            return jnp.stack(parts).reshape((2, rows) + parts[0].shape)

        project_done = deliver_columns(
            regroup([att_grads[h, g][:192].T for h, g in every_pair])
        )
        mix_done = deliver_rows(regroup([att_grads[h, g][192:] for h, g in every_pair]))
        up_done = deliver_columns(
            regroup([unpack_up(mlp_grads[h, g][:256]) for h, g in every_pair])
        )
        down_done = deliver_rows(regroup([mlp_grads[h, g][256:] for h, g in every_pair]))

    *pieces, project_shift_grad, up_shift_grad = [
        v[0]
        for v in call_streamed(
            small_kernel,
            "small_sums",
            1 << 24,
            (shares,),
            (SHAPE((1, part), F32),) * 6
            + (SHAPE((1, project_len), F32), SHAPE((1, up_len), F32)),
        )
    ]
    if paired:
        output, pieces, blocks = lax.optimization_barrier((output, pieces, blocks))
        project_done, mix_done, up_done, down_done = call(
            collect_kernel,
            "collect",
            1 << 26,
            (where, *blocks),
            (
                SHAPE(project_weight.shape[::-1], F32),
                SHAPE(output_weight.shape, F32),
                SHAPE(up_weight.shape, F32),
                SHAPE(down_weight.shape, F32),
            ),
            (),
        )
        project_done = project_done.T
    return (
        output[None],
        input_grad[None],
        project_done,
        project_shift_grad,
        mix_done,
        pieces[4],
        up_done,
        up_shift_grad,
        down_done,
        pieces[5],
        pieces[0],
        pieces[1],
        pieces[2],
        pieces[3],
    )


def solution(mesh):
    return jax.shard_map(
        on_device,
        mesh=mesh,
        in_specs=(
            P("col", "row", None),
            P("col", "row"),
            P("col", "row", None),
            P("row", "col"),
            P(("row", "col")),
            P("col", "row"),
            P(("row", "col")),
            P("row", "col"),
            P(("row", "col")),
            P("col", "row"),
            P(("row", "col")),
            P(("row", "col")),
            P(("row", "col")),
            P(("row", "col")),
            P(("row", "col")),
        ),
        out_specs=(
            P("col", "row", None),
            P("col", "row", None),
            P("row", "col"),
            P(("row", "col")),
            P("col", "row"),
            P(("row", "col")),
            P("row", "col"),
            P(("row", "col")),
            P("col", "row"),
            P(("row", "col")),
            P(("row", "col")),
            P(("row", "col")),
            P(("row", "col")),
            P(("row", "col")),
        ),
        check_vma=False,
    )
```
